32 devices in a mesh: dp: 8 (over z, x), pipe: 4 (over y, core).
Axes of the slice: x: 2, y: 2, z: 4, core: 2. Of those that a mesh axis runs over, the one named last changes fastest.
Arguments:
- patch_states: bfloat16 [16, 256, 1024], P('dp'), may hold values from -6 to 6
- byte_states: bfloat16 [16, 640, 1024], P('dp'), may hold values from -6 to 6
- cotangent: bfloat16 [16, 256, 1024], P('dp'), may hold values from -6 to 6
- patch_lengths: int32 [16, 256], P('dp'), may hold values from 1 to 8, 640 in all within a row
- row_lengths: int32 [16], P('dp'), may hold values from 1 to 256, 2560 in all
- attn_weights: bfloat16 [2, 3, 1024, 1024], P(None, None, ('dp', 'pipe')), may hold values from -0.1875 to 0.1875
- out_weights: bfloat16 [2, 1024, 1024], P(None, ('dp', 'pipe')), may hold values from -0.5 to 0.5
- gate_up: bfloat16 [2, 1024, 2816], P(None, ('dp', 'pipe')), may hold values from -0.1875 to 0.1875
- down_weight: bfloat16 [2816, 1024], P(('dp', 'pipe')), may hold values from -0.109375 to 0.109375
- gains: float32 [4, 1024], replicated, may hold values from 0.1 to 1.9
Outputs:
- outputs: bfloat16 [16, 256, 1024], P('dp', 'pipe')
- grad_patches: bfloat16 [16, 256, 1024], P('dp', 'pipe')
- grad_bytes: bfloat16 [16, 640, 1024], P('dp', 'pipe')
- grad_attn: float32 [2, 3, 1024, 1024], P(None, None, ('dp', 'pipe'))
- grad_out: float32 [2, 1024, 1024], P(None, ('dp', 'pipe'))
- grad_gate_up: float32 [2, 1024, 2816], P(None, ('dp', 'pipe'))
- grad_down: float32 [2816, 1024], P(('dp', 'pipe'))
- grad_gains: float32 [4, 1024], P(None, ('dp', 'pipe'))
The draws below stay inside these ranges and needn't reach their ends.
Inputs may be any that keep to these rules, and one draw needn't show every extreme that they name: `patch_lengths`: each row's 256 entries sum to 640; every row has a patch of exactly 8 bytes. Patches at or after row_lengths[r] are padding and are no keys of the global attention; some row is full.
All inputs are finite; a program needn't handle non-finite values. No bound on the sum of `row_lengths` on one device may be relied on, other than what follows from the above.
Results may differ from the reference program's by a relative error of at most 0.028.
Values may be sent and summed in bfloat16 or wider, within the bound.
A program may use at most 512 MiB of HBM per device.

```python
import math
import jax
import jax.numpy as jnp
import numpy as np
from jax import lax

D = 1024
HEADS = 16
HEAD_DIM = 64
FF = 2816
PATCH_MAX = 8
ROW_P = 256
ROW_B = 640
ROWS = 16


def levels(stream_key, dims, cuts, smallest, high):
    def one(position, parts):
        heights = jax.random.uniform(jax.random.fold_in(jax.random.fold_in(stream_key, 6), position), (parts,), jnp.float32, smallest / len(cuts), high / len(cuts))
        return jnp.repeat(jnp.exp(heights), dims[position] // parts).reshape((-1,) + (1,) * (len(dims) - position - 1))

    level = one(*cuts[0])
    for cut in cuts[1:]:
        level = level * one(*cut)
    return level


def length_profile(amount, total, bound, lean):
    loads = [(1 << 20) // math.isqrt(rank ** lean) + 1 for rank in range(2, amount + 1)]
    spare, given = total - bound - (amount - 1), [1] * (amount - 1)
    while spare > 0:
        candidates = [i for i in range(amount - 1) if given[i] < bound]
        pool, left = sum([loads[i] for i in candidates]), spare
        for i in candidates:
            more = min(bound - given[i], max(1, left * loads[i] // pool), spare)
            given[i] = given[i] + more
            spare = spare - more
    return np.array([bound] + given)


def uneven_parts(own_key, amount, total, most, skew):
    if amount == 2:
        one = jax.random.randint(own_key, (), max(1, total - most), min(most, total - 1) + 1)
        return jnp.stack([one, total - one])
    tallies = jnp.asarray(length_profile(amount, total, most, skew), jnp.int32)
    couples = (amount - 1) // 2
    source_of, sink = tallies[1:1 + 2 * couples:2], tallies[2:2 + 2 * couples:2]
    margin = jnp.minimum(source_of - 1, most - sink)
    moved = jax.random.randint(jax.random.fold_in(own_key, 1), (couples,), 0, 1 << 20) % (margin + 1)
    tallies = tallies.at[1:1 + 2 * couples:2].set(source_of - moved).at[2:2 + 2 * couples:2].set(sink + moved)
    return tallies[jax.random.permutation(jax.random.fold_in(own_key, 2), amount)]


def noise(key, extent, deviation, reach, pieces=(), held_as=jnp.bfloat16):
    entries = jax.random.normal(key, extent, jnp.float32) * deviation
    if len(pieces) > 0:
        entries = levels(key, extent, pieces, -0.22, 0.18) * entries
    return jnp.clip(entries, min=-reach, max=reach).astype(held_as)


def setup_inputs(seed: int = 0) -> dict:
    key_list = jax.random.split(jax.random.key(seed), 11)
    patch_states = noise(key_list[0], (ROWS, ROW_P, D), 1.0, 6.0, ((0, 8),))
    byte_states = noise(key_list[1], (ROWS, ROW_B, D), 1.0, 6.0, ((0, 8),))
    cotangent = noise(key_list[2], (ROWS, ROW_P, D), 1.0, 6.0, ((0, 8),))
    patch_lengths = jax.vmap(lambda own: uneven_parts(own, ROW_P, ROW_B, PATCH_MAX, 1))(jax.random.split(key_list[3], ROWS)).reshape((ROWS, ROW_P)).astype(jnp.int32)
    row_lengths = uneven_parts(key_list[4], ROWS, ROWS * ROW_P * 5 // 8, ROW_P, 1).astype(jnp.int32)
    attn_weights = noise(key_list[5], (2, 3, D, D), D ** -0.5, 0.1875, ((2, 32),))
    out_weights = noise(key_list[6], (2, D, D), (D // 8) ** -0.5, 0.5, ((1, 32),))
    gate_up = noise(key_list[7], (2, D, FF), D ** -0.5, 0.1875, ((1, 32),))
    down_weight = noise(key_list[8], (FF, D), FF ** -0.5, 0.109375, ((0, 32),))
    gains = jnp.clip(1.0 + 0.18 * jax.random.normal(key_list[9], (4, D), jnp.float32), 0.1, 1.9)
    return dict(patch_states=patch_states, byte_states=byte_states, cotangent=cotangent, patch_lengths=patch_lengths, row_lengths=row_lengths, attn_weights=attn_weights, out_weights=out_weights, gate_up=gate_up, down_weight=down_weight, gains=gains)


EPSILON = 1e-06
NEGATIVE = -1e+30

@jax.custom_vjp
def low(v):
    return lax.optimization_barrier(v.astype(jnp.bfloat16)).astype(jnp.float32)

@jax.custom_vjp
def low_back(v):
    return v

def low_keep(v):
    return (low(v), None)

def low_pass(kept, grad):
    return (grad,)

def back_keep(v):
    return (v, None)

def back_low(kept, grad):
    return (low(grad),)
low.defvjp(low_keep, low_pass)
low_back.defvjp(back_keep, back_low)

def round_both(values):
    return low(low_back(values))

def high_dot(left, right):
    return jnp.dot(left, right, precision=lax.Precision.HIGHEST)

def rms_norm(values, gain):
    return values * lax.rsqrt(lax.optimization_barrier(jnp.mean(values * values, axis=-1, keepdims=True)) + EPSILON) * gain

def cross_layer(patch_row, byte_row, patch_sizes, attn_stack, out_stack, gain_rows):
    row_count = patch_row.shape[0]
    byte_count = byte_row.shape[0]
    normed_q = low(rms_norm(patch_row, gain_rows[0]))
    normed_b = low(rms_norm(byte_row, gain_rows[1]))
    queries = round_both(high_dot(normed_q, attn_stack[0, 0])).reshape(row_count, HEADS, HEAD_DIM)
    key_rows = round_both(high_dot(normed_b, attn_stack[0, 1]))
    value_rows = round_both(high_dot(normed_b, attn_stack[0, 2]))
    starts = (jnp.cumsum(patch_sizes) - patch_sizes).astype(jnp.int32)
    offsets = jnp.arange(PATCH_MAX, dtype=jnp.int32)
    byte_index = jnp.minimum(starts[:, None] + offsets[None, :], byte_count - 1).astype(jnp.int32)
    live_slot = offsets[None, :] < patch_sizes[:, None]
    key_win = key_rows[byte_index].reshape(row_count, PATCH_MAX, HEADS, HEAD_DIM)
    value_win = value_rows[byte_index].reshape(row_count, PATCH_MAX, HEADS, HEAD_DIM)
    scores = low_back(jnp.einsum('phe,plhe->phl', queries, key_win, precision=lax.Precision.HIGHEST) * HEAD_DIM ** (-0.5))
    attention = low(jax.nn.softmax(jnp.where(live_slot[:, None, :], scores, NEGATIVE), axis=-1))
    mixed_rows = jnp.einsum('phl,plhe->phe', attention, value_win, precision=lax.Precision.HIGHEST)
    mixed_rows = round_both(mixed_rows.reshape(row_count, -1))
    return patch_row + low_back(high_dot(mixed_rows, out_stack[0]))

def global_layer(residual, seq_length, attn_stack, out_stack, gain_rows):
    row_count = residual.shape[0]
    normed = low(rms_norm(residual, gain_rows[2]))
    queries = round_both(high_dot(normed, attn_stack[1, 0])).reshape(row_count, HEADS, HEAD_DIM)
    key_rows = round_both(high_dot(normed, attn_stack[1, 1])).reshape(row_count, HEADS, HEAD_DIM)
    value_rows = round_both(high_dot(normed, attn_stack[1, 2])).reshape(row_count, HEADS, HEAD_DIM)
    block_rows = min(512, row_count)
    key_pos = jnp.arange(row_count, dtype=jnp.int32)

    def attend(begin_row):
        block_q = lax.dynamic_slice_in_dim(queries, begin_row, block_rows, 0)
        query_pos = begin_row + jnp.arange(block_rows, dtype=jnp.int32)
        scores = low_back(jnp.einsum('qhe,khe->hqk', block_q, key_rows, precision=lax.Precision.HIGHEST) * HEAD_DIM ** (-0.5))
        allowed = (key_pos[None, :] <= query_pos[:, None]) & (key_pos[None, :] < seq_length)
        attention = low(jax.nn.softmax(jnp.where(allowed[None], scores, NEGATIVE), axis=-1))
        return jnp.einsum('hqk,khe->qhe', attention, value_rows, precision=lax.Precision.HIGHEST)
    begins = jnp.arange(row_count // block_rows, dtype=jnp.int32) * block_rows
    mixed_rows = round_both(lax.map(jax.checkpoint(attend), begins).reshape(row_count, -1))
    return round_both(residual + low_back(high_dot(mixed_rows, out_stack[1])))

def two_layers(patch_row, byte_row, patch_sizes, seq_length, attn_stack, out_stack, gate_stack, down_rows, gain_rows):
    first_out = round_both(cross_layer(patch_row, byte_row, patch_sizes, attn_stack, out_stack, gain_rows))
    second_in = global_layer(first_out, seq_length, attn_stack, out_stack, gain_rows)
    normed = low(rms_norm(second_in, gain_rows[3]))
    gate_rows = low_back(high_dot(normed, gate_stack[0]))
    up_rows = low_back(high_dot(normed, gate_stack[1]))
    hidden = round_both(jax.nn.silu(gate_rows) * up_rows)
    return second_in + low_back(high_dot(hidden, down_rows))

def reference(patch_states, byte_states, cotangent, patch_lengths, row_lengths, attn_weights, out_weights, gate_up, down_weight, gains):
    params = (attn_weights.astype(jnp.float32), out_weights.astype(jnp.float32), gate_up.astype(jnp.float32), down_weight.astype(jnp.float32), gains.astype(jnp.float32))
    zeros = jax.tree.map(jnp.zeros_like, params)

    def per_row(totals, row_data):
        patch_row, byte_row, cot_row, patch_sizes, seq_length = row_data

        def forward(patch_in, byte_in, weights_in):
            return two_layers(patch_in, byte_in, patch_sizes, seq_length, *weights_in)
        result, pullback = jax.vjp(forward, patch_row.astype(jnp.float32), byte_row.astype(jnp.float32), params)
        grad_patch, grad_byte, grad_params = pullback(cot_row.astype(jnp.float32))
        totals = jax.tree.map(jnp.add, totals, grad_params)
        return (totals, (result.astype(jnp.bfloat16), grad_patch.astype(jnp.bfloat16), grad_byte.astype(jnp.bfloat16)))
    totals, (results, grad_patches, grad_bytes) = lax.scan(per_row, zeros, (patch_states, byte_states, cotangent, patch_lengths, row_lengths))
    return (results, grad_patches, grad_bytes, totals[0], totals[1], totals[2], totals[3], totals[4])
```

```python
import jax
import jax.numpy as jnp
from jax import lax
from jax.sharding import PartitionSpec as P

HEADS = 16
HEAD_DIM = 64
EPSILON = 1e-06
NEGATIVE = -1e30
SCALE = HEAD_DIM ** (-0.5)
BF = jnp.bfloat16
F32 = jnp.float32


def dot(left, right, contract):
    return lax.dot_general(left, right, (contract, ((), ())), preferred_element_type=F32)


def product(left, right):
    return dot(left, right, ((1,), (0,)))


def product_left(left, right):
    return dot(left, right, ((0,), (0,)))


def product_right(left, right):
    return dot(left, right, ((1,), (1,)))


def norm_rows(values, gain):
    factor = lax.rsqrt(jnp.mean(values * values, axis=-1, keepdims=True) + EPSILON)
    return (values * factor * gain).astype(BF), factor


def norm_back(values, factor, gain, gradient):
    weighted = gradient * gain
    grad_gain = jnp.sum(gradient * values * factor, axis=0)
    grad_values = factor * weighted - values * factor**3 * jnp.mean(weighted * values, axis=-1, keepdims=True)
    return grad_values, grad_gain


def heads_of(values):
    return values.reshape(values.shape[0], HEADS, HEAD_DIM).transpose(1, 0, 2)


def rows_of(values):
    return values.transpose(1, 0, 2).reshape(values.shape[1], -1).astype(BF)


def batched(left, right, left_dim, right_dim):
    return lax.dot_general(left, right, (((left_dim,), (right_dim,)), ((0,), (0,))), preferred_element_type=F32)


def attend(queries, keys, values, allowed):
    scores = batched(queries, keys, 2, 2) * SCALE
    weights = jax.nn.softmax(jnp.where(allowed[None], scores, NEGATIVE), axis=-1)
    low = weights.astype(BF)
    return weights, low, rows_of(batched(low, values, 2, 1))


def attend_back(queries, keys, values, weights, low, grad_mixed):
    grad_weights = batched(grad_mixed, values, 2, 2)
    grad_scores = weights * (grad_weights - jnp.sum(weights * grad_weights, axis=-1, keepdims=True))
    grad_scores = grad_scores.astype(BF)
    return (
        rows_of(batched(grad_scores, keys, 2, 1) * SCALE),
        rows_of(batched(grad_scores, queries, 1, 1) * SCALE),
        rows_of(batched(low, grad_mixed, 1, 1)),
    )


def local(patch_states, byte_states, cotangent, patch_lengths, row_lengths, attn_weights, out_weights, gate_up, down_weight, gains):
    everyone = ("dp", "pipe")
    micro = patch_states.shape[0]
    stages = lax.axis_size("pipe")
    share = stages // micro
    place = lax.axis_index("pipe")
    row, part = place // share, place % share
    attn = lax.all_gather(attn_weights, everyone, axis=2, tiled=True)
    outw = lax.all_gather(out_weights, everyone, axis=1, tiled=True)
    gate_stack = lax.all_gather(gate_up, everyone, axis=1, tiled=True)
    down = lax.all_gather(down_weight, everyone, axis=0, tiled=True)

    def mine(source):
        return lax.dynamic_index_in_dim(source, row, 0, keepdims=False)

    def half(values):
        count = values.shape[0] // share
        return lax.dynamic_slice_in_dim(values, part * count, count, 0)

    def weight_grad(left, right):
        return product_left(half(left), half(right)).astype(BF)

    patch = mine(patch_states).astype(F32)
    byte = mine(byte_states).astype(F32)
    cot = mine(cotangent)
    sizes = mine(patch_lengths)
    length = mine(row_lengths)
    patches, bytes_ = patch.shape[0], byte.shape[0]

    nq, fq = norm_rows(patch, gains[0])
    nb, fb = norm_rows(byte, gains[1])
    qc = heads_of(product(nq, attn[0, 0]).astype(BF))
    kc = heads_of(product(nb, attn[0, 1]).astype(BF))
    vc = heads_of(product(nb, attn[0, 2]).astype(BF))
    ends = jnp.cumsum(sizes)[:, None]
    position = jnp.arange(bytes_, dtype=jnp.int32)[None, :]
    window = (position >= ends - sizes[:, None]) & (position < ends)
    pc32, pc, oc = attend(qc, kc, vc, window)
    x1 = (patch + product(oc, outw[0])).astype(BF)
    x1f = x1.astype(F32)
    n1, f1 = norm_rows(x1f, gains[2])
    q = heads_of(product(n1, attn[1, 0]).astype(BF))
    k = heads_of(product(n1, attn[1, 1]).astype(BF))
    v = heads_of(product(n1, attn[1, 2]).astype(BF))
    slot = jnp.arange(patches, dtype=jnp.int32)
    allowed = (slot[None, :] <= slot[:, None]) & (slot[None, :] < length)
    a32, a, o = attend(q, k, v, allowed)
    x2 = (x1f + product(o, outw[1])).astype(BF)
    x2f = x2.astype(F32)
    n2, f2 = norm_rows(x2f, gains[3])
    gate = product(n2, gate_stack[0])
    up = product(n2, gate_stack[1])
    sig = jax.nn.sigmoid(gate)
    hidden = (gate * sig * up).astype(BF)
    result = (x2f + product(hidden, down)).astype(BF)

    grad_down = weight_grad(hidden, cot)
    dh = product_right(cot, down).astype(BF).astype(F32)
    dgate = (dh * up * sig * (1.0 + gate * (1.0 - sig))).astype(BF)
    dup = (dh * gate * sig).astype(BF)
    grad_gate_up = jnp.stack([weight_grad(n2, dgate), weight_grad(n2, dup)])
    dn2 = product_right(dgate, gate_stack[0]) + product_right(dup, gate_stack[1])
    back, gain3 = norm_back(x2f, f2, gains[3], dn2)
    dx2 = (cot.astype(F32) + back).astype(BF)
    do = heads_of(product_right(dx2, outw[1]).astype(BF))
    dq, dk, dv = attend_back(q, k, v, a32, a, do)
    dn1 = product_right(dq, attn[1, 0]) + product_right(dk, attn[1, 1]) + product_right(dv, attn[1, 2])
    back, gain2 = norm_back(x1f, f1, gains[2], dn1)
    dx1 = (dx2.astype(F32) + back).astype(BF)
    doc = heads_of(product_right(dx1, outw[0]).astype(BF))
    dqc, dkc, dvc = attend_back(qc, kc, vc, pc32, pc, doc)
    back, gain0 = norm_back(patch, fq, gains[0], product_right(dqc, attn[0, 0]))
    grad_patch = (dx1.astype(F32) + back).astype(BF)
    back, gain1 = norm_back(byte, fb, gains[1], product_right(dkc, attn[0, 1]) + product_right(dvc, attn[0, 2]))
    grad_byte = back.astype(BF)
    grad_attn = jnp.stack(
        [
            jnp.stack([weight_grad(nq, dqc), weight_grad(nb, dkc), weight_grad(nb, dvc)]),
            jnp.stack([weight_grad(n1, dq), weight_grad(n1, dk), weight_grad(n1, dv)]),
        ]
    )
    grad_out = jnp.stack([weight_grad(oc, dx1), weight_grad(o, dx2)])
    grad_gains = jnp.where(part == 0, jnp.stack([gain0, gain1, gain2, gain3]), 0.0)

    def to_owner(values):
        whole = lax.all_gather(half(values), "pipe", axis=0, tiled=True)
        whole = whole.reshape(micro, -1, values.shape[1])
        count = whole.shape[1] // stages
        return lax.dynamic_slice_in_dim(whole, place * count, count, 1)

    def summed(values, axis):
        return lax.psum_scatter(values, everyone, scatter_dimension=axis, tiled=True).astype(F32)

    return (
        to_owner(result),
        to_owner(grad_patch),
        to_owner(grad_byte),
        summed(grad_attn, 2),
        summed(grad_out, 1),
        summed(grad_gate_up, 1),
        summed(grad_down, 0),
        summed(grad_gains, 1),
    )


def solution(mesh):
    placed = (
        P("dp", None, None),
        P("dp", None, None),
        P("dp", None, None),
        P("dp", None),
        P("dp"),
        P(None, None, ("dp", "pipe"), None),
        P(None, ("dp", "pipe"), None),
        P(None, ("dp", "pipe"), None),
        P(("dp", "pipe"), None),
        P(),
    )
    return jax.shard_map(
        local,
        mesh=mesh,
        in_specs=placed,
        out_specs=(
            P("dp", "pipe", None),
            P("dp", "pipe", None),
            P("dp", "pipe", None),
            P(None, None, ("dp", "pipe"), None),
            P(None, ("dp", "pipe"), None),
            P(None, ("dp", "pipe"), None),
            P(("dp", "pipe"), None),
            P(None, ("dp", "pipe")),
        ),
        check_vma=False,
    )
```

```python
import functools
from types import SimpleNamespace

import jax
import jax.numpy as jnp
from jax import lax
from jax.experimental import pallas as pl
from jax.experimental.pallas import tpu as pltpu
from jax.sharding import PartitionSpec as P

HEADS = 16
HEAD_DIM = 64
EPSILON = 1e-06
NEGATIVE = -1e30
SCALE = HEAD_DIM ** (-0.5)
BF = jnp.bfloat16
F32 = jnp.float32
MESH = pl.DeviceIdType.MESH


def dot(left, right, contract):
    return lax.dot_general(left, right, (contract, ((), ())), preferred_element_type=F32)


def product(left, right):
    return dot(left, right, ((1,), (0,)))


def product_left(left, right):
    return dot(left, right, ((0,), (0,)))


def product_right(left, right):
    return dot(left, right, ((1,), (1,)))


def norm_rows(values, gain):
    factor = lax.rsqrt(jnp.mean(values * values, axis=-1, keepdims=True) + EPSILON)
    return (values * factor * gain).astype(BF), factor


def norm_back(values, factor, gain, gradient):
    weighted = gradient * gain
    grad_gain = jnp.sum(gradient * values * factor, axis=0)
    grad_values = factor * weighted - values * factor**3 * jnp.mean(weighted * values, axis=-1, keepdims=True)
    return grad_values, grad_gain


def heads_of(values):
    return values.reshape(values.shape[0], HEADS, HEAD_DIM).transpose(1, 0, 2)


def rows_of(values):
    return values.transpose(1, 0, 2).reshape(values.shape[1], -1).astype(BF)


def batched(left, right, left_dim, right_dim):
    return lax.dot_general(left, right, (((left_dim,), (right_dim,)), ((0,), (0,))), preferred_element_type=F32)


def attend(queries, keys, values, allowed):
    scores = batched(queries, keys, 2, 2) * SCALE
    weights = jax.nn.softmax(jnp.where(allowed[None], scores, NEGATIVE), axis=-1)
    low = weights.astype(BF)
    return weights, low, rows_of(batched(low, values, 2, 1))


def attend_back(queries, keys, values, weights, low, grad_mixed):
    grad_weights = batched(grad_mixed, values, 2, 2)
    grad_scores = weights * (grad_weights - jnp.sum(weights * grad_weights, axis=-1, keepdims=True))
    grad_scores = grad_scores.astype(BF)
    return (
        rows_of(batched(grad_scores, keys, 2, 1) * SCALE),
        rows_of(batched(grad_scores, queries, 1, 1) * SCALE),
        rows_of(batched(low, grad_mixed, 1, 1)),
    )


def gathered_step(patch_states, byte_states, cotangent, patch_lengths, row_lengths, attn_weights, out_weights, gate_up, down_weight, gains):
    everyone = ("dp", "pipe")
    micro = patch_states.shape[0]
    stages = lax.axis_size("pipe")
    share = stages // micro
    place = lax.axis_index("pipe")
    row, part = place // share, place % share
    attn = lax.all_gather(attn_weights, everyone, axis=2, tiled=True)
    outw = lax.all_gather(out_weights, everyone, axis=1, tiled=True)
    gate_stack = lax.all_gather(gate_up, everyone, axis=1, tiled=True)
    down = lax.all_gather(down_weight, everyone, axis=0, tiled=True)

    def mine(source):
        return lax.dynamic_index_in_dim(source, row, 0, keepdims=False)

    def half(values):
        count = values.shape[0] // share
        return lax.dynamic_slice_in_dim(values, part * count, count, 0)

    def weight_grad(left, right):
        return product_left(half(left), half(right)).astype(BF)

    patch = mine(patch_states).astype(F32)
    byte = mine(byte_states).astype(F32)
    cot = mine(cotangent)
    sizes = mine(patch_lengths)
    length = mine(row_lengths)
    patches, bytes_ = patch.shape[0], byte.shape[0]

    nq, fq = norm_rows(patch, gains[0])
    nb, fb = norm_rows(byte, gains[1])
    qc = heads_of(product(nq, attn[0, 0]).astype(BF))
    kc = heads_of(product(nb, attn[0, 1]).astype(BF))
    vc = heads_of(product(nb, attn[0, 2]).astype(BF))
    ends = jnp.cumsum(sizes)[:, None]
    position = jnp.arange(bytes_, dtype=jnp.int32)[None, :]
    window = (position >= ends - sizes[:, None]) & (position < ends)
    pc32, pc, oc = attend(qc, kc, vc, window)
    x1 = (patch + product(oc, outw[0])).astype(BF)
    x1f = x1.astype(F32)
    n1, f1 = norm_rows(x1f, gains[2])
    q = heads_of(product(n1, attn[1, 0]).astype(BF))
    k = heads_of(product(n1, attn[1, 1]).astype(BF))
    v = heads_of(product(n1, attn[1, 2]).astype(BF))
    slot = jnp.arange(patches, dtype=jnp.int32)
    allowed = (slot[None, :] <= slot[:, None]) & (slot[None, :] < length)
    a32, a, o = attend(q, k, v, allowed)
    x2 = (x1f + product(o, outw[1])).astype(BF)
    x2f = x2.astype(F32)
    n2, f2 = norm_rows(x2f, gains[3])
    gate = product(n2, gate_stack[0])
    up = product(n2, gate_stack[1])
    sig = jax.nn.sigmoid(gate)
    hidden = (gate * sig * up).astype(BF)
    result = (x2f + product(hidden, down)).astype(BF)

    grad_down = weight_grad(hidden, cot)
    dh = product_right(cot, down).astype(BF).astype(F32)
    dgate = (dh * up * sig * (1.0 + gate * (1.0 - sig))).astype(BF)
    dup = (dh * gate * sig).astype(BF)
    grad_gate_up = jnp.stack([weight_grad(n2, dgate), weight_grad(n2, dup)])
    dn2 = product_right(dgate, gate_stack[0]) + product_right(dup, gate_stack[1])
    back, gain3 = norm_back(x2f, f2, gains[3], dn2)
    dx2 = (cot.astype(F32) + back).astype(BF)
    do = heads_of(product_right(dx2, outw[1]).astype(BF))
    dq, dk, dv = attend_back(q, k, v, a32, a, do)
    dn1 = product_right(dq, attn[1, 0]) + product_right(dk, attn[1, 1]) + product_right(dv, attn[1, 2])
    back, gain2 = norm_back(x1f, f1, gains[2], dn1)
    dx1 = (dx2.astype(F32) + back).astype(BF)
    doc = heads_of(product_right(dx1, outw[0]).astype(BF))
    dqc, dkc, dvc = attend_back(qc, kc, vc, pc32, pc, doc)
    back, gain0 = norm_back(patch, fq, gains[0], product_right(dqc, attn[0, 0]))
    grad_patch = (dx1.astype(F32) + back).astype(BF)
    back, gain1 = norm_back(byte, fb, gains[1], product_right(dkc, attn[0, 1]) + product_right(dvc, attn[0, 2]))
    grad_byte = back.astype(BF)
    grad_attn = jnp.stack(
        [
            jnp.stack([weight_grad(nq, dqc), weight_grad(nb, dkc), weight_grad(nb, dvc)]),
            jnp.stack([weight_grad(n1, dq), weight_grad(n1, dk), weight_grad(n1, dv)]),
        ]
    )
    grad_out = jnp.stack([weight_grad(oc, dx1), weight_grad(o, dx2)])
    grad_gains = jnp.where(part == 0, jnp.stack([gain0, gain1, gain2, gain3]), 0.0)

    def to_owner(values):
        whole = lax.all_gather(half(values), "pipe", axis=0, tiled=True)
        whole = whole.reshape(micro, -1, values.shape[1])
        count = whole.shape[1] // stages
        return lax.dynamic_slice_in_dim(whole, place * count, count, 1)

    def summed(values, axis):
        return lax.psum_scatter(values, everyone, scatter_dimension=axis, tiled=True).astype(F32)

    return (
        to_owner(result),
        to_owner(grad_patch),
        to_owner(grad_byte),
        summed(grad_attn, 2),
        summed(grad_out, 1),
        summed(grad_gate_up, 1),
        summed(grad_down, 0),
        summed(grad_gains, 1),
    )


LINE = 4
SIDE = 2
RANKS = 4
GROUPS = LINE * SIDE
ROWS_HERE = 2
PATCHES = 256
BYTES = 640
WIDTH = 1024
MINE = WIDTH // RANKS
HEADS_MINE = MINE // HEAD_DIM
TOKENS = PATCHES // RANKS
TOKENS_B = BYTES // RANKS
SHARD = WIDTH // (GROUPS * RANKS)
SEG = SHARD * RANKS
UNITS = 88
PADDED = 96
HIDDEN = GROUPS * PADDED
NSEM = 512
BIG = (("attn0", 0), ("attn1", 1))


def scratch_plan():
    b = lambda *shape: pltpu.VMEM(shape, BF)
    f = lambda *shape: pltpu.VMEM(shape, F32)
    plan = dict(
        sem=pltpu.SemaphoreType.DMA((NSEM,)),
        wa=b(6, WIDTH, MINE),
        won=b(2, LINE, SIDE, SHARD, WIDTH),
        woh=b(2, 2, 2, HEAD_DIM, WIDTH),
        wg=b(WIDTH, 2 * HIDDEN),
        wd=b(HIDDEN, WIDTH),
        da=b(6, WIDTH, MINE),
        don=b(2, GROUPS, SHARD, WIDTH),
        dg=b(WIDTH, 2 * HIDDEN),
        dd=b(HIDDEN, WIDTH),
        xa=b(6, LINE, SEG, MINE),
        xo=b(2, LINE, SHARD, WIDTH),
        xg=b(LINE, SEG, 2 * HIDDEN),
        xd=b(LINE, PADDED, WIDTH),
        za=b(6, LINE + 1, SEG, MINE),
        zo=b(2, LINE + 1, SHARD, WIDTH),
        zg=b(LINE + 1, SEG, 2 * HIDDEN),
        zd=b(LINE + 1, PADDED, WIDTH),
        nq=b(ROWS_HERE, PATCHES, WIDTH),
        nb=b(ROWS_HERE, BYTES, WIDTH),
        qc=b(ROWS_HERE, PATCHES, MINE),
        kc=b(ROWS_HERE, BYTES, MINE),
        vc=b(ROWS_HERE, BYTES, MINE),
        oc=b(ROWS_HERE, PATCHES, MINE),
        x1=b(8, TOKENS, WIDTH),
        n1=b(ROWS_HERE, PATCHES, WIDTH),
        qkv=b(3, ROWS_HERE, PATCHES, MINE),
        o=b(ROWS_HERE, PATCHES, MINE),
        x2=b(8, TOKENS, WIDTH),
        n2=b(ROWS_HERE, PATCHES, WIDTH),
        fac=b(ROWS_HERE, PATCHES, 2 * HIDDEN),
        hid=b(ROWS_HERE, PATCHES, HIDDEN),
        dx2=b(8, TOKENS, WIDTH),
        dx1=b(8, TOKENS, WIDTH),
        dmix=b(ROWS_HERE, PATCHES, MINE),
        dqkv=b(3, ROWS_HERE, PATCHES, MINE),
        dqc=b(ROWS_HERE, PATCHES, MINE),
        dkc=b(ROWS_HERE, BYTES, MINE),
        dvc=b(ROWS_HERE, BYTES, MINE),
        p=b(8, TOKENS, WIDTH),
        r1=b(ROWS_HERE, 2, TOKENS, WIDTH),
        q2=b(ROWS_HERE, TOKENS, WIDTH),
        r2=b(ROWS_HERE, TOKENS, WIDTH),
        bp=b(8, TOKENS_B, WIDTH),
        br1=b(ROWS_HERE, 2, TOKENS_B, WIDTH),
        bq2=b(ROWS_HERE, TOKENS_B, WIDTH),
        br2=b(ROWS_HERE, TOKENS_B, WIDTH),
        bown=b(ROWS_HERE, TOKENS_B, WIDTH),
        gn=f(8, WIDTH),
        gs=f(5, 8, WIDTH),
        gr=f(5, 8, WIDTH),
    )
    return plan


INS = ("patch", "byte", "cot", "lens", "gains", "wa_in", "wg_in", "wo_in", "wd_in")
OUTS = ("out", "gpatch", "gbyte", "g_attn", "g_out", "g_gate", "g_down", "g_gain")


def step_kernel(names, *refs):
    m = SimpleNamespace(**dict(zip(INS + OUTS + tuple(names), refs)))
    dp, pipe = lax.axis_index("dp"), lax.axis_index("pipe")
    z, x, y, c = dp // SIDE, dp % SIDE, pipe // 2, pipe % 2
    at = lambda z, x, y, c: (z * SIDE + x, y * 2 + c)
    sibling, across, aside = at(z, x, y, 1 - c), at(z, x, 1 - y, c), at(z, 1 - x, y, c)
    right, left = at((z + 1) % LINE, x, y, c), at((z + LINE - 1) % LINE, x, y, c)
    corner, mirror, pair = at(z, x, 1 - y, 1 - c), at(LINE - 1 - z, x, y, c), at(z + 1 - 2 * (z % 2), x, y, c)
    counter = [0]

    def take(count=1):
        first = counter[0]
        counter[0] += count
        assert counter[0] <= NSEM
        return first

    unfinished = []

    def remote(src, dst, device, send=None, recv=None):
        send = take() if send is None else send
        recv = take() if recv is None else recv
        return pltpu.make_async_remote_copy(
            src_ref=src, dst_ref=dst, send_sem=m.sem.at[send], recv_sem=m.sem.at[recv], device_id=device, device_id_type=MESH
        )

    def begin(copy):
        copy.start()
        unfinished.append(copy.wait_send)
        return copy

    def near(src, dst):
        copy = pltpu.make_async_copy(src, dst, m.sem.at[take()])
        copy.start()
        return copy

    barrier = pltpu.get_barrier_semaphore()
    for device in (sibling, across, corner, aside, mirror):
        pl.semaphore_signal(barrier, inc=1, device_id=device, device_id_type=MESH)

    @pl.when(z < LINE - 1)
    def _():
        pl.semaphore_signal(barrier, inc=1, device_id=right, device_id_type=MESH)

    @pl.when(z > 0)
    def _():
        pl.semaphore_signal(barrier, inc=1, device_id=left, device_id_type=MESH)

    bytes_in = near(m.byte, m.bp)
    local_out = near(m.wo_in, m.won.at[:, z, x])
    local_down = near(m.wd_in, m.wd.at[pl.ds(dp * PADDED, PADDED)])
    pl.semaphore_wait(barrier, 5 + (z < LINE - 1).astype(jnp.int32) + (z > 0).astype(jnp.int32))

    def attn_part(layer):
        src = lambda q: m.wa_in.at[q, pl.ds(3 * layer, 3)]
        dst = m.wa.at[pl.ds(3 * layer, 3), pl.ds(dp * SEG + pipe * SHARD, SHARD)]
        return src, dst

    def gate_part():
        return (lambda q: m.wg_in.at[q]), m.wg.at[pl.ds(dp * SEG + pipe * SHARD, SHARD)]

    def spread(part):
        src, dst = part
        copies = [near(src(pipe), dst)]
        for device in (across, corner, sibling):
            copies.append(begin(remote(src(device[1]), dst, device)))
        return copies

    def arrived(copies):
        copies[0].wait()
        for copy in copies[1:]:
            copy.wait_recv()

    exchange0, exchange1 = spread(attn_part(0)), spread(attn_part(1))
    exchange2 = spread(gate_part())

    class Gather:
        def __init__(self, view):
            self.view = view
            self.sx, self.rx = take(LINE), take(LINE)
            self.sr, self.rr = take(LINE), take(LINE)
            self.sl, self.rl = take(LINE), take(LINE)

        def copy(self, block, device, send, recv):
            there = self.view(block * SIDE + x)
            return remote(there, there, device, send + block, recv + block)

        def aside(self, block):
            return self.copy(block, aside, self.sx, self.rx)

        def right(self, block):
            return self.copy(block, right, self.sr, self.rr)

        def left(self, block):
            return self.copy(block, left, self.sl, self.rl)

        def start(self):
            self.aside(z).start()

            @pl.when(z < LINE - 1)
            def _():
                self.right(z).start()

            @pl.when(z > 0)
            def _():
                self.left(z).start()

        def hop(self, k):
            @pl.when(z - k >= 0)
            def _():
                self.right(z - k).wait_recv()
                self.aside(z - k).start()

                @pl.when(z < LINE - 1)
                def _():
                    self.right(z - k).start()

            @pl.when(z + k < LINE)
            def _():
                self.left(z + k).wait_recv()
                self.aside(z + k).start()

                @pl.when(z > 0)
                def _():
                    self.left(z + k).start()

        def ready(self):
            for block in range(LINE):
                self.aside(block).wait_recv()

        def finish(self):
            for block in range(LINE):
                self.aside(block).wait_send()

                @pl.when((z < LINE - 1) & (z >= block))
                def _():
                    self.right(block).wait_send()

                @pl.when((z > 0) & (z <= block))
                def _():
                    self.left(block).wait_send()

    g_out0 = Gather(lambda d: m.won.at[0, d // SIDE, d % SIDE])
    g_out1 = Gather(lambda d: m.won.at[1, d // SIDE, d % SIDE])
    g_attn0 = Gather(lambda d: m.wa.at[pl.ds(0, 3), pl.ds(d * SEG, SEG)])
    g_attn1 = Gather(lambda d: m.wa.at[pl.ds(3, 3), pl.ds(d * SEG, SEG)])
    g_gate = Gather(lambda d: m.wg.at[pl.ds(d * SEG, SEG)])
    g_down = Gather(lambda d: m.wd.at[pl.ds(d * PADDED, PADDED)])

    def begin_after(copies, gather):
        arrived(copies)
        gather.start()

    queue = []

    def pump(count):
        for _ in range(min(count, len(queue))):
            queue.pop(0)()

    def swap_out(layer):
        mine, there = m.won.at[layer, pl.ds(2 * c, 2)], m.woh.at[layer, :, :, pl.ds(c * SHARD, SHARD)]
        keep = near(mine, there)
        give = remote(m.won.at[layer, pl.ds(2 * (1 - c), 2)], there, sibling)
        give.start()
        return keep, give

    lane = lax.broadcasted_iota(jnp.int32, (1, MINE), 1) // HEAD_DIM
    head_mask = [(lane == j).astype(F32).astype(BF) for j in range(HEADS_MINE)]

    def gain(index):
        return m.gains[index : index + 1, :]

    def factor_of(values):
        return lax.rsqrt(jnp.mean(values * values, axis=-1, keepdims=True) + EPSILON)

    def normed(values, index):
        values = values.astype(F32)
        return (values * factor_of(values) * gain(index)).astype(BF)

    def norm_back(values, gradient, index):
        values = values.astype(F32)
        factor = factor_of(values)
        weighted = gradient * gain(index)
        m.gn[index : index + 1, :] += jnp.sum(gradient * values * factor, axis=0, keepdims=True)
        return factor * weighted - values * (factor * factor * factor) * jnp.mean(weighted * values, axis=-1, keepdims=True)

    def normed_rows(src, dst, index, r):
        for part in range(RANKS):
            for half in range(2):
                rows = pl.ds(half * (TOKENS // 2), TOKENS // 2)
                dst[r, pl.ds(part * TOKENS + half * (TOKENS // 2), TOKENS // 2)] = normed(src[4 * r + part, rows], index)

    class Reduce:
        def __init__(self, p, r1, q2, r2, tokens):
            self.p, self.r1, self.q2, self.r2, self.tokens = p, r1, q2, r2, tokens
            self.first, self.second = {}, {}

        def give(self, r):
            self.first[r] = [
                remote(self.p.at[4 * r + 2 * side + 1 - c], self.r1.at[r, side], sibling) for side in range(2)
            ]
            for copy in self.first[r]:
                copy.start()

        def cross(self, r):
            for copy in self.first[r]:
                copy.wait_recv()
            other = 4 * r + 2 * (1 - y) + c
            self.q2[r] = (self.p[other].astype(F32) + self.r1[r, 1 - y].astype(F32)).astype(BF)
            self.second[r] = remote(self.q2.at[r], self.r2.at[r], across)
            self.second[r].start()

        def arrive(self, r):
            self.second[r].wait_recv()

        def free(self):
            for r in range(ROWS_HERE):
                for copy in self.first[r]:
                    copy.wait_send()
                self.second[r].wait_send()

        def total(self, r, rows):
            own = 4 * r + pipe
            return (
                self.p[own, rows].astype(F32) + self.r1[r, y, rows].astype(F32) + self.r2[r, rows].astype(F32)
            )

    class Share:
        def __init__(self, values):
            self.values, self.copies, self.last = values, {}, {}

        def give(self, r):
            there = self.values.at[4 * r + pipe]
            self.copies[r] = [begin(remote(there, there, across)), begin(remote(there, there, sibling))]

        def relay(self, r):
            self.copies[r][0].wait_recv()
            there = self.values.at[4 * r + 2 * (1 - y) + c]
            self.last[r] = begin(remote(there, there, sibling))

        def ready(self, r):
            self.copies[r][1].wait_recv()
            self.last[r].wait_recv()

    halves = [pl.ds(h * (TOKENS // 2), TOKENS // 2) for h in range(2)]

    def to_owner(reduce, left_of, right_ref, r, right_transposed=False):
        for n in range(4):
            cols = pl.ds(n * 256, 256)
            reduce.p[4 * r : 4 * r + 4, :, cols] = left_of(r, n).astype(BF).reshape(4, reduce.tokens, 256)
        reduce.give(r)

    queue_start = [
        lambda: (local_out.wait(), g_out0.start()),
        lambda: begin_after(exchange0, g_attn0),
    ]
    for step in queue_start:
        step()
    m.gn[...] = jnp.zeros_like(m.gn)

    @pl.loop(0, ROWS_HERE * PATCHES // 32)
    def _(i):
        rows = pl.ds((i % 8) * 32, 32)
        m.nq[i // 8, rows] = normed(m.patch[i // 8, rows], 0)

    bytes_in.wait()

    @pl.loop(0, 8)
    def _(i):
        for part in range(5):
            rows = pl.ds(part * 32, 32)
            m.nb[i // 4, pl.ds((i % 4) * TOKENS_B + part * 32, 32)] = normed(m.bp[i, rows], 1)

    def hops(gather):
        return [functools.partial(gather.hop, k) for k in (1, 2, 3)]

    h_out0, h_attn0, h_out1, h_attn1, h_gate, h_down = map(hops, (g_out0, g_attn0, g_out1, g_attn1, g_gate, g_down))
    queue += [h_out0[0], g_out1.start, h_attn0[0], h_out0[1], h_attn0[1], h_out0[2]]
    queue += [lambda: begin_after(exchange1, g_attn1), h_attn0[2]]
    pump(8)
    queue += [h_out1[0], h_attn1[0], h_out1[1], lambda: begin_after(exchange2, g_gate), h_attn1[1], h_out1[2], h_attn1[2]]
    queue += [lambda: (local_down.wait(), g_down.start()), h_gate[0], h_gate[1], h_gate[2]] + h_down
    g_out0.ready()
    swap0 = swap_out(0)
    g_attn0.ready()

    for r in range(ROWS_HERE):
        m.qc[r] = product(m.nq[r], m.wa[0]).astype(BF)

    @pl.loop(0, 4)
    def _(i):
        rows = pl.ds((i % 2) * (BYTES // 2), BYTES // 2)
        block = m.nb[i // 2, rows]
        m.kc[i // 2, rows] = product(block, m.wa[1]).astype(BF)
        m.vc[i // 2, rows] = product(block, m.wa[2]).astype(BF)

    pump(2)

    def window(r):
        sizes = m.lens[pl.ds(r, 1), :]
        i = lax.broadcasted_iota(jnp.int32, (PATCHES, PATCHES), 0)
        j = lax.broadcasted_iota(jnp.int32, (PATCHES, PATCHES), 1)
        first = jnp.sum(jnp.where(j < i, sizes, 0.0), axis=1, keepdims=True)
        last = jnp.sum(jnp.where(j <= i, sizes, 0.0), axis=1, keepdims=True)
        position = lax.broadcasted_iota(jnp.int32, (PATCHES, BYTES), 1).astype(F32)
        return (position >= first) & (position < last)

    def causal(r):
        length = m.lens[pl.ds(ROWS_HERE + r, 1), :]
        i = lax.broadcasted_iota(jnp.int32, (PATCHES, PATCHES), 0)
        j = lax.broadcasted_iota(jnp.int32, (PATCHES, PATCHES), 1)
        return (j <= i) & (j.astype(F32) < length)

    def weights_of(query, keys, allowed):
        scores = jnp.where(allowed, product_right(query, keys) * SCALE, NEGATIVE)
        raised = jnp.exp(scores - jnp.max(scores, axis=-1, keepdims=True))
        return raised / jnp.sum(raised, axis=-1, keepdims=True)

    def attend(r, allowed, queries, keys, values, mixed):
        total = None
        for j in range(HEADS_MINE):
            low = weights_of(queries[r] * head_mask[j], keys[r], allowed).astype(BF)
            term = product(low, values[r] * head_mask[j])
            total = term if total is None else total + term
        mixed[r] = total.astype(BF)

    def attend_back(r, allowed, queries, keys, values, grad, dq, dk, dv):
        sums = [None, None, None]
        for j in range(HEADS_MINE):
            query, mixed = queries[r] * head_mask[j], grad[r] * head_mask[j]
            weights = weights_of(query, keys[r], allowed)
            grad_weights = product_right(mixed, values[r])
            grad_scores = weights * (grad_weights - jnp.sum(weights * grad_weights, axis=-1, keepdims=True))
            grad_scores = grad_scores.astype(BF)
            terms = (
                product(grad_scores, keys[r] * head_mask[j]),
                product_left(grad_scores, query),
                product_left(weights.astype(BF), mixed),
            )
            sums = [t if s is None else s + t for s, t in zip(sums, terms)]
        dq[r] = (sums[0] * SCALE).astype(BF)
        dk[r] = (sums[1] * SCALE).astype(BF)
        dv[r] = sums[2].astype(BF)

    @pl.loop(0, ROWS_HERE)
    def _(r):
        attend(r, window(r), m.qc, m.kc, m.vc, m.oc)

    pump(2)
    for copy in swap0[:1]:
        copy.wait()
    swap0[1].wait_recv()

    def out_rows(layer):
        return lambda n: m.woh[layer, :, :, :, pl.ds(n * 256, 256)].reshape(MINE, 256)

    def residual(reduce, share, base, result, r):
        reduce.arrive(r)
        for rows in halves:
            result[4 * r + pipe, rows] = (base(r, rows) + reduce.total(r, rows)).astype(BF)
        share.give(r)

    first_sum, first_share = Reduce(m.p, m.r1, m.q2, m.r2, TOKENS), Share(m.x1)
    for r in range(ROWS_HERE):
        to_owner(first_sum, lambda r, n: product(m.oc[r], out_rows(0)(n)), None, r)
    for r in range(ROWS_HERE):
        first_sum.cross(r)
    own_patch = lambda r, rows: m.patch[r, pl.ds(pipe * TOKENS + rows.start, TOKENS // 2)].astype(F32)
    for r in range(ROWS_HERE):
        residual(first_sum, first_share, own_patch, m.x1, r)
    pump(2)
    for r in range(ROWS_HERE):
        first_share.relay(r)
    for r in range(ROWS_HERE):
        first_share.ready(r)
        normed_rows(m.x1, m.n1, 2, r)

    pump(2)
    g_out1.ready()
    swap1 = swap_out(1)
    g_attn1.ready()
    for r in range(ROWS_HERE):
        for part in range(3):
            m.qkv[part, r] = product(m.n1[r], m.wa[3 + part]).astype(BF)
    queries, keys, values = m.qkv.at[0], m.qkv.at[1], m.qkv.at[2]

    @pl.loop(0, ROWS_HERE)
    def _(r):
        attend(r, causal(r), queries, keys, values, m.o)

    swap1[0].wait()
    swap1[1].wait_recv()
    first_sum.free()
    second_sum, second_share = Reduce(m.p, m.r1, m.q2, m.r2, TOKENS), Share(m.x2)
    for r in range(ROWS_HERE):
        to_owner(second_sum, lambda r, n: product(m.o[r], out_rows(1)(n)), None, r)
    for r in range(ROWS_HERE):
        second_sum.cross(r)
    own_of = lambda values: lambda r, rows: values[4 * r + pipe, rows].astype(F32)
    for r in range(ROWS_HERE):
        residual(second_sum, second_share, own_of(m.x1), m.x2, r)
    pump(1)
    for r in range(ROWS_HERE):
        second_share.relay(r)
    for r in range(ROWS_HERE):
        second_share.ready(r)
        normed_rows(m.x2, m.n2, 3, r)

    pump(2)
    g_gate.ready()
    tiles = HIDDEN // 256
    for r in range(ROWS_HERE):

        @pl.loop(0, tiles)
        def _(n, r=r):
            first = pl.ds(pl.multiple_of(n * 256, 256), 256)
            later = pl.ds(pl.multiple_of(HIDDEN + n * 256, 256), 256)
            gate = product(m.n2[r], m.wg[:, first])
            up = product(m.n2[r], m.wg[:, later])
            sig = jax.nn.sigmoid(gate)
            silu = gate * sig
            m.hid[r, :, first] = (silu * up).astype(BF)
            m.fac[r, :, first] = (up * sig * (1.0 + gate * (1.0 - sig))).astype(BF)
            m.fac[r, :, later] = silu.astype(BF)

    class Scatter:
        def __init__(self, mine, xbuf, zbuf, rows):
            self.mine, self.xbuf, self.zbuf, self.rows = mine, xbuf, zbuf, rows
            self.sx, self.rx = take(LINE), take(LINE)
            self.sr, self.rr = take(LINE), take(LINE)
            self.sl, self.rl = take(LINE), take(LINE)

        def aside(self, block):
            return remote(self.mine(block * SIDE + 1 - x), self.xbuf(block), aside, self.sx + block, self.rx + block)

        def start(self):
            for block in (3, 0, 2, 1):
                self.aside(block).start()

        def add(self, into, values):
            into[...] = (into[...].astype(F32) + values[...].astype(F32)).astype(BF)

        def add_x(self, block):
            self.aside(block).wait_recv()
            self.add(self.mine(block * SIDE + x), self.xbuf(block))

        def right(self, block):
            return remote(self.mine(block * SIDE + x), self.zbuf(block), right, self.sr + block, self.rr + block)

        def left(self, block, slot):
            return remote(self.mine(block * SIDE + x), self.zbuf(slot), left, self.sl + block, self.rl + block)

        def go_right(self, block):
            @pl.when((z > 0) & (z <= block))
            def _():
                self.right(block).wait_recv()
                self.add(self.mine(block * SIDE + x), self.zbuf(block))

            @pl.when(z < block)
            def _():
                self.right(block).start()

        def go_left(self, block):
            @pl.when((z < LINE - 1) & (z >= block))
            def _():
                slot = jnp.where(z == block, LINE, block)
                self.left(block, slot).wait_recv()
                self.add(self.mine(block * SIDE + x), self.zbuf(slot))

            @pl.when(z > block)
            def _():
                self.left(block, jnp.where(z - 1 == block, LINE, block)).start()

        def steps(self):
            take_x = lambda block: functools.partial(self.add_x, block)
            return [
                lambda: (self.add_x(3), self.go_right(3)),
                lambda: (self.add_x(0), self.go_left(0)),
                lambda: (self.add_x(2), self.go_right(2)),
                lambda: (self.add_x(1), self.go_left(1)),
                lambda: (self.go_right(1), self.go_left(2)),
            ]

        def finish(self):
            for block in range(LINE):
                self.aside(block).wait_send()

                @pl.when(z < block)
                def _():
                    self.right(block).wait_send()

                @pl.when(z > block)
                def _():
                    self.left(block, 0).wait_send()

    s_down = Scatter(lambda d: m.dd.at[pl.ds(d * PADDED, PADDED)], lambda b: m.xd.at[b], lambda b: m.zd.at[b], PADDED)

    @pl.loop(0, tiles)
    def _(n):
        cols = pl.ds(pl.multiple_of(n * 256, 256), 256)
        for half in range(2):
            wide = pl.ds(half * 512, 512)
            total = product_left(m.hid[0, :, cols], m.cot[0, :, wide]) + product_left(m.hid[1, :, cols], m.cot[1, :, wide])
            m.dd[cols, wide] = total.astype(BF)

    pump(len(queue))
    s_down.start()
    tasks = s_down.steps()

    def work(count):
        for _ in range(min(count, len(tasks))):
            tasks.pop(0)()

    g_down.ready()
    for r in range(ROWS_HERE):

        @pl.loop(0, tiles)
        def _(n, r=r):
            first = pl.ds(pl.multiple_of(n * 256, 256), 256)
            later = pl.ds(pl.multiple_of(HIDDEN + n * 256, 256), 256)
            grad = product_right(m.cot[r], m.wd[first, :]).astype(BF).astype(F32)
            m.fac[r, :, first] = (grad * m.fac[r, :, first].astype(F32)).astype(BF)
            m.fac[r, :, later] = (grad * m.fac[r, :, later].astype(F32)).astype(BF)

    second_sum.free()
    third_sum, third_share = Reduce(m.p, m.r1, m.q2, m.r2, TOKENS), Share(m.dx2)
    for r in range(ROWS_HERE):
        to_owner(third_sum, lambda r, n: product_right(m.fac[r], m.wg[n * 256 : n * 256 + 256, :]), None, r)

    s_gate = Scatter(lambda d: m.dg.at[pl.ds(d * SEG, SEG)], lambda b: m.xg.at[b], lambda b: m.zg.at[b], SEG)

    def gate_grad(i):
        n = i % (2 * tiles)
        rows = pl.ds(pl.multiple_of((i // (2 * tiles)) * 256, 256), 256)
        cols = pl.ds(pl.multiple_of(n * 256, 256), 256)
        total = product_left(m.n2[0, :, rows], m.fac[0, :, cols]) + product_left(m.n2[1, :, rows], m.fac[1, :, cols])
        m.dg[rows, cols] = total.astype(BF)

    pl.loop(0, 4 * tiles)(gate_grad)
    for r in range(ROWS_HERE):
        third_sum.cross(r)
    pl.loop(4 * tiles, 8 * tiles)(gate_grad)
    s_gate.start()

    def gradient_in(reduce, share, base, values, index, result, r):
        reduce.arrive(r)
        for rows in halves:
            back = norm_back(values(r, rows), reduce.total(r, rows), index)
            result(r, rows, (base(r, rows) + back).astype(BF))
        if share is not None:
            share.give(r)

    def into(ref):
        def store(r, rows, value):
            ref[4 * r + pipe, rows] = value

        return store

    own_cot = lambda r, rows: m.cot[r, pl.ds(pipe * TOKENS + rows.start, TOKENS // 2)].astype(F32)
    for r in range(ROWS_HERE):
        gradient_in(third_sum, third_share, own_cot, own_of(m.x2), 3, into(m.dx2), r)

    out_sum = Reduce(m.bp.at[:, pl.ds(0, TOKENS)], m.br1.at[:, :, pl.ds(0, TOKENS)], m.bq2.at[:, pl.ds(0, TOKENS)], m.br2.at[:, pl.ds(0, TOKENS)], TOKENS)
    for r in range(ROWS_HERE):
        to_owner(out_sum, lambda r, n: product(m.hid[r], m.wd[:, n * 256 : n * 256 + 256]), None, r)
    for r in range(ROWS_HERE):
        third_share.relay(r)
    for r in range(ROWS_HERE):
        out_sum.cross(r)

    def rows_of(ref, r):
        return ref[4 * r : 4 * r + 4].reshape(PATCHES, WIDTH)

    def mixed_back(share, grads, layer, r):
        share.ready(r)
        m.dmix[r] = product_right(rows_of(grads, r), m.woh[layer].reshape(MINE, WIDTH)).astype(BF)

    for r in range(ROWS_HERE):
        mixed_back(third_share, m.dx2, 1, r)

    @pl.loop(0, ROWS_HERE)
    def _(r):
        attend_back(r, causal(r), queries, keys, values, m.dmix, m.dqkv.at[0], m.dqkv.at[1], m.dqkv.at[2])

    third_sum.free()
    fourth_sum, fourth_share = Reduce(m.p, m.r1, m.q2, m.r2, TOKENS), Share(m.dx1)

    def attn_back(r, n, layer, parts):
        rows = pl.ds(n * 256, 256)
        total = None
        for part, ref in parts:
            term = product_right(ref[r], m.wa[3 * layer + part, rows, :])
            total = term if total is None else total + term
        return total

    for r in range(ROWS_HERE):
        to_owner(fourth_sum, lambda r, n: attn_back(r, n, 1, [(i, m.dqkv.at[i]) for i in range(3)]), None, r)

    def own_half(layer, which):
        return m.won.at[layer, :, which]

    def out_grad(layer, mixed, grads):
        (g_out0, g_out1)[layer].finish()
        (swap0, swap1)[layer][1].wait_send()
        for n in range(4):
            cols = pl.ds(n * 256, 256)
            total = None
            for r in range(ROWS_HERE):
                term = product_left(mixed[r], grads[4 * r : 4 * r + 4, :, cols].reshape(PATCHES, 256))
                total = term if total is None else total + term
            m.won[layer, :, :, :, cols] = total.astype(BF).reshape(LINE, SIDE, SHARD, 256)
        there = m.don.at[layer, pl.ds(HEADS_MINE * c, HEADS_MINE)]
        keep = near(own_half(layer, c), there)
        give = remote(own_half(layer, 1 - c), there, sibling)
        begin(give)
        return keep, give

    def attn_grad(layer, part, left, right, count):
        @pl.loop(0, 4)
        def _(n):
            cols = pl.ds(pl.multiple_of(n * 256, 256), 256)
            total = None
            for r in range(ROWS_HERE):
                term = product_left(left[r, :, cols], right[r])
                total = term if total is None else total + term
            m.da[3 * layer + part, cols, :] = total.astype(BF)

    def scatter_out(layer):
        return Scatter(lambda d: m.don.at[layer, d], lambda b: m.xo.at[layer, b], lambda b: m.zo.at[layer, b], SHARD)

    def scatter_attn(first, count):
        part = pl.ds(first, count)
        return Scatter(
            lambda d: m.da.at[part, pl.ds(d * SEG, SEG)], lambda b: m.xa.at[part, b], lambda b: m.za.at[part, b], SEG
        )

    swap2 = out_grad(1, m.o, m.dx2)
    for r in range(ROWS_HERE):
        fourth_sum.cross(r)
    for part in range(3):
        attn_grad(1, part, m.n1, m.dqkv.at[part], PATCHES)
    s_attn1, s_out1 = scatter_attn(3, 3), scatter_out(1)
    s_attn1.start()
    swap2[0].wait()
    swap2[1].wait_recv()
    s_out1.start()
    for r in range(ROWS_HERE):
        out_sum.arrive(r)
        for rows in halves:
            m.out[r, rows] = (own_of(m.x2)(r, rows) + out_sum.total(r, rows)).astype(BF)
    for r in range(ROWS_HERE):
        gradient_in(fourth_sum, fourth_share, own_of(m.dx2), own_of(m.x1), 2, into(m.dx1), r)
    for r in range(ROWS_HERE):
        fourth_share.relay(r)
    work(2)
    for r in range(ROWS_HERE):
        mixed_back(fourth_share, m.dx1, 0, r)

    @pl.loop(0, ROWS_HERE)
    def _(r):
        attend_back(r, window(r), m.qc, m.kc, m.vc, m.dmix, m.dqc, m.dkc, m.dvc)

    out_sum.free()
    fourth_sum.free()
    byte_sum = Reduce(m.bp, m.br1, m.bq2, m.br2, TOKENS_B)
    fifth_sum = Reduce(m.p, m.r1, m.q2, m.r2, TOKENS)
    for r in range(ROWS_HERE):
        to_owner(
            byte_sum,
            lambda r, n: product_right(m.dkc[r], m.wa[1, n * 256 : n * 256 + 256, :])
            + product_right(m.dvc[r], m.wa[2, n * 256 : n * 256 + 256, :]),
            None,
            r,
        )
    for r in range(ROWS_HERE):
        to_owner(fifth_sum, lambda r, n: product_right(m.dqc[r], m.wa[0, n * 256 : n * 256 + 256, :]), None, r)
    own_bytes = [near(m.byte.at[4 * r + pipe], m.bown.at[r]) for r in range(ROWS_HERE)]
    swap3 = out_grad(0, m.oc, m.dx1)
    for r in range(ROWS_HERE):
        byte_sum.cross(r)
    attn_grad(0, 1, m.nb, m.dkc, BYTES)
    attn_grad(0, 2, m.nb, m.dvc, BYTES)
    attn_grad(0, 0, m.nq, m.dqc, PATCHES)
    s_attn0, s_out0 = scatter_attn(0, 3), scatter_out(0)
    s_attn0.start()
    swap3[0].wait()
    swap3[1].wait_recv()
    s_out0.start()
    for r in range(ROWS_HERE):
        fifth_sum.cross(r)

    def back_to_pipe(rows_ref, dst):
        copies = [near(rows_ref(pipe), dst)]
        for device in (across, corner, sibling):
            copies.append(begin(remote(rows_ref(device[1]), dst, device)))
        return copies

    def attn_home(layer):
        src = lambda q: m.da.at[pl.ds(3 * layer, 3), pl.ds(dp * SEG + q * SHARD, SHARD)]
        return back_to_pipe(src, m.g_attn.at[pipe, pl.ds(3 * layer, 3)])

    def gate_home():
        src = lambda q: m.dg.at[pl.ds(dp * SEG + q * SHARD, SHARD)]
        return back_to_pipe(src, m.g_gate.at[pipe])

    work(len(tasks))
    tasks += s_gate.steps()
    work(len(tasks))
    home = [gate_home()]
    for r in range(ROWS_HERE):
        gradient_in(
            fifth_sum,
            None,
            own_of(m.dx1),
            own_patch,
            0,
            lambda r, rows, value: m.gpatch.__setitem__((r, rows), value),
            r,
        )
    for copy in own_bytes:
        copy.wait()
    for r in range(ROWS_HERE):
        byte_sum.arrive(r)
        for part in range(5):
            rows = pl.ds(part * 32, 32)
            back = norm_back(m.bown[r, rows], byte_sum.total(r, rows), 1)
            m.gbyte[r, rows] = back.astype(BF)

    gain_steps = []
    for k, device in enumerate((sibling, across, aside, pair, mirror)):

        def gain_step(k=k, device=device):
            m.gs[k] = m.gn[...]
            copy = begin(remote(m.gs.at[k], m.gr.at[k], device))

            def done():
                copy.wait_recv()
                m.gn[...] += m.gr[k]

            return done

        gain_steps.append(gain_step)

    tasks += s_attn1.steps()
    work(len(tasks))
    home.append(attn_home(1))
    tasks += s_out1.steps()
    pending = gain_steps[0]()
    work(3)
    pending()
    pending = gain_steps[1]()
    work(len(tasks))
    pending()
    pending = gain_steps[2]()
    tasks += s_attn0.steps()
    work(3)
    pending()
    pending = gain_steps[3]()
    work(len(tasks))
    home.append(attn_home(0))
    pending()
    pending = gain_steps[4]()
    tasks += s_out0.steps()
    work(len(tasks))
    pending()
    m.g_gain[...] = m.gn[...]
    m.g_down[...] = m.dd[pl.ds(dp * PADDED, PADDED), :]
    for layer in range(2):
        m.g_out[layer] = m.don[layer, dp]
    for copies in home:
        arrived(copies)
    for gather in (g_attn0, g_attn1, g_gate, g_down):
        gather.finish()
    for scatter in (s_down, s_gate, s_attn1, s_out1, s_attn0, s_out0):
        scatter.finish()
    byte_sum.free()
    fifth_sum.free()
    for wait in unfinished:
        wait()


def fused_step(patch_states, byte_states, cotangent, patch_lengths, row_lengths, attn_weights, out_weights, gate_up, down_weight, gains):
    wa = attn_weights.reshape(6, SHARD, 2, HEADS_MINE, 2, HEAD_DIM).transpose(4, 2, 0, 1, 3, 5).reshape(RANKS, 6, SHARD, MINE)
    wg = gate_up.reshape(2, SHARD, GROUPS, RANKS, UNITS)
    wg = jnp.pad(wg, ((0, 0),) * 4 + ((0, PADDED - UNITS),)).transpose(3, 1, 0, 2, 4).reshape(RANKS, SHARD, 2 * HIDDEN)
    wd = jnp.pad(down_weight, ((0, PADDED - UNITS), (0, 0)))
    lens = jnp.concatenate(
        [patch_lengths.astype(F32), jnp.broadcast_to(row_lengths.astype(F32)[:, None], (ROWS_HERE, PATCHES))], axis=0
    )
    lens = jnp.pad(lens, ((0, 4), (0, 0)))
    gains = jnp.pad(gains, ((0, 4), (0, 0)))
    plan = scratch_plan()
    vmem, anywhere = pl.BlockSpec(memory_space=pltpu.VMEM), pl.BlockSpec(memory_space=pl.ANY)
    shape = jax.ShapeDtypeStruct
    results = pl.pallas_call(
        functools.partial(step_kernel, tuple(plan)),
        out_shape=(
            shape((ROWS_HERE, TOKENS, WIDTH), BF),
            shape((ROWS_HERE, TOKENS, WIDTH), BF),
            shape((ROWS_HERE, TOKENS_B, WIDTH), BF),
            shape((RANKS, 6, SHARD, MINE), BF),
            shape((2, SHARD, WIDTH), BF),
            shape((RANKS, SHARD, 2 * HIDDEN), BF),
            shape((PADDED, WIDTH), BF),
            shape((8, WIDTH), F32),
        ),
        in_specs=[vmem, anywhere, vmem, vmem, vmem, anywhere, anywhere, anywhere, anywhere],
        out_specs=[vmem] * 8,
        scratch_shapes=list(plan.values()),
        compiler_params=pltpu.CompilerParams(collective_id=0, has_side_effects=True, vmem_limit_bytes=63 * 2**20),
    )(patch_states, byte_states.reshape(8, TOKENS_B, WIDTH), cotangent, lens, gains, wa, wg, out_weights, wd)
    out, gpatch, gbyte, g_attn, g_out, g_gate, g_down, g_gain = results
    g_attn = g_attn.reshape(2, 2, 6, SHARD, HEADS_MINE, HEAD_DIM).transpose(2, 3, 1, 4, 0, 5)
    g_attn = g_attn.reshape(2, 3, SHARD, WIDTH).astype(F32)
    g_gate = g_gate.reshape(RANKS, SHARD, 2, GROUPS, PADDED)[..., :UNITS].transpose(2, 1, 3, 0, 4)
    g_gate = g_gate.reshape(2, SHARD, GROUPS * RANKS * UNITS).astype(F32)
    first = (lax.axis_index("dp") * RANKS + lax.axis_index("pipe")) * SHARD
    g_gain = lax.dynamic_slice(g_gain, (0, first), (4, SHARD))
    return out, gpatch, gbyte, g_attn, g_out.astype(F32), g_gate, g_down[:UNITS].astype(F32), g_gain


def solution(mesh):
    placed = (
        P("dp", None, None),
        P("dp", None, None),
        P("dp", None, None),
        P("dp", None),
        P("dp"),
        P(None, None, ("dp", "pipe"), None),
        P(None, ("dp", "pipe"), None),
        P(None, ("dp", "pipe"), None),
        P(("dp", "pipe"), None),
        P(),
    )
    return jax.shard_map(
        fused_step if mesh.shape["dp"] == GROUPS else gathered_step,
        mesh=mesh,
        in_specs=placed,
        out_specs=(
            P("dp", "pipe", None),
            P("dp", "pipe", None),
            P("dp", "pipe", None),
            P(None, None, ("dp", "pipe"), None),
            P(None, ("dp", "pipe"), None),
            P(None, ("dp", "pipe"), None),
            P(("dp", "pipe"), None),
            P(None, ("dp", "pipe")),
        ),
        check_vma=False,
    )
```

```python
import functools
from types import SimpleNamespace

import jax
import jax.numpy as jnp
from jax import lax
from jax.experimental import pallas as pl
from jax.experimental.pallas import tpu as pltpu
from jax.sharding import PartitionSpec as P

HEADS = 16
HEAD_DIM = 64
EPSILON = 1e-06
NEGATIVE = -1e30
SCALE = HEAD_DIM ** (-0.5)
BF = jnp.bfloat16
F32 = jnp.float32
MESH = pl.DeviceIdType.MESH


def dot(left, right, contract):
    return lax.dot_general(left, right, (contract, ((), ())), preferred_element_type=F32)


def product(left, right):
    return dot(left, right, ((1,), (0,)))


def product_left(left, right):
    return dot(left, right, ((0,), (0,)))


def product_right(left, right):
    return dot(left, right, ((1,), (1,)))


def norm_rows(values, gain):
    factor = lax.rsqrt(jnp.mean(values * values, axis=-1, keepdims=True) + EPSILON)
    return (values * factor * gain).astype(BF), factor


def norm_back(values, factor, gain, gradient):
    weighted = gradient * gain
    grad_gain = jnp.sum(gradient * values * factor, axis=0)
    grad_values = factor * weighted - values * factor**3 * jnp.mean(weighted * values, axis=-1, keepdims=True)
    return grad_values, grad_gain


def heads_of(values):
    return values.reshape(values.shape[0], HEADS, HEAD_DIM).transpose(1, 0, 2)


def rows_of(values):
    return values.transpose(1, 0, 2).reshape(values.shape[1], -1).astype(BF)


def batched(left, right, left_dim, right_dim):
    return lax.dot_general(left, right, (((left_dim,), (right_dim,)), ((0,), (0,))), preferred_element_type=F32)


def attend(queries, keys, values, allowed):
    scores = batched(queries, keys, 2, 2) * SCALE
    weights = jax.nn.softmax(jnp.where(allowed[None], scores, NEGATIVE), axis=-1)
    low = weights.astype(BF)
    return weights, low, rows_of(batched(low, values, 2, 1))


def attend_back(queries, keys, values, weights, low, grad_mixed):
    grad_weights = batched(grad_mixed, values, 2, 2)
    grad_scores = weights * (grad_weights - jnp.sum(weights * grad_weights, axis=-1, keepdims=True))
    grad_scores = grad_scores.astype(BF)
    return (
        rows_of(batched(grad_scores, keys, 2, 1) * SCALE),
        rows_of(batched(grad_scores, queries, 1, 1) * SCALE),
        rows_of(batched(low, grad_mixed, 1, 1)),
    )


def gathered_step(patch_states, byte_states, cotangent, patch_lengths, row_lengths, attn_weights, out_weights, gate_up, down_weight, gains):
    everyone = ("dp", "pipe")
    micro = patch_states.shape[0]
    stages = lax.axis_size("pipe")
    share = stages // micro
    place = lax.axis_index("pipe")
    row, part = place // share, place % share
    attn = lax.all_gather(attn_weights, everyone, axis=2, tiled=True)
    outw = lax.all_gather(out_weights, everyone, axis=1, tiled=True)
    gate_stack = lax.all_gather(gate_up, everyone, axis=1, tiled=True)
    down = lax.all_gather(down_weight, everyone, axis=0, tiled=True)

    def mine(source):
        return lax.dynamic_index_in_dim(source, row, 0, keepdims=False)

    def half(values):
        count = values.shape[0] // share
        return lax.dynamic_slice_in_dim(values, part * count, count, 0)

    def weight_grad(left, right):
        return product_left(half(left), half(right)).astype(BF)

    patch = mine(patch_states).astype(F32)
    byte = mine(byte_states).astype(F32)
    cot = mine(cotangent)
    sizes = mine(patch_lengths)
    length = mine(row_lengths)
    patches, bytes_ = patch.shape[0], byte.shape[0]

    nq, fq = norm_rows(patch, gains[0])
    nb, fb = norm_rows(byte, gains[1])
    qc = heads_of(product(nq, attn[0, 0]).astype(BF))
    kc = heads_of(product(nb, attn[0, 1]).astype(BF))
    vc = heads_of(product(nb, attn[0, 2]).astype(BF))
    ends = jnp.cumsum(sizes)[:, None]
    position = jnp.arange(bytes_, dtype=jnp.int32)[None, :]
    window = (position >= ends - sizes[:, None]) & (position < ends)
    pc32, pc, oc = attend(qc, kc, vc, window)
    x1 = (patch + product(oc, outw[0])).astype(BF)
    x1f = x1.astype(F32)
    n1, f1 = norm_rows(x1f, gains[2])
    q = heads_of(product(n1, attn[1, 0]).astype(BF))
    k = heads_of(product(n1, attn[1, 1]).astype(BF))
    v = heads_of(product(n1, attn[1, 2]).astype(BF))
    slot = jnp.arange(patches, dtype=jnp.int32)
    allowed = (slot[None, :] <= slot[:, None]) & (slot[None, :] < length)
    a32, a, o = attend(q, k, v, allowed)
    x2 = (x1f + product(o, outw[1])).astype(BF)
    x2f = x2.astype(F32)
    n2, f2 = norm_rows(x2f, gains[3])
    gate = product(n2, gate_stack[0])
    up = product(n2, gate_stack[1])
    sig = jax.nn.sigmoid(gate)
    hidden = (gate * sig * up).astype(BF)
    result = (x2f + product(hidden, down)).astype(BF)

    grad_down = weight_grad(hidden, cot)
    dh = product_right(cot, down).astype(BF).astype(F32)
    dgate = (dh * up * sig * (1.0 + gate * (1.0 - sig))).astype(BF)
    dup = (dh * gate * sig).astype(BF)
    grad_gate_up = jnp.stack([weight_grad(n2, dgate), weight_grad(n2, dup)])
    dn2 = product_right(dgate, gate_stack[0]) + product_right(dup, gate_stack[1])
    back, gain3 = norm_back(x2f, f2, gains[3], dn2)
    dx2 = (cot.astype(F32) + back).astype(BF)
    do = heads_of(product_right(dx2, outw[1]).astype(BF))
    dq, dk, dv = attend_back(q, k, v, a32, a, do)
    dn1 = product_right(dq, attn[1, 0]) + product_right(dk, attn[1, 1]) + product_right(dv, attn[1, 2])
    back, gain2 = norm_back(x1f, f1, gains[2], dn1)
    dx1 = (dx2.astype(F32) + back).astype(BF)
    doc = heads_of(product_right(dx1, outw[0]).astype(BF))
    dqc, dkc, dvc = attend_back(qc, kc, vc, pc32, pc, doc)
    back, gain0 = norm_back(patch, fq, gains[0], product_right(dqc, attn[0, 0]))
    grad_patch = (dx1.astype(F32) + back).astype(BF)
    back, gain1 = norm_back(byte, fb, gains[1], product_right(dkc, attn[0, 1]) + product_right(dvc, attn[0, 2]))
    grad_byte = back.astype(BF)
    grad_attn = jnp.stack(
        [
            jnp.stack([weight_grad(nq, dqc), weight_grad(nb, dkc), weight_grad(nb, dvc)]),
            jnp.stack([weight_grad(n1, dq), weight_grad(n1, dk), weight_grad(n1, dv)]),
        ]
    )
    grad_out = jnp.stack([weight_grad(oc, dx1), weight_grad(o, dx2)])
    grad_gains = jnp.where(part == 0, jnp.stack([gain0, gain1, gain2, gain3]), 0.0)

    def to_owner(values):
        whole = lax.all_gather(half(values), "pipe", axis=0, tiled=True)
        whole = whole.reshape(micro, -1, values.shape[1])
        count = whole.shape[1] // stages
        return lax.dynamic_slice_in_dim(whole, place * count, count, 1)

    def summed(values, axis):
        return lax.psum_scatter(values, everyone, scatter_dimension=axis, tiled=True).astype(F32)

    return (
        to_owner(result),
        to_owner(grad_patch),
        to_owner(grad_byte),
        summed(grad_attn, 2),
        summed(grad_out, 1),
        summed(grad_gate_up, 1),
        summed(grad_down, 0),
        summed(grad_gains, 1),
    )


LINE = 4
SIDE = 2
RANKS = 4
GROUPS = LINE * SIDE
ROWS_HERE = 2
PATCHES = 256
BYTES = 640
WIDTH = 1024
MINE = WIDTH // RANKS
HEADS_MINE = MINE // HEAD_DIM
TOKENS = PATCHES // RANKS
TOKENS_B = BYTES // RANKS
SHARD = WIDTH // (GROUPS * RANKS)
SEG = SHARD * RANKS
UNITS = 88
PADDED = 96
HIDDEN = GROUPS * PADDED
NSEM = 512
BIG = (("attn0", 0), ("attn1", 1))


def scratch_plan():
    b = lambda *shape: pltpu.VMEM(shape, BF)
    plan = dict(
        sem=pltpu.SemaphoreType.DMA((NSEM,)),
        wa=b(6, WIDTH, MINE),
        won=b(2, LINE, SIDE, SHARD, WIDTH),
        woh=b(2, 2, 2, HEAD_DIM, WIDTH),
        wg=b(WIDTH, 2 * HIDDEN),
        wd=b(HIDDEN, WIDTH),
        da=b(6, WIDTH, MINE),
        don=b(2, GROUPS, SHARD, WIDTH),
        dg=b(WIDTH, 2 * HIDDEN),
        dd=b(HIDDEN, WIDTH),
        xa=b(6, LINE, SEG, MINE),
        xo=b(2, LINE, SHARD, WIDTH),
        xg=b(LINE, SEG, 2 * HIDDEN),
        xd=b(PADDED, WIDTH),
        za=b(6, LINE + 1, SEG, MINE),
        zo=b(2, LINE + 1, SHARD, WIDTH),
        zg=b(LINE + 1, SEG, 2 * HIDDEN),
        zd=b(LINE + 1, SIDE * PADDED, WIDTH),
        nq=b(ROWS_HERE, PATCHES, WIDTH),
        nb=b(ROWS_HERE, BYTES, WIDTH),
        qc=b(ROWS_HERE, PATCHES, MINE),
        kc=b(ROWS_HERE, BYTES, MINE),
        vc=b(ROWS_HERE, BYTES, MINE),
        oc=b(ROWS_HERE, PATCHES, MINE),
        x1=b(8, TOKENS, WIDTH),
        n1=b(ROWS_HERE, PATCHES, WIDTH),
        qkv=b(3, ROWS_HERE, PATCHES, MINE),
        o=b(ROWS_HERE, PATCHES, MINE),
        x2=b(8, TOKENS, WIDTH),
        n2=b(ROWS_HERE, PATCHES, WIDTH),
        fac=b(ROWS_HERE, PATCHES, 2 * HIDDEN),
        hid=b(ROWS_HERE, PATCHES, HIDDEN),
        dx2=b(8, TOKENS, WIDTH),
        dx1=b(8, TOKENS, WIDTH),
        dmix=b(ROWS_HERE, PATCHES, MINE),
        dqkv=b(ROWS_HERE, PATCHES, 3 * MINE),
        dqc=b(ROWS_HERE, PATCHES, MINE),
        dkvc=b(ROWS_HERE, BYTES, 2 * MINE),
        p=b(8, TOKENS, WIDTH),
        r1=b(ROWS_HERE, 2, TOKENS, WIDTH),
        q2=b(ROWS_HERE, TOKENS, WIDTH),
        r2=b(ROWS_HERE, TOKENS, WIDTH),
        bp=b(8, TOKENS_B, WIDTH),
        br1=b(ROWS_HERE, 2, TOKENS_B, WIDTH),
        bq2=b(ROWS_HERE, TOKENS_B, WIDTH),
        br2=b(ROWS_HERE, TOKENS_B, WIDTH),
        bown=b(ROWS_HERE, TOKENS_B, WIDTH),
    )
    return plan


INS = ("patch", "byte", "cot", "lens", "gains", "wa_in", "wg_in", "wo_in", "wd_in")
OUTS = ("out", "gpatch", "gbyte", "g_attn", "g_out", "g_gate", "g_down")


def step_kernel(names, *refs):
    m = SimpleNamespace(**dict(zip(INS + OUTS + tuple(names), refs)))
    dp, pipe = lax.axis_index("dp"), lax.axis_index("pipe")
    z, x, y, c = dp // SIDE, dp % SIDE, pipe // 2, pipe % 2
    at = lambda z, x, y, c: (z * SIDE + x, y * 2 + c)
    sibling, across, aside = at(z, x, y, 1 - c), at(z, x, 1 - y, c), at(z, 1 - x, y, c)
    right, left = at((z + 1) % LINE, x, y, c), at((z + LINE - 1) % LINE, x, y, c)
    corner = at(z, x, 1 - y, 1 - c)
    counter = [0]

    def take(count=1):
        first = counter[0]
        counter[0] += count
        assert counter[0] <= NSEM
        return first

    unfinished = []

    def remote(src, dst, device, send=None, recv=None):
        send = take() if send is None else send
        recv = take() if recv is None else recv
        return pltpu.make_async_remote_copy(
            src_ref=src, dst_ref=dst, send_sem=m.sem.at[send], recv_sem=m.sem.at[recv], device_id=device, device_id_type=MESH
        )

    def begin(copy):
        copy.start()
        unfinished.append(copy.wait_send)
        return copy

    def near(src, dst):
        copy = pltpu.make_async_copy(src, dst, m.sem.at[take()])
        copy.start()
        return copy

    barrier = pltpu.get_barrier_semaphore()
    for device in (sibling, across, corner, aside):
        pl.semaphore_signal(barrier, inc=1, device_id=device, device_id_type=MESH)

    @pl.when(z < LINE - 1)
    def _():
        pl.semaphore_signal(barrier, inc=1, device_id=right, device_id_type=MESH)

    @pl.when(z > 0)
    def _():
        pl.semaphore_signal(barrier, inc=1, device_id=left, device_id_type=MESH)

    bytes_in = near(m.byte, m.bp)
    local_out = near(m.wo_in, m.won.at[:, z, x])
    local_down = near(m.wd_in, m.wd.at[pl.ds(dp * PADDED, PADDED)])
    pl.semaphore_wait(barrier, 4 + (z < LINE - 1).astype(jnp.int32) + (z > 0).astype(jnp.int32))

    def attn_part(layer):
        src = lambda q: m.wa_in.at[q, pl.ds(3 * layer, 3)]
        dst = m.wa.at[pl.ds(3 * layer, 3), pl.ds(dp * SEG + pipe * SHARD, SHARD)]
        return src, dst

    def gate_part():
        return (lambda q: m.wg_in.at[q]), m.wg.at[pl.ds(dp * SEG + pipe * SHARD, SHARD)]

    def spread(part):
        src, dst = part
        copies = [near(src(pipe), dst)]
        for device in (across, corner, sibling):
            copies.append(begin(remote(src(device[1]), dst, device)))
        return copies

    def arrived(copies):
        copies[0].wait()
        for copy in copies[1:]:
            copy.wait_recv()

    exchange0, exchange1 = spread(attn_part(0)), spread(attn_part(1))
    exchange2 = spread(gate_part())

    class Gather:
        def __init__(self, view):
            self.view = view
            self.sx, self.rx = take(LINE), take(LINE)
            self.sr, self.rr = take(LINE), take(LINE)
            self.sl, self.rl = take(LINE), take(LINE)

        def copy(self, block, device, send, recv):
            there = self.view(block * SIDE + x)
            return remote(there, there, device, send + block, recv + block)

        def aside(self, block):
            return self.copy(block, aside, self.sx, self.rx)

        def right(self, block):
            return self.copy(block, right, self.sr, self.rr)

        def left(self, block):
            return self.copy(block, left, self.sl, self.rl)

        def start(self):
            self.aside(z).start()

            @pl.when(z < LINE - 1)
            def _():
                self.right(z).start()

            @pl.when(z > 0)
            def _():
                self.left(z).start()

        def hop(self, k):
            @pl.when(z - k >= 0)
            def _():
                self.right(z - k).wait_recv()
                self.aside(z - k).start()

                @pl.when(z < LINE - 1)
                def _():
                    self.right(z - k).start()

            @pl.when(z + k < LINE)
            def _():
                self.left(z + k).wait_recv()
                self.aside(z + k).start()

                @pl.when(z > 0)
                def _():
                    self.left(z + k).start()

        def ready(self):
            for block in range(LINE):
                self.aside(block).wait_recv()

        def finish(self):
            for block in range(LINE):
                self.aside(block).wait_send()

                @pl.when((z < LINE - 1) & (z >= block))
                def _():
                    self.right(block).wait_send()

                @pl.when((z > 0) & (z <= block))
                def _():
                    self.left(block).wait_send()

    class GatherPairs(Gather):
        def copy(self, block, device, send, recv):
            there = self.view(block * SIDE, SIDE)
            return remote(there, there, device, send + block, recv + block)

        def start(self):
            there = self.view(z * SIDE + x, 1)
            self.side = begin(remote(there, there, aside, self.sx, self.rx))

        def line(self):
            self.side.wait_recv()

            @pl.when(z < LINE - 1)
            def _():
                self.right(z).start()

            @pl.when(z > 0)
            def _():
                self.left(z).start()

        def hop(self, k):
            @pl.when(z - k >= 0)
            def _():
                self.right(z - k).wait_recv()

                @pl.when(z < LINE - 1)
                def _():
                    self.right(z - k).start()

            @pl.when(z + k < LINE)
            def _():
                self.left(z + k).wait_recv()

                @pl.when(z > 0)
                def _():
                    self.left(z + k).start()

        def ready(self):
            pass

        def finish(self):
            for block in range(LINE):

                @pl.when((z < LINE - 1) & (z >= block))
                def _():
                    self.right(block).wait_send()

                @pl.when((z > 0) & (z <= block))
                def _():
                    self.left(block).wait_send()

    g_out0 = Gather(lambda d: m.won.at[0, d // SIDE, d % SIDE])
    g_out1 = Gather(lambda d: m.won.at[1, d // SIDE, d % SIDE])
    g_attn0 = Gather(lambda d: m.wa.at[pl.ds(0, 3), pl.ds(d * SEG, SEG)])
    g_attn1 = Gather(lambda d: m.wa.at[pl.ds(3, 3), pl.ds(d * SEG, SEG)])
    g_gate = Gather(lambda d: m.wg.at[pl.ds(d * SEG, SEG)])
    g_down = GatherPairs(lambda d, count: m.wd.at[pl.ds(d * PADDED, count * PADDED)])

    def begin_after(copies, gather):
        arrived(copies)
        gather.start()

    queue = []

    def pump(count):
        for _ in range(min(count, len(queue))):
            queue.pop(0)()

    def swap_out(layer):
        mine, there = m.won.at[layer, pl.ds(2 * c, 2)], m.woh.at[layer, :, :, pl.ds(c * SHARD, SHARD)]
        keep = near(mine, there)
        give = remote(m.won.at[layer, pl.ds(2 * (1 - c), 2)], there, sibling)
        give.start()
        return keep, give

    lane = lax.broadcasted_iota(jnp.int32, (1, MINE), 1) // HEAD_DIM
    head_mask = [(lane == j).astype(F32).astype(BF) for j in range(HEADS_MINE)]

    def gain(index):
        return m.gains[index : index + 1, :]

    def factor_of(values):
        return lax.rsqrt(jnp.mean(values * values, axis=-1, keepdims=True) + EPSILON)

    def normed(values, index):
        values = values.astype(F32)
        return (values * factor_of(values) * gain(index)).astype(BF)

    def norm_back(values, gradient, index):
        values = values.astype(F32)
        factor = factor_of(values)
        weighted = gradient * gain(index)
        return factor * weighted - values * (factor * factor * factor) * jnp.mean(weighted * values, axis=-1, keepdims=True)

    def normed_rows(src, dst, index, r):
        for part in range(RANKS):
            for half in range(2):
                rows = pl.ds(half * (TOKENS // 2), TOKENS // 2)
                dst[r, pl.ds(part * TOKENS + half * (TOKENS // 2), TOKENS // 2)] = normed(src[4 * r + part, rows], index)

    class Reduce:
        def __init__(self, p, r1, q2, r2, tokens):
            self.p, self.r1, self.q2, self.r2, self.tokens = p, r1, q2, r2, tokens
            self.first, self.second = {}, {}

        def give(self, r):
            self.first[r] = [
                remote(self.p.at[4 * r + 2 * side + 1 - c], self.r1.at[r, side], sibling) for side in range(2)
            ]
            for copy in self.first[r]:
                copy.start()

        def cross(self, r):
            for copy in self.first[r]:
                copy.wait_recv()
            other = 4 * r + 2 * (1 - y) + c
            self.q2[r] = (self.p[other].astype(F32) + self.r1[r, 1 - y].astype(F32)).astype(BF)
            self.second[r] = remote(self.q2.at[r], self.r2.at[r], across)
            self.second[r].start()

        def arrive(self, r):
            self.second[r].wait_recv()

        def free(self):
            for r in range(ROWS_HERE):
                for copy in self.first[r]:
                    copy.wait_send()
                self.second[r].wait_send()

        def total(self, r, rows):
            own = 4 * r + pipe
            return (
                self.p[own, rows].astype(F32) + self.r1[r, y, rows].astype(F32) + self.r2[r, rows].astype(F32)
            )

    class Share:
        def __init__(self, values):
            self.values, self.copies, self.last = values, {}, {}

        def give(self, r):
            there = self.values.at[4 * r + pipe]
            self.copies[r] = [begin(remote(there, there, across)), begin(remote(there, there, sibling))]

        def relay(self, r):
            self.copies[r][0].wait_recv()
            there = self.values.at[4 * r + 2 * (1 - y) + c]
            self.last[r] = begin(remote(there, there, sibling))

        def ready(self, r):
            self.copies[r][1].wait_recv()
            self.last[r].wait_recv()

    halves = [pl.ds(h * (TOKENS // 2), TOKENS // 2) for h in range(2)]

    def to_owner(reduce, left_of, r):
        for n in range(4):
            cols = pl.ds(n * 256, 256)
            reduce.p[4 * r : 4 * r + 4, :, cols] = left_of(r, n).astype(BF).reshape(4, reduce.tokens, 256)
        reduce.give(r)

    local_out.wait()
    g_out0.start()
    g_out1.start()
    local_down.wait()
    g_down.start()
    begin_after(exchange0, g_attn0)

    @pl.loop(0, ROWS_HERE * PATCHES // 32)
    def _(i):
        rows = pl.ds((i % 8) * 32, 32)
        m.nq[i // 8, rows] = normed(m.patch[i // 8, rows], 0)

    bytes_in.wait()

    @pl.loop(0, 8)
    def _(i):
        for part in range(5):
            rows = pl.ds(part * 32, 32)
            m.nb[i // 4, pl.ds((i % 4) * TOKENS_B + part * 32, 32)] = normed(m.bp[i, rows], 1)

    def hops(gather):
        return [functools.partial(gather.hop, k) for k in (1, 2, 3)]

    h_out0, h_attn0, h_out1, h_attn1, h_gate, h_down = map(hops, (g_out0, g_attn0, g_out1, g_attn1, g_gate, g_down))
    queue += [h_out0[0], h_out1[0], h_attn0[0], h_out0[1], h_out1[1], h_attn0[1], h_out0[2], h_out1[2]]
    queue += [lambda: begin_after(exchange1, g_attn1), h_attn0[2]]
    pump(len(queue))
    queue += [h_attn1[0], lambda: begin_after(exchange2, g_gate), h_attn1[1], h_attn1[2]]
    queue += h_gate[:2] + [g_down.line, h_gate[2]] + h_down
    g_out0.ready()
    swap0 = swap_out(0)
    g_attn0.ready()

    for r in range(ROWS_HERE):
        m.qc[r] = product(m.nq[r], m.wa[0]).astype(BF)

    @pl.loop(0, 4)
    def _(i):
        rows = pl.ds((i % 2) * (BYTES // 2), BYTES // 2)
        block = m.nb[i // 2, rows]
        m.kc[i // 2, rows] = product(block, m.wa[1]).astype(BF)
        m.vc[i // 2, rows] = product(block, m.wa[2]).astype(BF)

    pump(2)

    def window(r):
        sizes = m.lens[pl.ds(r, 1), :]
        i = lax.broadcasted_iota(jnp.int32, (PATCHES, PATCHES), 0)
        j = lax.broadcasted_iota(jnp.int32, (PATCHES, PATCHES), 1)
        first = jnp.sum(jnp.where(j < i, sizes, 0.0), axis=1, keepdims=True)
        last = jnp.sum(jnp.where(j <= i, sizes, 0.0), axis=1, keepdims=True)
        position = lax.broadcasted_iota(jnp.int32, (PATCHES, BYTES), 1).astype(F32)
        return (position >= first) & (position < last)

    def causal(r):
        length = m.lens[pl.ds(ROWS_HERE + r, 1), :]
        i = lax.broadcasted_iota(jnp.int32, (PATCHES, PATCHES), 0)
        j = lax.broadcasted_iota(jnp.int32, (PATCHES, PATCHES), 1)
        return (j <= i) & (j.astype(F32) < length)

    def weights_of(query, keys, allowed):
        scores = jnp.where(allowed, product_right(query, keys) * SCALE, NEGATIVE)
        raised = jnp.exp(scores - jnp.max(scores, axis=-1, keepdims=True))
        return raised / jnp.sum(raised, axis=-1, keepdims=True)

    def attend(r, allowed, queries, keys, values, mixed):
        total = None
        for j in range(HEADS_MINE):
            low = weights_of(queries[r] * head_mask[j], keys[r], allowed).astype(BF)
            term = product(low, values[r] * head_mask[j])
            total = term if total is None else total + term
        mixed[r] = total.astype(BF)

    def attend_back(r, allowed, queries, keys, values, grad):
        sums = [None, None, None]
        for j in range(HEADS_MINE):
            query, mixed = queries[r] * head_mask[j], grad[r] * head_mask[j]
            weights = weights_of(query, keys[r], allowed)
            grad_weights = product_right(mixed, values[r])
            grad_scores = weights * (grad_weights - jnp.sum(weights * grad_weights, axis=-1, keepdims=True))
            grad_scores = grad_scores.astype(BF)
            terms = (
                product(grad_scores, keys[r] * head_mask[j]),
                product_left(grad_scores, query),
                product_left(weights.astype(BF), mixed),
            )
            sums = [t if s is None else s + t for s, t in zip(sums, terms)]
        return (sums[0] * SCALE).astype(BF), (sums[1] * SCALE).astype(BF), sums[2].astype(BF)

    @pl.loop(0, ROWS_HERE)
    def _(r):
        attend(r, window(r), m.qc, m.kc, m.vc, m.oc)

    pump(2)
    for copy in swap0[:1]:
        copy.wait()
    swap0[1].wait_recv()

    def out_rows(layer):
        return lambda n: m.woh[layer, :, :, :, pl.ds(n * 256, 256)].reshape(MINE, 256)

    def residual(reduce, share, base, result, r):
        reduce.arrive(r)
        for rows in halves:
            result[4 * r + pipe, rows] = (base(r, rows) + reduce.total(r, rows)).astype(BF)
        share.give(r)

    first_sum, first_share = Reduce(m.p, m.r1, m.q2, m.r2, TOKENS), Share(m.x1)
    for r in range(ROWS_HERE):
        to_owner(first_sum, lambda r, n: product(m.oc[r], out_rows(0)(n)), r)
    for r in range(ROWS_HERE):
        first_sum.cross(r)
    own_patch = lambda r, rows: m.patch[r, pl.ds(pipe * TOKENS + rows.start, TOKENS // 2)].astype(F32)
    for r in range(ROWS_HERE):
        residual(first_sum, first_share, own_patch, m.x1, r)
    pump(2)
    for r in range(ROWS_HERE):
        first_share.relay(r)
    for r in range(ROWS_HERE):
        first_share.ready(r)
        normed_rows(m.x1, m.n1, 2, r)

    pump(2)
    g_out1.ready()
    swap1 = swap_out(1)
    g_attn1.ready()
    for r in range(ROWS_HERE):
        for part in range(3):
            m.qkv[part, r] = product(m.n1[r], m.wa[3 + part]).astype(BF)
    queries, keys, values = m.qkv.at[0], m.qkv.at[1], m.qkv.at[2]

    @pl.loop(0, ROWS_HERE)
    def _(r):
        attend(r, causal(r), queries, keys, values, m.o)

    swap1[0].wait()
    swap1[1].wait_recv()
    first_sum.free()
    second_sum, second_share = Reduce(m.p, m.r1, m.q2, m.r2, TOKENS), Share(m.x2)
    for r in range(ROWS_HERE):
        to_owner(second_sum, lambda r, n: product(m.o[r], out_rows(1)(n)), r)
    for r in range(ROWS_HERE):
        second_sum.cross(r)
    own_of = lambda values: lambda r, rows: values[4 * r + pipe, rows].astype(F32)
    for r in range(ROWS_HERE):
        residual(second_sum, second_share, own_of(m.x1), m.x2, r)
    pump(1)
    for r in range(ROWS_HERE):
        second_share.relay(r)
    for r in range(ROWS_HERE):
        second_share.ready(r)
        normed_rows(m.x2, m.n2, 3, r)

    pump(len(queue) - 1)
    g_gate.ready()
    tiles = HIDDEN // 256
    for r in range(ROWS_HERE):

        @pl.loop(0, tiles)
        def _(n, r=r):
            first = pl.ds(pl.multiple_of(n * 256, 256), 256)
            later = pl.ds(pl.multiple_of(HIDDEN + n * 256, 256), 256)
            gate = product(m.n2[r], m.wg[:, first])
            up = product(m.n2[r], m.wg[:, later])
            sig = jax.nn.sigmoid(gate)
            silu = gate * sig
            m.hid[r, :, first] = (silu * up).astype(BF)
            m.fac[r, :, first] = (up * sig * (1.0 + gate * (1.0 - sig))).astype(BF)
            m.fac[r, :, later] = silu.astype(BF)

    class Scatter:
        def __init__(self, mine, xbuf, zbuf):
            self.mine, self.xbuf, self.zbuf = mine, xbuf, zbuf
            self.sx, self.rx = take(LINE), take(LINE)
            self.sr, self.rr = take(LINE), take(LINE)
            self.sl, self.rl = take(LINE), take(LINE)

        def aside(self, block):
            return remote(self.mine(block * SIDE + 1 - x), self.xbuf(block), aside, self.sx + block, self.rx + block)

        def start(self):
            for block in (3, 0, 2, 1):
                self.aside(block).start()

        def add(self, into, values):
            into[...] = (into[...].astype(F32) + values[...].astype(F32)).astype(BF)

        def line(self, block):
            return self.mine(block * SIDE + x)

        def right(self, block):
            return remote(self.line(block), self.zbuf(block), right, self.sr + block, self.rr + block)

        def left(self, block, slot):
            return remote(self.line(block), self.zbuf(slot), left, self.sl + block, self.rl + block)

        def send_left(self, block):
            self.left(block, jnp.where(z - 1 == block, LINE, block)).start()

        def emit(self, rightward, leftward):
            @pl.when(z == 0)
            def _():
                for block in rightward:
                    self.right(block).start()

            @pl.when(z == LINE - 1)
            def _():
                for block in leftward:
                    self.send_left(block)

        def take(self, block):
            self.aside(block).wait_recv()
            self.add(self.line(block), self.xbuf(block))
            self.emit(*{3: ((3,), ()), 0: ((), (0,)), 2: ((2,), ()), 1: ((1,), (1, 2))}[block])

        def tick(self, t):
            @pl.when((z >= 1) & (z <= t))
            def _():
                block = LINE - 1 - t + z
                self.right(block).wait_recv()
                self.add(self.line(block), self.zbuf(block))

                @pl.when(z < block)
                def _():
                    self.right(block).start()

            @pl.when((z < LINE - 1) & (z >= LINE - 1 - t))
            def _():
                block = t - (LINE - 1) + z
                slot = jnp.where(z == block, LINE, block)
                self.left(block, slot).wait_recv()
                self.add(self.line(block), self.zbuf(slot))

                @pl.when(z > block)
                def _():
                    self.send_left(block)

        def finish(self):
            for block in range(LINE):
                self.aside(block).wait_send()
            self.finish_line()

        def finish_line(self):
            for block in range(LINE):

                @pl.when(z < block)
                def _():
                    self.right(block).wait_send()

                @pl.when(z > block)
                def _():
                    self.left(block, 0).wait_send()

    class ScatterPairs(Scatter):
        def line(self, block):
            return self.mine(block * SIDE, SIDE)

        def start(self):
            self.emit((3, 2, 1), (0, 1, 2))

        def cross(self):
            self.side = begin(remote(self.mine(z * SIDE + 1 - x, 1), self.xbuf, aside, self.sx, self.rx))

        def last(self):
            self.side.wait_recv()
            self.add(self.mine(z * SIDE + x, 1), self.xbuf)

    pump(1)

    s_down = ScatterPairs(lambda d, count: m.dd.at[pl.ds(d * PADDED, count * PADDED)], m.xd, lambda b: m.zd.at[b])

    @pl.loop(0, tiles)
    def _(n):
        cols = pl.ds(pl.multiple_of(n * 256, 256), 256)
        for half in range(2):
            wide = pl.ds(half * 512, 512)
            total = product_left(m.hid[0, :, cols], m.cot[0, :, wide]) + product_left(m.hid[1, :, cols], m.cot[1, :, wide])
            m.dd[cols, wide] = total.astype(BF)

    s_down.start()
    for r in range(ROWS_HERE):

        @pl.loop(0, tiles)
        def _(n, r=r):
            first = pl.ds(pl.multiple_of(n * 256, 256), 256)
            later = pl.ds(pl.multiple_of(HIDDEN + n * 256, 256), 256)
            grad = product_right(m.cot[r], m.wd[first, :]).astype(BF).astype(F32)
            m.fac[r, :, first] = (grad * m.fac[r, :, first].astype(F32)).astype(BF)
            m.fac[r, :, later] = (grad * m.fac[r, :, later].astype(F32)).astype(BF)

    second_sum.free()
    third_sum, third_share = Reduce(m.p, m.r1, m.q2, m.r2, TOKENS), Share(m.dx2)
    for r in range(ROWS_HERE):
        to_owner(third_sum, lambda r, n: product_right(m.fac[r], m.wg[n * 256 : n * 256 + 256, :]), r)

    s_gate = Scatter(lambda d: m.dg.at[pl.ds(d * SEG, SEG)], lambda b: m.xg.at[b], lambda b: m.zg.at[b])

    def gate_grad(i):
        rows = pl.ds(pl.multiple_of(i * 256, 256), 256)
        total = product_left(m.n2[0, :, rows], m.fac[0]) + product_left(m.n2[1, :, rows], m.fac[1])
        m.dg[rows, :] = total.astype(BF)

    pl.loop(0, 2)(gate_grad)
    for r in range(ROWS_HERE):
        third_sum.cross(r)
    pl.loop(2, 4)(gate_grad)
    s_gate.start()

    def gradient_in(reduce, share, base, values, index, result, r):
        reduce.arrive(r)
        for rows in halves:
            back = norm_back(values(r, rows), reduce.total(r, rows), index)
            result(r, rows, (base(r, rows) + back).astype(BF))
        if share is not None:
            share.give(r)

    def into(ref):
        def store(r, rows, value):
            ref[4 * r + pipe, rows] = value

        return store

    own_cot = lambda r, rows: m.cot[r, pl.ds(pipe * TOKENS + rows.start, TOKENS // 2)].astype(F32)
    for r in range(ROWS_HERE):
        gradient_in(third_sum, third_share, own_cot, own_of(m.x2), 3, into(m.dx2), r)

    early = pl.ds(0, TOKENS)
    out_sum = Reduce(m.bp.at[:, early], m.br1.at[:, :, early], m.bq2.at[:, early], m.br2.at[:, early], TOKENS)
    for r in range(ROWS_HERE):
        to_owner(out_sum, lambda r, n: product(m.hid[r], m.wd[:, n * 256 : n * 256 + 256]), r)
    s_down.tick(1)
    for r in range(ROWS_HERE):
        third_share.relay(r)
    for r in range(ROWS_HERE):
        out_sum.cross(r)

    def rows_of(ref, r):
        return ref[4 * r : 4 * r + 4].reshape(PATCHES, WIDTH)

    def mixed_back(share, grads, layer, r):
        share.ready(r)
        m.dmix[r] = product_right(rows_of(grads, r), m.woh[layer].reshape(MINE, WIDTH)).astype(BF)

    for r in range(ROWS_HERE):
        mixed_back(third_share, m.dx2, 1, r)

    @pl.loop(0, ROWS_HERE)
    def _(r):
        dq, dk, dv = attend_back(r, causal(r), queries, keys, values, m.dmix)
        m.dqkv[r, :, 0:MINE] = dq
        m.dqkv[r, :, MINE : 2 * MINE] = dk
        m.dqkv[r, :, 2 * MINE : 3 * MINE] = dv

    third_sum.free()
    fourth_sum, fourth_share = Reduce(m.p, m.r1, m.q2, m.r2, TOKENS), Share(m.dx1)

    def attn_back(left, n, first, count):
        total = None
        for part in range(count):
            term = product_right(left[:, part * MINE : part * MINE + MINE], m.wa[first + part, pl.ds(n * 256, 256), :])
            total = term if total is None else total + term
        return total

    for r in range(ROWS_HERE):
        to_owner(fourth_sum, lambda r, n: attn_back(m.dqkv.at[r], n, 3, 3), r)

    def own_half(layer, which):
        return m.won.at[layer, :, which]

    def out_grad(layer, mixed, grads):
        (g_out0, g_out1)[layer].finish()
        (swap0, swap1)[layer][1].wait_send()
        total = None
        for r in range(ROWS_HERE):
            term = product_left(mixed[r], rows_of(grads, r))
            total = term if total is None else total + term
        m.won[layer] = total.astype(BF).reshape(LINE, SIDE, SHARD, WIDTH)
        there = m.don.at[layer, pl.ds(HEADS_MINE * c, HEADS_MINE)]
        keep = near(own_half(layer, c), there)
        give = remote(own_half(layer, 1 - c), there, sibling)
        begin(give)
        return keep, give

    def swapped(swap):
        swap[0].wait()
        swap[1].wait_recv()

    def attn_grad(first, count, left, right):
        @pl.loop(0, 4)
        def _(n):
            cols = pl.ds(pl.multiple_of(n * 256, 256), 256)
            total = product_left(left[0, :, cols], right[0]) + product_left(left[1, :, cols], right[1])
            for part in range(count):
                m.da[first + part, cols, :] = total[:, part * MINE : part * MINE + MINE].astype(BF)

    def scatter_out(layer):
        return Scatter(lambda d: m.don.at[layer, d], lambda b: m.xo.at[layer, b], lambda b: m.zo.at[layer, b])

    def scatter_attn(first, count):
        part = pl.ds(first, count)
        return Scatter(lambda d: m.da.at[part, pl.ds(d * SEG, SEG)], lambda b: m.xa.at[part, b], lambda b: m.za.at[part, b])

    swap2 = out_grad(1, m.o, m.dx2)
    for r in range(ROWS_HERE):
        fourth_sum.cross(r)
    attn_grad(3, 3, m.n1, m.dqkv)
    s_out1, s_attn1 = scatter_out(1), scatter_attn(3, 3)
    swapped(swap2)
    s_out1.start()
    s_attn1.start()
    s_down.tick(2)
    s_gate.take(3)
    for r in range(ROWS_HERE):
        out_sum.arrive(r)
        for rows in halves:
            m.out[r, rows] = (own_of(m.x2)(r, rows) + out_sum.total(r, rows)).astype(BF)
    for r in range(ROWS_HERE):
        gradient_in(fourth_sum, fourth_share, own_of(m.dx2), own_of(m.x1), 2, into(m.dx1), r)
    s_gate.take(0)
    s_down.tick(3)
    s_down.cross()
    for r in range(ROWS_HERE):
        fourth_share.relay(r)
    for r in range(ROWS_HERE):
        mixed_back(fourth_share, m.dx1, 0, r)
    swap3 = out_grad(0, m.oc, m.dx1)
    s_out0 = scatter_out(0)
    s_gate.take(2)
    swapped(swap3)
    s_out0.start()

    @pl.loop(0, ROWS_HERE)
    def _(r):
        dq, dk, dv = attend_back(r, window(r), m.qc, m.kc, m.vc, m.dmix)
        m.dqc[r] = dq
        m.dkvc[r, :, 0:MINE] = dk
        m.dkvc[r, :, MINE : 2 * MINE] = dv

    out_sum.free()
    fourth_sum.free()
    byte_sum = Reduce(m.bp, m.br1, m.bq2, m.br2, TOKENS_B)
    fifth_sum = Reduce(m.p, m.r1, m.q2, m.r2, TOKENS)
    for r in range(ROWS_HERE):
        to_owner(byte_sum, lambda r, n: attn_back(m.dkvc.at[r], n, 1, 2), r)
    for r in range(ROWS_HERE):
        to_owner(fifth_sum, lambda r, n: attn_back(m.dqc.at[r], n, 0, 1), r)
    own_bytes = [near(m.byte.at[4 * r + pipe], m.bown.at[r]) for r in range(ROWS_HERE)]
    for r in range(ROWS_HERE):
        byte_sum.cross(r)
    attn_grad(1, 2, m.nb, m.dkvc)
    s_attn0b = scatter_attn(1, 2)
    s_attn0b.start()
    attn_grad(0, 1, m.nq, m.dqc)
    s_attn0a = scatter_attn(0, 1)
    s_attn0a.start()
    for r in range(ROWS_HERE):
        fifth_sum.cross(r)

    def back_to_pipe(rows_ref, dst):
        copies = [near(rows_ref(pipe), dst)]
        for device in (across, corner, sibling):
            copies.append(begin(remote(rows_ref(device[1]), dst, device)))
        return copies

    def attn_home(first, count):
        src = lambda q: m.da.at[pl.ds(first, count), pl.ds(dp * SEG + q * SHARD, SHARD)]
        return back_to_pipe(src, m.g_attn.at[pipe, pl.ds(first, count)])

    def gate_home():
        src = lambda q: m.dg.at[pl.ds(dp * SEG + q * SHARD, SHARD)]
        return back_to_pipe(src, m.g_gate.at[pipe])

    s_gate.tick(1)
    s_gate.take(1)
    s_down.last()
    s_gate.tick(2)
    for block in (3, 0, 2, 1):
        s_out1.take(block)
    for r in range(ROWS_HERE):
        gradient_in(
            fifth_sum,
            None,
            own_of(m.dx1),
            own_patch,
            0,
            lambda r, rows, value: m.gpatch.__setitem__((r, rows), value),
            r,
        )
    s_gate.tick(3)
    home = [gate_home()]
    for copy in own_bytes:
        copy.wait()
    for r in range(ROWS_HERE):
        byte_sum.arrive(r)
        for part in range(5):
            rows = pl.ds(part * 32, 32)
            back = norm_back(m.bown[r, rows], byte_sum.total(r, rows), 1)
            m.gbyte[r, rows] = back.astype(BF)
    s_attn1.take(3)
    s_attn1.take(0)
    s_out1.tick(1)
    s_attn1.take(2)
    s_out1.tick(2)
    s_attn1.tick(1)
    s_attn1.take(1)
    s_out1.tick(3)
    s_attn1.tick(2)
    for block in (3, 0, 2, 1):
        s_out0.take(block)
    s_attn1.tick(3)
    home.append(attn_home(3, 3))
    s_out0.tick(1)
    s_attn0b.take(3)
    s_attn0b.take(0)
    s_out0.tick(2)
    s_attn0b.take(2)
    s_out0.tick(3)
    s_attn0b.tick(1)
    s_attn0b.take(1)
    s_attn0b.tick(2)
    for block in (3, 0, 2, 1):
        s_attn0a.take(block)
    s_attn0b.tick(3)
    home.append(attn_home(1, 2))
    s_attn0a.tick(1)
    s_attn0a.tick(2)
    s_attn0a.tick(3)
    home.append(attn_home(0, 1))
    m.g_down[...] = m.dd[pl.ds(dp * PADDED, PADDED), :]
    for layer in range(2):
        m.g_out[layer] = m.don[layer, dp]
    for copies in home:
        arrived(copies)
    for gather in (g_attn0, g_attn1, g_gate, g_down):
        gather.finish()
    s_down.finish_line()
    for scatter in (s_gate, s_attn1, s_out1, s_attn0a, s_attn0b, s_out0):
        scatter.finish()
    byte_sum.free()
    fifth_sum.free()
    for wait in unfinished:
        wait()


def fused_step(patch_states, byte_states, cotangent, patch_lengths, row_lengths, attn_weights, out_weights, gate_up, down_weight, gains):
    wa = attn_weights.reshape(6, SHARD, 2, HEADS_MINE, 2, HEAD_DIM).transpose(4, 2, 0, 1, 3, 5).reshape(RANKS, 6, SHARD, MINE)
    wg = gate_up.reshape(2, SHARD, GROUPS, RANKS, UNITS)
    wg = jnp.pad(wg, ((0, 0),) * 4 + ((0, PADDED - UNITS),)).transpose(3, 1, 0, 2, 4).reshape(RANKS, SHARD, 2 * HIDDEN)
    wd = jnp.pad(down_weight, ((0, PADDED - UNITS), (0, 0)))
    lens = jnp.concatenate(
        [patch_lengths.astype(F32), jnp.broadcast_to(row_lengths.astype(F32)[:, None], (ROWS_HERE, PATCHES))], axis=0
    )
    lens = jnp.pad(lens, ((0, 4), (0, 0)))
    gains = jnp.pad(gains, ((0, 4), (0, 0)))
    plan = scratch_plan()
    vmem, anywhere = pl.BlockSpec(memory_space=pltpu.VMEM), pl.BlockSpec(memory_space=pl.ANY)
    shape = jax.ShapeDtypeStruct
    results = pl.pallas_call(
        functools.partial(step_kernel, tuple(plan)),
        out_shape=(
            shape((ROWS_HERE, TOKENS, WIDTH), BF),
            shape((ROWS_HERE, TOKENS, WIDTH), BF),
            shape((ROWS_HERE, TOKENS_B, WIDTH), BF),
            shape((RANKS, 6, SHARD, MINE), BF),
            shape((2, SHARD, WIDTH), BF),
            shape((RANKS, SHARD, 2 * HIDDEN), BF),
            shape((PADDED, WIDTH), BF),
        ),
        in_specs=[vmem, anywhere, vmem, vmem, vmem, anywhere, anywhere, anywhere, anywhere],
        out_specs=[vmem] * 7,
        scratch_shapes=list(plan.values()),
        compiler_params=pltpu.CompilerParams(collective_id=0, has_side_effects=True, vmem_limit_bytes=63 * 2**20),
    )(patch_states, byte_states.reshape(8, TOKENS_B, WIDTH), cotangent, lens, gains, wa, wg, out_weights, wd)
    out, gpatch, gbyte, g_attn, g_out, g_gate, g_down = results
    per_part = jnp.sum(wa.astype(F32) * g_attn.astype(F32), axis=(0, 3))
    per_gate = jnp.sum(wg.astype(F32) * g_gate.astype(F32), axis=(0, 2))
    first = (lax.axis_index("dp") * RANKS + lax.axis_index("pipe")) * SHARD
    own_gains = lax.dynamic_slice(gains, (0, first), (4, SHARD))
    g_gain = jnp.stack([per_part[0], per_part[1] + per_part[2], per_part[3] + per_part[4] + per_part[5], per_gate]) / own_gains
    g_attn = g_attn.reshape(2, 2, 6, SHARD, HEADS_MINE, HEAD_DIM).transpose(2, 3, 1, 4, 0, 5)
    g_attn = g_attn.reshape(2, 3, SHARD, WIDTH).astype(F32)
    g_gate = g_gate.reshape(RANKS, SHARD, 2, GROUPS, PADDED)[..., :UNITS].transpose(2, 1, 3, 0, 4)
    g_gate = g_gate.reshape(2, SHARD, GROUPS * RANKS * UNITS).astype(F32)
    return out, gpatch, gbyte, g_attn, g_out.astype(F32), g_gate, g_down[:UNITS].astype(F32), g_gain


def solution(mesh):
    placed = (
        P("dp", None, None),
        P("dp", None, None),
        P("dp", None, None),
        P("dp", None),
        P("dp"),
        P(None, None, ("dp", "pipe"), None),
        P(None, ("dp", "pipe"), None),
        P(None, ("dp", "pipe"), None),
        P(("dp", "pipe"), None),
        P(),
    )
    return jax.shard_map(
        fused_step if mesh.shape["dp"] == GROUPS else gathered_step,
        mesh=mesh,
        in_specs=placed,
        out_specs=(
            P("dp", "pipe", None),
            P("dp", "pipe", None),
            P("dp", "pipe", None),
            P(None, None, ("dp", "pipe"), None),
            P(None, ("dp", "pipe"), None),
            P(None, ("dp", "pipe"), None),
            P(("dp", "pipe"), None),
            P(None, ("dp", "pipe")),
        ),
        check_vma=False,
    )
```

```python
import functools
from types import SimpleNamespace

import jax
import jax.numpy as jnp
from jax import lax
from jax.experimental import pallas as pl
from jax.experimental.pallas import tpu as pltpu
from jax.sharding import PartitionSpec as P

HEADS = 16
HEAD_DIM = 64
EPSILON = 1e-06
NEGATIVE = -1e30
SCALE = HEAD_DIM ** (-0.5)
BF = jnp.bfloat16
F32 = jnp.float32
MESH = pl.DeviceIdType.MESH


def dot(left, right, contract):
    return lax.dot_general(left, right, (contract, ((), ())), preferred_element_type=F32)


def product(left, right):
    return dot(left, right, ((1,), (0,)))


def product_left(left, right):
    return dot(left, right, ((0,), (0,)))


def product_right(left, right):
    return dot(left, right, ((1,), (1,)))


def norm_rows(values, gain):
    factor = lax.rsqrt(jnp.mean(values * values, axis=-1, keepdims=True) + EPSILON)
    return (values * factor * gain).astype(BF), factor


def norm_back(values, factor, gain, gradient):
    weighted = gradient * gain
    grad_gain = jnp.sum(gradient * values * factor, axis=0)
    grad_values = factor * weighted - values * factor**3 * jnp.mean(weighted * values, axis=-1, keepdims=True)
    return grad_values, grad_gain


def heads_of(values):
    return values.reshape(values.shape[0], HEADS, HEAD_DIM).transpose(1, 0, 2)


def rows_of(values):
    return values.transpose(1, 0, 2).reshape(values.shape[1], -1).astype(BF)


def batched(left, right, left_dim, right_dim):
    return lax.dot_general(left, right, (((left_dim,), (right_dim,)), ((0,), (0,))), preferred_element_type=F32)


def attend(queries, keys, values, allowed):
    scores = batched(queries, keys, 2, 2) * SCALE
    weights = jax.nn.softmax(jnp.where(allowed[None], scores, NEGATIVE), axis=-1)
    low = weights.astype(BF)
    return weights, low, rows_of(batched(low, values, 2, 1))


def attend_back(queries, keys, values, weights, low, grad_mixed):
    grad_weights = batched(grad_mixed, values, 2, 2)
    grad_scores = weights * (grad_weights - jnp.sum(weights * grad_weights, axis=-1, keepdims=True))
    grad_scores = grad_scores.astype(BF)
    return (
        rows_of(batched(grad_scores, keys, 2, 1) * SCALE),
        rows_of(batched(grad_scores, queries, 1, 1) * SCALE),
        rows_of(batched(low, grad_mixed, 1, 1)),
    )


def gathered_step(patch_states, byte_states, cotangent, patch_lengths, row_lengths, attn_weights, out_weights, gate_up, down_weight, gains):
    everyone = ("dp", "pipe")
    micro = patch_states.shape[0]
    stages = lax.axis_size("pipe")
    share = stages // micro
    place = lax.axis_index("pipe")
    row, part = place // share, place % share
    attn = lax.all_gather(attn_weights, everyone, axis=2, tiled=True)
    outw = lax.all_gather(out_weights, everyone, axis=1, tiled=True)
    gate_stack = lax.all_gather(gate_up, everyone, axis=1, tiled=True)
    down = lax.all_gather(down_weight, everyone, axis=0, tiled=True)

    def mine(source):
        return lax.dynamic_index_in_dim(source, row, 0, keepdims=False)

    def half(values):
        count = values.shape[0] // share
        return lax.dynamic_slice_in_dim(values, part * count, count, 0)

    def weight_grad(left, right):
        return product_left(half(left), half(right)).astype(BF)

    patch = mine(patch_states).astype(F32)
    byte = mine(byte_states).astype(F32)
    cot = mine(cotangent)
    sizes = mine(patch_lengths)
    length = mine(row_lengths)
    patches, bytes_ = patch.shape[0], byte.shape[0]

    nq, fq = norm_rows(patch, gains[0])
    nb, fb = norm_rows(byte, gains[1])
    qc = heads_of(product(nq, attn[0, 0]).astype(BF))
    kc = heads_of(product(nb, attn[0, 1]).astype(BF))
    vc = heads_of(product(nb, attn[0, 2]).astype(BF))
    ends = jnp.cumsum(sizes)[:, None]
    position = jnp.arange(bytes_, dtype=jnp.int32)[None, :]
    window = (position >= ends - sizes[:, None]) & (position < ends)
    pc32, pc, oc = attend(qc, kc, vc, window)
    x1 = (patch + product(oc, outw[0])).astype(BF)
    x1f = x1.astype(F32)
    n1, f1 = norm_rows(x1f, gains[2])
    q = heads_of(product(n1, attn[1, 0]).astype(BF))
    k = heads_of(product(n1, attn[1, 1]).astype(BF))
    v = heads_of(product(n1, attn[1, 2]).astype(BF))
    slot = jnp.arange(patches, dtype=jnp.int32)
    allowed = (slot[None, :] <= slot[:, None]) & (slot[None, :] < length)
    a32, a, o = attend(q, k, v, allowed)
    x2 = (x1f + product(o, outw[1])).astype(BF)
    x2f = x2.astype(F32)
    n2, f2 = norm_rows(x2f, gains[3])
    gate = product(n2, gate_stack[0])
    up = product(n2, gate_stack[1])
    sig = jax.nn.sigmoid(gate)
    hidden = (gate * sig * up).astype(BF)
    result = (x2f + product(hidden, down)).astype(BF)

    grad_down = weight_grad(hidden, cot)
    dh = product_right(cot, down).astype(BF).astype(F32)
    dgate = (dh * up * sig * (1.0 + gate * (1.0 - sig))).astype(BF)
    dup = (dh * gate * sig).astype(BF)
    grad_gate_up = jnp.stack([weight_grad(n2, dgate), weight_grad(n2, dup)])
    dn2 = product_right(dgate, gate_stack[0]) + product_right(dup, gate_stack[1])
    back, gain3 = norm_back(x2f, f2, gains[3], dn2)
    dx2 = (cot.astype(F32) + back).astype(BF)
    do = heads_of(product_right(dx2, outw[1]).astype(BF))
    dq, dk, dv = attend_back(q, k, v, a32, a, do)
    dn1 = product_right(dq, attn[1, 0]) + product_right(dk, attn[1, 1]) + product_right(dv, attn[1, 2])
    back, gain2 = norm_back(x1f, f1, gains[2], dn1)
    dx1 = (dx2.astype(F32) + back).astype(BF)
    doc = heads_of(product_right(dx1, outw[0]).astype(BF))
    dqc, dkc, dvc = attend_back(qc, kc, vc, pc32, pc, doc)
    back, gain0 = norm_back(patch, fq, gains[0], product_right(dqc, attn[0, 0]))
    grad_patch = (dx1.astype(F32) + back).astype(BF)
    back, gain1 = norm_back(byte, fb, gains[1], product_right(dkc, attn[0, 1]) + product_right(dvc, attn[0, 2]))
    grad_byte = back.astype(BF)
    grad_attn = jnp.stack(
        [
            jnp.stack([weight_grad(nq, dqc), weight_grad(nb, dkc), weight_grad(nb, dvc)]),
            jnp.stack([weight_grad(n1, dq), weight_grad(n1, dk), weight_grad(n1, dv)]),
        ]
    )
    grad_out = jnp.stack([weight_grad(oc, dx1), weight_grad(o, dx2)])
    grad_gains = jnp.where(part == 0, jnp.stack([gain0, gain1, gain2, gain3]), 0.0)

    def to_owner(values):
        whole = lax.all_gather(half(values), "pipe", axis=0, tiled=True)
        whole = whole.reshape(micro, -1, values.shape[1])
        count = whole.shape[1] // stages
        return lax.dynamic_slice_in_dim(whole, place * count, count, 1)

    def summed(values, axis):
        return lax.psum_scatter(values, everyone, scatter_dimension=axis, tiled=True).astype(F32)

    return (
        to_owner(result),
        to_owner(grad_patch),
        to_owner(grad_byte),
        summed(grad_attn, 2),
        summed(grad_out, 1),
        summed(grad_gate_up, 1),
        summed(grad_down, 0),
        summed(grad_gains, 1),
    )


LINE = 4
SIDE = 2
RANKS = 4
GROUPS = LINE * SIDE
ROWS_HERE = 2
PATCHES = 256
BYTES = 640
WIDTH = 1024
MINE = WIDTH // RANKS
HEADS_MINE = MINE // HEAD_DIM
TOKENS = PATCHES // RANKS
TOKENS_B = BYTES // RANKS
SHARD = WIDTH // (GROUPS * RANKS)
SEG = SHARD * RANKS
UNITS = 88
PADDED = 96
HIDDEN = GROUPS * PADDED
NSEM = 512
BIG = (("attn0", 0), ("attn1", 1))


def scratch_plan():
    b = lambda *shape: pltpu.VMEM(shape, BF)
    plan = dict(
        sem=pltpu.SemaphoreType.DMA((NSEM,)),
        wa=b(6, WIDTH, MINE),
        won=b(2, LINE, SIDE, SHARD, WIDTH),
        woh=b(2, 2, 2, HEAD_DIM, WIDTH),
        wg=b(WIDTH, 2 * HIDDEN),
        wd=b(HIDDEN, WIDTH),
        da=b(6, WIDTH, MINE),
        don=b(2, GROUPS, SHARD, WIDTH),
        dg=b(WIDTH, 2 * HIDDEN),
        dd=b(HIDDEN, WIDTH),
        xa=b(6, LINE, SEG, MINE),
        xo=b(2, LINE, SHARD, WIDTH),
        xg=b(LINE, SEG, 2 * HIDDEN),
        xd=b(PADDED, WIDTH),
        za=b(6, LINE + 1, SEG, MINE),
        zo=b(2, LINE + 1, SHARD, WIDTH),
        zg=b(LINE + 1, SEG, 2 * HIDDEN),
        zd=b(LINE + 1, SIDE * PADDED, WIDTH),
        nq=b(ROWS_HERE, PATCHES, WIDTH),
        nb=b(ROWS_HERE, BYTES, WIDTH),
        qc=b(ROWS_HERE, PATCHES, MINE),
        kc=b(ROWS_HERE, BYTES, MINE),
        vc=b(ROWS_HERE, BYTES, MINE),
        oc=b(ROWS_HERE, PATCHES, MINE),
        x1=b(8, TOKENS, WIDTH),
        n1=b(ROWS_HERE, PATCHES, WIDTH),
        qkv=b(3, ROWS_HERE, PATCHES, MINE),
        o=b(ROWS_HERE, PATCHES, MINE),
        x2=b(8, TOKENS, WIDTH),
        n2=b(ROWS_HERE, PATCHES, WIDTH),
        fac=b(ROWS_HERE, PATCHES, 2 * HIDDEN),
        hid=b(ROWS_HERE, PATCHES, HIDDEN),
        dx2=b(8, TOKENS, WIDTH),
        dx1=b(8, TOKENS, WIDTH),
        dmix=b(ROWS_HERE, PATCHES, MINE),
        dqkv=b(ROWS_HERE, PATCHES, 3 * MINE),
        dqc=b(ROWS_HERE, PATCHES, MINE),
        dkvc=b(ROWS_HERE, BYTES, 2 * MINE),
        p=b(8, TOKENS, WIDTH),
        r1=b(ROWS_HERE, 2, TOKENS, WIDTH),
        q2=b(ROWS_HERE, TOKENS, WIDTH),
        r2=b(ROWS_HERE, TOKENS, WIDTH),
        bp=b(8, TOKENS_B, WIDTH),
        br1=b(ROWS_HERE, 2, TOKENS_B, WIDTH),
        br2=b(ROWS_HERE, TOKENS_B, WIDTH),
    )
    return plan


INS = ("patch", "byte", "cot", "sizes", "lengths", "attn", "wo_in", "gate_up", "down", "gains")
OUTS = ("out", "gpatch", "gbyte", "g_attn", "g_out", "g_gate", "g_down")


def step_kernel(names, *refs):
    m = SimpleNamespace(**dict(zip(INS + OUTS + tuple(names), refs)))
    dp, pipe = lax.axis_index("dp"), lax.axis_index("pipe")
    z, x, y, c = dp // SIDE, dp % SIDE, pipe // 2, pipe % 2
    at = lambda z, x, y, c: (z * SIDE + x, y * 2 + c)
    sibling, across, aside = at(z, x, y, 1 - c), at(z, x, 1 - y, c), at(z, 1 - x, y, c)
    right, left = at((z + 1) % LINE, x, y, c), at((z + LINE - 1) % LINE, x, y, c)
    corner = at(z, x, 1 - y, 1 - c)
    counter = [0]

    def take(count=1):
        first = counter[0]
        counter[0] += count
        assert counter[0] <= NSEM
        return first

    unfinished = []

    def remote(src, dst, device, send=None, recv=None):
        send = take() if send is None else send
        recv = take() if recv is None else recv
        return pltpu.make_async_remote_copy(
            src_ref=src, dst_ref=dst, send_sem=m.sem.at[send], recv_sem=m.sem.at[recv], device_id=device, device_id_type=MESH
        )

    def begin(copy):
        copy.start()
        unfinished.append(copy.wait_send)
        return copy

    def near(src, dst):
        copy = pltpu.make_async_copy(src, dst, m.sem.at[take()])
        copy.start()
        return copy

    barrier = pltpu.get_barrier_semaphore()
    for device in (sibling, across, corner, aside):
        pl.semaphore_signal(barrier, inc=1, device_id=device, device_id_type=MESH)

    @pl.when(z < LINE - 1)
    def _():
        pl.semaphore_signal(barrier, inc=1, device_id=right, device_id_type=MESH)

    @pl.when(z > 0)
    def _():
        pl.semaphore_signal(barrier, inc=1, device_id=left, device_id_type=MESH)

    bytes_in = near(m.byte, m.bp)
    local_out = near(m.wo_in, m.won.at[:, z, x])
    pl.semaphore_wait(barrier, 4 + (z < LINE - 1).astype(jnp.int32) + (z > 0).astype(jnp.int32))

    class Gather:
        def __init__(self, view):
            self.view = view
            self.sx, self.rx = take(LINE), take(LINE)
            self.sr, self.rr = take(LINE), take(LINE)
            self.sl, self.rl = take(LINE), take(LINE)

        def copy(self, block, device, send, recv):
            there = self.view(block * SIDE + x)
            return remote(there, there, device, send + block, recv + block)

        def aside(self, block):
            return self.copy(block, aside, self.sx, self.rx)

        def right(self, block):
            return self.copy(block, right, self.sr, self.rr)

        def left(self, block):
            return self.copy(block, left, self.sl, self.rl)

        def start(self):
            self.aside(z).start()

            @pl.when(z < LINE - 1)
            def _():
                self.right(z).start()

            @pl.when(z > 0)
            def _():
                self.left(z).start()

        def hop(self, k):
            @pl.when(z - k >= 0)
            def _():
                self.right(z - k).wait_recv()
                self.aside(z - k).start()

                @pl.when(z < LINE - 1)
                def _():
                    self.right(z - k).start()

            @pl.when(z + k < LINE)
            def _():
                self.left(z + k).wait_recv()
                self.aside(z + k).start()

                @pl.when(z > 0)
                def _():
                    self.left(z + k).start()

        def ready(self):
            for block in range(LINE):
                self.aside(block).wait_recv()

        def finish(self):
            for block in range(LINE):
                self.aside(block).wait_send()

                @pl.when((z < LINE - 1) & (z >= block))
                def _():
                    self.right(block).wait_send()

                @pl.when((z > 0) & (z <= block))
                def _():
                    self.left(block).wait_send()

    class GatherPairs(Gather):
        def copy(self, block, device, send, recv):
            there = self.view(block * SIDE, SIDE)
            return remote(there, there, device, send + block, recv + block)

        def start(self):
            there = self.view(z * SIDE + x, 1)
            self.side = begin(remote(there, there, aside, self.sx, self.rx))

        def line(self):
            self.side.wait_recv()

            @pl.when(z < LINE - 1)
            def _():
                self.right(z).start()

            @pl.when(z > 0)
            def _():
                self.left(z).start()

        def hop(self, k):
            @pl.when(z - k >= 0)
            def _():
                self.right(z - k).wait_recv()

                @pl.when(z < LINE - 1)
                def _():
                    self.right(z - k).start()

            @pl.when(z + k < LINE)
            def _():
                self.left(z + k).wait_recv()

                @pl.when(z > 0)
                def _():
                    self.left(z + k).start()

        def ready(self):
            pass

        def finish(self):
            for block in range(LINE):

                @pl.when((z < LINE - 1) & (z >= block))
                def _():
                    self.right(block).wait_send()

                @pl.when((z > 0) & (z <= block))
                def _():
                    self.left(block).wait_send()

    g_out0 = Gather(lambda d: m.won.at[0, d // SIDE, d % SIDE])
    g_out1 = Gather(lambda d: m.won.at[1, d // SIDE, d % SIDE])
    g_attn0 = Gather(lambda d: m.wa.at[pl.ds(0, 3), pl.ds(d * SEG, SEG)])
    g_attn1 = Gather(lambda d: m.wa.at[pl.ds(3, 3), pl.ds(d * SEG, SEG)])
    g_gate = Gather(lambda d: m.wg.at[pl.ds(d * SEG, SEG)])
    g_down = GatherPairs(lambda d, count: m.wd.at[pl.ds(d * PADDED, count * PADDED)])

    def pieces(values, starts, width):
        return jnp.concatenate([values[:, first : first + width] for first in starts], axis=1)

    def spread(src, dst):
        copies = [near(src(pipe), dst)]
        for device in (across, corner, sibling):
            copies.append(begin_early(remote(src(device[1]), dst, device)))
        return copies

    early_sends = []

    def begin_early(copy):
        copy.start()
        early_sends.append(copy.wait_send)
        return copy

    def arrived(copies):
        copies[0].wait()
        for copy in copies[1:]:
            copy.wait_recv()

    def spread_attn(layer):
        for part in range(3 * layer, 3 * layer + 3):
            values = m.attn[part].astype(F32)
            for rank in range(RANKS):
                heads = [8 * (rank % 2) + 2 * j + rank // 2 for j in range(HEADS_MINE)]
                m.xa[part, rank, 0:SHARD, :] = pieces(values, [h * HEAD_DIM for h in heads], HEAD_DIM).astype(BF)
        three = pl.ds(3 * layer, 3)
        return spread(lambda q: m.xa.at[three, q, pl.ds(0, SHARD)], m.wa.at[three, pl.ds(dp * SEG + pipe * SHARD, SHARD)])

    def spread_gate():
        for which in range(2):
            values = m.gate_up[which].astype(F32)
            values = jnp.concatenate([values, jnp.zeros((SHARD, 128), F32)], axis=1)
            keep = (lax.broadcasted_iota(jnp.int32, (SHARD, HIDDEN), 1) % PADDED) < UNITS
            for rank in range(RANKS):
                starts = [UNITS * (RANKS * d + rank) for d in range(GROUPS)]
                runs = jnp.where(keep, pieces(values, starts, PADDED), 0.0)
                m.xg[rank, 0:SHARD, which * HIDDEN : (which + 1) * HIDDEN] = runs.astype(BF)
        return spread(lambda q: m.xg.at[q, pl.ds(0, SHARD)], m.wg.at[pl.ds(dp * SEG + pipe * SHARD, SHARD)])

    def begin_after(copies, gather):
        arrived(copies)
        gather.start()

    queue = []

    def pump(count):
        for _ in range(min(count, len(queue))):
            queue.pop(0)()

    def swap_out(layer):
        mine, there = m.won.at[layer, pl.ds(2 * c, 2)], m.woh.at[layer, :, :, pl.ds(c * SHARD, SHARD)]
        keep = near(mine, there)
        give = remote(m.won.at[layer, pl.ds(2 * (1 - c), 2)], there, sibling)
        give.start()
        return keep, give

    lane = lax.broadcasted_iota(jnp.int32, (1, MINE), 1) // HEAD_DIM
    head_mask = [(lane == j).astype(F32).astype(BF) for j in range(HEADS_MINE)]

    def gain(index):
        return m.gains[index : index + 1, :]

    def factor_of(values):
        return lax.rsqrt(jnp.mean(values * values, axis=-1, keepdims=True) + EPSILON)

    def normed(values, index):
        values = values.astype(F32)
        return (values * factor_of(values) * gain(index)).astype(BF)

    def norm_back(values, gradient, index):
        values = values.astype(F32)
        factor = factor_of(values)
        weighted = gradient * gain(index)
        return factor * weighted - values * (factor * factor * factor) * jnp.mean(weighted * values, axis=-1, keepdims=True)

    def normed_rows(src, dst, index, r):
        for part in range(RANKS):
            for half in range(2):
                rows = pl.ds(half * (TOKENS // 2), TOKENS // 2)
                dst[r, pl.ds(part * TOKENS + half * (TOKENS // 2), TOKENS // 2)] = normed(src[4 * r + part, rows], index)

    class Reduce:
        def __init__(self, p, r1, q2, r2, tokens):
            self.p, self.r1, self.q2, self.r2, self.tokens = p, r1, q2, r2, tokens
            self.first, self.second = {}, {}

        def give(self, r):
            self.first[r] = [
                remote(self.p.at[4 * r + 2 * side + 1 - c], self.r1.at[r, side], sibling) for side in range(2)
            ]
            for copy in self.first[r]:
                copy.start()

        def cross(self, r):
            for copy in self.first[r]:
                copy.wait_recv()
            other = 4 * r + 2 * (1 - y) + c
            self.q2[r] = (self.p[other].astype(F32) + self.r1[r, 1 - y].astype(F32)).astype(BF)
            self.second[r] = remote(self.q2.at[r], self.r2.at[r], across)
            self.second[r].start()

        def arrive(self, r):
            self.second[r].wait_recv()

        def free(self):
            for r in range(ROWS_HERE):
                for copy in self.first[r]:
                    copy.wait_send()
                self.second[r].wait_send()

        def total(self, r, rows):
            own = 4 * r + pipe
            return (
                self.p[own, rows].astype(F32) + self.r1[r, y, rows].astype(F32) + self.r2[r, rows].astype(F32)
            )

    class Share:
        def __init__(self, values):
            self.values, self.copies, self.last = values, {}, {}

        def give(self, r):
            there = self.values.at[4 * r + pipe]
            self.copies[r] = [begin(remote(there, there, across)), begin(remote(there, there, sibling))]

        def relay(self, r):
            self.copies[r][0].wait_recv()
            there = self.values.at[4 * r + 2 * (1 - y) + c]
            self.last[r] = begin(remote(there, there, sibling))

        def ready(self, r):
            self.copies[r][1].wait_recv()
            self.last[r].wait_recv()

    halves = [pl.ds(h * (TOKENS // 2), TOKENS // 2) for h in range(2)]

    def to_owner(reduce, left_of, r):
        for n in range(4):
            cols = pl.ds(n * 256, 256)
            reduce.p[4 * r : 4 * r + 4, :, cols] = left_of(r, n).astype(BF).reshape(4, reduce.tokens, 256)
        reduce.give(r)

    local_out.wait()
    g_out0.start()
    g_out1.start()
    m.wd[pl.ds(pl.multiple_of(dp * PADDED, 32), PADDED), :] = jnp.concatenate(
        [m.down[...], jnp.zeros((PADDED - UNITS, WIDTH), BF)], axis=0
    )
    g_down.start()
    exchange0 = spread_attn(0)
    exchange1 = spread_attn(1)
    exchange2 = spread_gate()
    begin_after(exchange0, g_attn0)

    @pl.loop(0, ROWS_HERE * PATCHES // 32)
    def _(i):
        rows = pl.ds((i % 8) * 32, 32)
        m.nq[i // 8, rows] = normed(m.patch[i // 8, rows], 0)

    bytes_in.wait()

    @pl.loop(0, 8)
    def _(i):
        for part in range(5):
            rows = pl.ds(part * 32, 32)
            m.nb[i // 4, pl.ds((i % 4) * TOKENS_B + part * 32, 32)] = normed(m.bp[i, rows], 1)

    def hops(gather):
        return [functools.partial(gather.hop, k) for k in (1, 2, 3)]

    h_out0, h_attn0, h_out1, h_attn1, h_gate, h_down = map(hops, (g_out0, g_attn0, g_out1, g_attn1, g_gate, g_down))
    queue += [h_out0[0], h_out1[0], h_attn0[0], h_out0[1], h_out1[1], h_attn0[1], h_out0[2], h_out1[2]]
    queue += [lambda: begin_after(exchange1, g_attn1), h_attn0[2]]
    queue += [h_attn1[0], lambda: begin_after(exchange2, g_gate), h_attn1[1], h_attn1[2]]
    pump(len(queue))
    queue += [lambda: [wait() for wait in early_sends]] + h_gate[:2] + [g_down.line, h_gate[2]] + h_down
    g_out0.ready()
    swap0 = swap_out(0)
    g_attn0.ready()

    for r in range(ROWS_HERE):
        m.qc[r] = product(m.nq[r], m.wa[0]).astype(BF)

    @pl.loop(0, 4)
    def _(i):
        rows = pl.ds((i % 2) * (BYTES // 2), BYTES // 2)
        block = m.nb[i // 2, rows]
        m.kc[i // 2, rows] = product(block, m.wa[1]).astype(BF)
        m.vc[i // 2, rows] = product(block, m.wa[2]).astype(BF)

    def window(r):
        sizes = m.sizes[pl.ds(r, 1), :].astype(F32)
        i = lax.broadcasted_iota(jnp.int32, (PATCHES, PATCHES), 0)
        j = lax.broadcasted_iota(jnp.int32, (PATCHES, PATCHES), 1)
        first = jnp.sum(jnp.where(j < i, sizes, 0.0), axis=1, keepdims=True)
        last = jnp.sum(jnp.where(j <= i, sizes, 0.0), axis=1, keepdims=True)
        position = lax.broadcasted_iota(jnp.int32, (PATCHES, BYTES), 1).astype(F32)
        return (position >= first) & (position < last)

    def causal(r):
        length = m.lengths[r]
        i = lax.broadcasted_iota(jnp.int32, (PATCHES, PATCHES), 0)
        j = lax.broadcasted_iota(jnp.int32, (PATCHES, PATCHES), 1)
        return (j <= i) & (j < length)

    def weights_of(query, keys, allowed):
        scores = jnp.where(allowed, product_right(query, keys) * SCALE, NEGATIVE)
        raised = jnp.exp(scores - jnp.max(scores, axis=-1, keepdims=True))
        return raised / jnp.sum(raised, axis=-1, keepdims=True)

    def attend(r, allowed, queries, keys, values, mixed):
        total = None
        for j in range(HEADS_MINE):
            low = weights_of(queries[r] * head_mask[j], keys[r], allowed).astype(BF)
            term = product(low, values[r] * head_mask[j])
            total = term if total is None else total + term
        mixed[r] = total.astype(BF)

    def attend_back(r, allowed, queries, keys, values, grad):
        sums = [None, None, None]
        for j in range(HEADS_MINE):
            query, mixed = queries[r] * head_mask[j], grad[r] * head_mask[j]
            weights = weights_of(query, keys[r], allowed)
            grad_weights = product_right(mixed, values[r])
            grad_scores = weights * (grad_weights - jnp.sum(weights * grad_weights, axis=-1, keepdims=True))
            grad_scores = grad_scores.astype(BF)
            terms = (
                product(grad_scores, keys[r] * head_mask[j]),
                product_left(grad_scores, query),
                product_left(weights.astype(BF), mixed),
            )
            sums = [t if s is None else s + t for s, t in zip(sums, terms)]
        return (sums[0] * SCALE).astype(BF), (sums[1] * SCALE).astype(BF), sums[2].astype(BF)

    @pl.loop(0, ROWS_HERE)
    def _(r):
        attend(r, window(r), m.qc, m.kc, m.vc, m.oc)

    swap0[0].wait()
    swap0[1].wait_recv()

    def out_rows(layer):
        return lambda n: m.woh[layer, :, :, :, pl.ds(n * 256, 256)].reshape(MINE, 256)

    def residual(reduce, share, base, result, r):
        reduce.arrive(r)
        for rows in halves:
            result[4 * r + pipe, rows] = (base(r, rows) + reduce.total(r, rows)).astype(BF)
        share.give(r)

    first_sum, first_share = Reduce(m.p, m.r1, m.q2, m.r2, TOKENS), Share(m.x1)
    for r in range(ROWS_HERE):
        to_owner(first_sum, lambda r, n: product(m.oc[r], out_rows(0)(n)), r)
    pump(2)
    for r in range(ROWS_HERE):
        first_sum.cross(r)
    pump(2)
    own_patch = lambda r, rows: m.patch[r, pl.ds(pipe * TOKENS + rows.start, TOKENS // 2)].astype(F32)
    for r in range(ROWS_HERE):
        residual(first_sum, first_share, own_patch, m.x1, r)
    for r in range(ROWS_HERE):
        first_share.relay(r)
    for r in range(ROWS_HERE):
        first_share.ready(r)
        normed_rows(m.x1, m.n1, 2, r)

    g_out1.ready()
    swap1 = swap_out(1)
    g_attn1.ready()
    for r in range(ROWS_HERE):
        for part in range(3):
            m.qkv[part, r] = product(m.n1[r], m.wa[3 + part]).astype(BF)
    queries, keys, values = m.qkv.at[0], m.qkv.at[1], m.qkv.at[2]

    @pl.loop(0, ROWS_HERE)
    def _(r):
        attend(r, causal(r), queries, keys, values, m.o)

    swap1[0].wait()
    swap1[1].wait_recv()
    first_sum.free()
    second_sum, second_share = Reduce(m.p, m.r1, m.q2, m.r2, TOKENS), Share(m.x2)
    for r in range(ROWS_HERE):
        to_owner(second_sum, lambda r, n: product(m.o[r], out_rows(1)(n)), r)
    pump(1)
    for r in range(ROWS_HERE):
        second_sum.cross(r)
    pump(1)
    own_of = lambda values: lambda r, rows: values[4 * r + pipe, rows].astype(F32)
    for r in range(ROWS_HERE):
        residual(second_sum, second_share, own_of(m.x1), m.x2, r)
    for r in range(ROWS_HERE):
        second_share.relay(r)
    for r in range(ROWS_HERE):
        second_share.ready(r)
        normed_rows(m.x2, m.n2, 3, r)

    pump(len(queue) - 1)
    g_gate.ready()
    tiles = HIDDEN // 256
    for r in range(ROWS_HERE):

        @pl.loop(0, tiles)
        def _(n, r=r):
            first = pl.ds(pl.multiple_of(n * 256, 256), 256)
            later = pl.ds(pl.multiple_of(HIDDEN + n * 256, 256), 256)
            gate = product(m.n2[r], m.wg[:, first])
            up = product(m.n2[r], m.wg[:, later])
            sig = jax.nn.sigmoid(gate)
            silu = gate * sig
            m.hid[r, :, first] = (silu * up).astype(BF)
            m.fac[r, :, first] = (up * sig * (1.0 + gate * (1.0 - sig))).astype(BF)
            m.fac[r, :, later] = silu.astype(BF)

    class Scatter:
        def __init__(self, mine, xbuf, zbuf):
            self.mine, self.xbuf, self.zbuf = mine, xbuf, zbuf
            self.sx, self.rx = take(LINE), take(LINE)
            self.sr, self.rr = take(LINE), take(LINE)
            self.sl, self.rl = take(LINE), take(LINE)

        def aside(self, block):
            return remote(self.mine(block * SIDE + 1 - x), self.xbuf(block), aside, self.sx + block, self.rx + block)

        def start(self):
            for block in (3, 0, 2, 1):
                self.aside(block).start()

        def add(self, into, values):
            into[...] = (into[...].astype(F32) + values[...].astype(F32)).astype(BF)

        def line(self, block):
            return self.mine(block * SIDE + x)

        def right(self, block):
            return remote(self.line(block), self.zbuf(block), right, self.sr + block, self.rr + block)

        def left(self, block, slot):
            return remote(self.line(block), self.zbuf(slot), left, self.sl + block, self.rl + block)

        def send_left(self, block):
            self.left(block, jnp.where(z - 1 == block, LINE, block)).start()

        def emit(self, rightward, leftward):
            @pl.when(z == 0)
            def _():
                for block in rightward:
                    self.right(block).start()

            @pl.when(z == LINE - 1)
            def _():
                for block in leftward:
                    self.send_left(block)

        def take(self, block):
            self.aside(block).wait_recv()
            self.add(self.line(block), self.xbuf(block))
            self.emit(*{3: ((3,), ()), 0: ((), (0,)), 2: ((2,), ()), 1: ((1,), (1, 2))}[block])

        def tick(self, t):
            @pl.when((z >= 1) & (z <= t))
            def _():
                block = LINE - 1 - t + z
                self.right(block).wait_recv()
                self.add(self.line(block), self.zbuf(block))

                @pl.when(z < block)
                def _():
                    self.right(block).start()

            @pl.when((z < LINE - 1) & (z >= LINE - 1 - t))
            def _():
                block = t - (LINE - 1) + z
                slot = jnp.where(z == block, LINE, block)
                self.left(block, slot).wait_recv()
                self.add(self.line(block), self.zbuf(slot))

                @pl.when(z > block)
                def _():
                    self.send_left(block)

        def finish(self):
            for block in range(LINE):
                self.aside(block).wait_send()
            self.finish_line()

        def finish_line(self):
            for block in range(LINE):

                @pl.when(z < block)
                def _():
                    self.right(block).wait_send()

                @pl.when(z > block)
                def _():
                    self.left(block, 0).wait_send()

    class ScatterPairs(Scatter):
        def line(self, block):
            return self.mine(block * SIDE, SIDE)

        def start(self):
            self.emit((3, 2, 1), (0, 1, 2))

        def cross(self):
            self.side = begin(remote(self.mine(z * SIDE + 1 - x, 1), self.xbuf, aside, self.sx, self.rx))

        def last(self):
            self.side.wait_recv()
            self.add(self.mine(z * SIDE + x, 1), self.xbuf)

    pump(1)

    s_down = ScatterPairs(lambda d, count: m.dd.at[pl.ds(d * PADDED, count * PADDED)], m.xd, lambda b: m.zd.at[b])

    @pl.loop(0, tiles)
    def _(n):
        cols = pl.ds(pl.multiple_of(n * 256, 256), 256)
        for half in range(2):
            wide = pl.ds(half * 512, 512)
            total = product_left(m.hid[0, :, cols], m.cot[0, :, wide]) + product_left(m.hid[1, :, cols], m.cot[1, :, wide])
            m.dd[cols, wide] = total.astype(BF)

    s_down.start()
    for r in range(ROWS_HERE):

        @pl.loop(0, tiles)
        def _(n, r=r):
            first = pl.ds(pl.multiple_of(n * 256, 256), 256)
            later = pl.ds(pl.multiple_of(HIDDEN + n * 256, 256), 256)
            grad = product_right(m.cot[r], m.wd[first, :]).astype(BF).astype(F32)
            m.fac[r, :, first] = (grad * m.fac[r, :, first].astype(F32)).astype(BF)
            m.fac[r, :, later] = (grad * m.fac[r, :, later].astype(F32)).astype(BF)

    second_sum.free()
    third_sum, third_share = Reduce(m.p, m.r1, m.q2, m.r2, TOKENS), Share(m.dx2)
    for r in range(ROWS_HERE):
        to_owner(third_sum, lambda r, n: product_right(m.fac[r], m.wg[n * 256 : n * 256 + 256, :]), r)

    s_gate = Scatter(lambda d: m.dg.at[pl.ds(d * SEG, SEG)], lambda b: m.xg.at[b], lambda b: m.zg.at[b])

    def gate_grad(i):
        rows = pl.ds(pl.multiple_of(i * 256, 256), 256)
        total = product_left(m.n2[0, :, rows], m.fac[0]) + product_left(m.n2[1, :, rows], m.fac[1])
        m.dg[rows, :] = total.astype(BF)

    pl.loop(0, 2)(gate_grad)
    for r in range(ROWS_HERE):
        third_sum.cross(r)
    pl.loop(2, 4)(gate_grad)
    s_gate.start()
    s_down.tick(1)

    def gradient_in(reduce, share, base, values, index, result, r):
        reduce.arrive(r)
        for rows in halves:
            back = norm_back(values(r, rows), reduce.total(r, rows), index)
            result(r, rows, (base(r, rows) + back).astype(BF))
        if share is not None:
            share.give(r)

    def into(ref):
        def store(r, rows, value):
            ref[4 * r + pipe, rows] = value

        return store

    own_cot = lambda r, rows: m.cot[r, pl.ds(pipe * TOKENS + rows.start, TOKENS // 2)].astype(F32)
    for r in range(ROWS_HERE):
        gradient_in(third_sum, third_share, own_cot, own_of(m.x2), 3, into(m.dx2), r)

    early = pl.ds(0, TOKENS)
    out_sum = Reduce(m.bp.at[:, early], m.br1.at[:, :, early], m.n2.at[:, early], m.br2.at[:, early], TOKENS)
    for r in range(ROWS_HERE):
        to_owner(out_sum, lambda r, n: product(m.hid[r], m.wd[:, n * 256 : n * 256 + 256]), r)
    for r in range(ROWS_HERE):
        third_share.relay(r)
    for r in range(ROWS_HERE):
        out_sum.cross(r)

    def rows_of(ref, r):
        return ref[4 * r : 4 * r + 4].reshape(PATCHES, WIDTH)

    def mixed_back(share, grads, layer, r):
        share.ready(r)
        m.dmix[r] = product_right(rows_of(grads, r), m.woh[layer].reshape(MINE, WIDTH)).astype(BF)

    s_gate.take(3)
    s_down.tick(2)
    for r in range(ROWS_HERE):
        mixed_back(third_share, m.dx2, 1, r)

    @pl.loop(0, ROWS_HERE)
    def _(r):
        dq, dk, dv = attend_back(r, causal(r), queries, keys, values, m.dmix)
        m.dqkv[r, :, 0:MINE] = dq
        m.dqkv[r, :, MINE : 2 * MINE] = dk
        m.dqkv[r, :, 2 * MINE : 3 * MINE] = dv

    third_sum.free()
    fourth_sum, fourth_share = Reduce(m.p, m.r1, m.q2, m.r2, TOKENS), Share(m.dx1)

    def attn_back(left, n, first, count):
        total = None
        for part in range(count):
            term = product_right(left[:, part * MINE : part * MINE + MINE], m.wa[first + part, pl.ds(n * 256, 256), :])
            total = term if total is None else total + term
        return total

    for r in range(ROWS_HERE):
        to_owner(fourth_sum, lambda r, n: attn_back(m.dqkv.at[r], n, 3, 3), r)

    def own_half(layer, which):
        return m.won.at[layer, :, which]

    def out_grad(layer, mixed, grads):
        (g_out0, g_out1)[layer].finish()
        (swap0, swap1)[layer][1].wait_send()
        total = None
        for r in range(ROWS_HERE):
            term = product_left(mixed[r], rows_of(grads, r))
            total = term if total is None else total + term
        m.won[layer] = total.astype(BF).reshape(LINE, SIDE, SHARD, WIDTH)
        there = m.don.at[layer, pl.ds(HEADS_MINE * c, HEADS_MINE)]
        keep = near(own_half(layer, c), there)
        give = remote(own_half(layer, 1 - c), there, sibling)
        begin(give)
        return keep, give

    def swapped(swap):
        swap[0].wait()
        swap[1].wait_recv()

    def attn_grad(first, count, left, right):
        @pl.loop(0, 4)
        def _(n):
            cols = pl.ds(pl.multiple_of(n * 256, 256), 256)
            total = product_left(left[0, :, cols], right[0]) + product_left(left[1, :, cols], right[1])
            for part in range(count):
                m.da[first + part, cols, :] = total[:, part * MINE : part * MINE + MINE].astype(BF)

    def scatter_out(layer):
        return Scatter(lambda d: m.don.at[layer, d], lambda b: m.xo.at[layer, b], lambda b: m.zo.at[layer, b])

    def scatter_attn(first, count):
        part = pl.ds(first, count)
        return Scatter(lambda d: m.da.at[part, pl.ds(d * SEG, SEG)], lambda b: m.xa.at[part, b], lambda b: m.za.at[part, b])

    swap2 = out_grad(1, m.o, m.dx2)
    for r in range(ROWS_HERE):
        fourth_sum.cross(r)
    attn_grad(3, 3, m.n1, m.dqkv)
    s_out1, s_attn1 = scatter_out(1), scatter_attn(3, 3)
    swapped(swap2)
    s_out1.start()
    s_attn1.start()
    s_gate.take(0)
    for r in range(ROWS_HERE):
        out_sum.arrive(r)
        for rows in halves:
            m.out[r, rows] = (own_of(m.x2)(r, rows) + out_sum.total(r, rows)).astype(BF)
    for r in range(ROWS_HERE):
        gradient_in(fourth_sum, fourth_share, own_of(m.dx2), own_of(m.x1), 2, into(m.dx1), r)
    s_down.tick(3)
    s_down.cross()
    s_gate.take(2)
    for r in range(ROWS_HERE):
        fourth_share.relay(r)
    for r in range(ROWS_HERE):
        mixed_back(fourth_share, m.dx1, 0, r)
    swap3 = out_grad(0, m.oc, m.dx1)
    s_out0 = scatter_out(0)
    s_gate.tick(1)
    s_gate.take(1)
    swapped(swap3)
    s_out0.start()

    @pl.loop(0, ROWS_HERE)
    def _(r):
        dq, dk, dv = attend_back(r, window(r), m.qc, m.kc, m.vc, m.dmix)
        m.dqc[r] = dq
        m.dkvc[r, :, 0:MINE] = dk
        m.dkvc[r, :, MINE : 2 * MINE] = dv

    out_sum.free()
    fourth_sum.free()
    byte_sum = Reduce(m.bp, m.br1, m.n2.at[:, pl.ds(0, TOKENS_B)], m.br2, TOKENS_B)
    fifth_sum = Reduce(m.p, m.r1, m.q2, m.r2, TOKENS)
    for r in range(ROWS_HERE):
        to_owner(byte_sum, lambda r, n: attn_back(m.dkvc.at[r], n, 1, 2), r)
    for r in range(ROWS_HERE):
        to_owner(fifth_sum, lambda r, n: attn_back(m.dqc.at[r], n, 0, 1), r)
    own_bytes = [near(m.byte.at[4 * r + pipe], m.gbyte.at[r]) for r in range(ROWS_HERE)]
    for r in range(ROWS_HERE):
        byte_sum.cross(r)
    attn_grad(1, 2, m.nb, m.dkvc)
    s_attn0b = scatter_attn(1, 2)
    s_attn0b.start()
    attn_grad(0, 1, m.nq, m.dqc)
    s_attn0a = scatter_attn(0, 1)
    s_attn0a.start()
    for r in range(ROWS_HERE):
        fifth_sum.cross(r)

    def back_to_pipe(rows_ref, dst):
        copies = [near(rows_ref(pipe), dst)]
        for device in (across, corner, sibling):
            copies.append(begin(remote(rows_ref(device[1]), dst, device)))
        return copies

    def attn_home(first, count):
        src = lambda q: m.da.at[pl.ds(first, count), pl.ds(dp * SEG + q * SHARD, SHARD)]
        return back_to_pipe(src, m.g_attn.at[pipe, pl.ds(first, count)])

    def gate_home():
        src = lambda q: m.dg.at[pl.ds(dp * SEG + q * SHARD, SHARD)]
        return back_to_pipe(src, m.g_gate.at[pipe])

    s_gate.tick(2)
    for block in (3, 0, 2, 1):
        s_out1.take(block)
    for r in range(ROWS_HERE):
        gradient_in(
            fifth_sum,
            None,
            own_of(m.dx1),
            own_patch,
            0,
            lambda r, rows, value: m.gpatch.__setitem__((r, rows), value),
            r,
        )
    s_gate.tick(3)
    home = [gate_home()]
    for copy in own_bytes:
        copy.wait()
    for r in range(ROWS_HERE):
        byte_sum.arrive(r)
        for part in range(5):
            rows = pl.ds(part * 32, 32)
            back = norm_back(m.gbyte[r, rows], byte_sum.total(r, rows), 1)
            m.gbyte[r, rows] = back.astype(BF)
    s_attn1.take(3)
    s_attn1.take(0)
    s_out1.tick(1)
    s_attn1.take(2)
    s_out1.tick(2)
    s_attn1.tick(1)
    s_attn1.take(1)
    s_out1.tick(3)
    s_attn1.tick(2)
    for block in (3, 0, 2, 1):
        s_out0.take(block)
    s_attn1.tick(3)
    home.append(attn_home(3, 3))
    s_down.last()
    s_out0.tick(1)
    s_attn0b.take(3)
    s_attn0b.take(0)
    s_out0.tick(2)
    s_attn0b.take(2)
    s_out0.tick(3)
    s_attn0b.tick(1)
    s_attn0b.take(1)
    s_attn0b.tick(2)
    for block in (3, 0, 2, 1):
        s_attn0a.take(block)
    s_attn0b.tick(3)
    home.append(attn_home(1, 2))
    s_attn0a.tick(1)
    s_attn0a.tick(2)
    s_attn0a.tick(3)
    home.append(attn_home(0, 1))
    m.g_down[...] = m.dd[pl.ds(pl.multiple_of(dp * PADDED, 32), PADDED), :]
    for layer in range(2):
        m.g_out[layer] = m.don[layer, dp]
    for copies in home:
        arrived(copies)
    for gather in (g_attn0, g_attn1, g_gate, g_down):
        gather.finish()
    s_down.finish_line()
    for scatter in (s_gate, s_attn1, s_out1, s_attn0a, s_attn0b, s_out0):
        scatter.finish()
    byte_sum.free()
    fifth_sum.free()
    for wait in unfinished:
        wait()


def finish_kernel(out, gpatch, gbyte, attn, gate_up, gains, da, do, dg, dd, out_, gpatch_, gbyte_, g_attn, g_out, g_gate, g_down, g_gain):
    for src, dst in ((out, out_), (gpatch, gpatch_), (gbyte, gbyte_)):
        dst[...] = src[...]
    place = lax.axis_index("dp") * RANKS + lax.axis_index("pipe")
    for part in range(6):
        got = [da[rank, part].astype(F32) for rank in range(RANKS)]
        heads = []
        for head in range(HEADS):
            rank, j = 2 * (head % 2) + head // 8, (head % 8) // 2
            heads.append(got[rank][:, j * HEAD_DIM : (j + 1) * HEAD_DIM])
        g_attn[part] = jnp.concatenate(heads, axis=1)
    for which in range(2):
        got = [dg[rank, :, which * HIDDEN : (which + 1) * HIDDEN].astype(F32) for rank in range(RANKS)]
        runs = [got[rank][:, PADDED * d : PADDED * d + UNITS] for d in range(GROUPS) for rank in range(RANKS)]
        g_gate[which] = jnp.concatenate(runs, axis=1)
    g_out[...] = do[...].astype(F32)
    g_down[...] = dd[0:UNITS].astype(F32)

    column = lax.broadcasted_iota(jnp.int32, (SHARD, WIDTH), 1)
    own = column == lax.broadcasted_iota(jnp.int32, (SHARD, WIDTH), 0) + place * SHARD

    def gain_gradient(row, parts):
        total = None
        for weight, grad in parts:
            term = jnp.sum(weight.astype(F32) * grad, axis=1, keepdims=True)
            total = term if total is None else total + term
        total = total / jnp.sum(jnp.where(own, gains[row : row + 1, :], 0.0), axis=1, keepdims=True)
        g_gain[row : row + 1, :] = jnp.transpose(jnp.broadcast_to(total, (SHARD, 128)))[0:1, :]

    gain_gradient(0, [(attn[0], g_attn[0])])
    gain_gradient(1, [(attn[i], g_attn[i]) for i in (1, 2)])
    gain_gradient(2, [(attn[i], g_attn[i]) for i in (3, 4, 5)])
    gain_gradient(3, [(gate_up[i], g_gate[i]) for i in range(2)])

def fused_step(patch_states, byte_states, cotangent, patch_lengths, row_lengths, attn_weights, out_weights, gate_up, down_weight, gains):
    plan = scratch_plan()
    vmem, anywhere = pl.BlockSpec(memory_space=pltpu.VMEM), pl.BlockSpec(memory_space=pl.ANY)
    shape = jax.ShapeDtypeStruct
    results = pl.pallas_call(
        functools.partial(step_kernel, tuple(plan)),
        out_shape=(
            shape((ROWS_HERE, TOKENS, WIDTH), BF),
            shape((ROWS_HERE, TOKENS, WIDTH), BF),
            shape((ROWS_HERE, TOKENS_B, WIDTH), BF),
            shape((RANKS, 6, SHARD, MINE), BF),
            shape((2, SHARD, WIDTH), BF),
            shape((RANKS, SHARD, 2 * HIDDEN), BF),
            shape((PADDED, WIDTH), BF),
        ),
        in_specs=[vmem, anywhere, vmem, vmem, pl.BlockSpec(memory_space=pltpu.SMEM), vmem, anywhere, vmem, vmem, vmem],
        out_specs=[vmem] * 7,
        scratch_shapes=list(plan.values()),
        compiler_params=pltpu.CompilerParams(collective_id=0, has_side_effects=True, vmem_limit_bytes=63 * 2**20),
    )(
        patch_states,
        byte_states.reshape(8, TOKENS_B, WIDTH),
        cotangent,
        patch_lengths,
        row_lengths,
        attn_weights.reshape(6, SHARD, WIDTH),
        out_weights,
        gate_up,
        down_weight,
        gains,
    )
    finished = pl.pallas_call(
        finish_kernel,
        out_shape=(
            *(shape(array.shape, array.dtype) for array in results[:3]),
            shape((6, SHARD, WIDTH), F32),
            shape(out_weights.shape, F32),
            shape(gate_up.shape, F32),
            shape(down_weight.shape, F32),
            shape((4, SHARD), F32),
        ),
        in_specs=[vmem] * 10,
        out_specs=[vmem] * 8,
        compiler_params=pltpu.CompilerParams(vmem_limit_bytes=63 * 2**20),
    )(*results[:3], attn_weights.reshape(6, SHARD, WIDTH), gate_up, gains, *results[3:])
    return (*finished[:3], finished[3].reshape(attn_weights.shape), *finished[4:])


def solution(mesh):
    placed = (
        P("dp", None, None),
        P("dp", None, None),
        P("dp", None, None),
        P("dp", None),
        P("dp"),
        P(None, None, ("dp", "pipe"), None),
        P(None, ("dp", "pipe"), None),
        P(None, ("dp", "pipe"), None),
        P(("dp", "pipe"), None),
        P(),
    )
    return jax.shard_map(
        fused_step if mesh.shape["dp"] == GROUPS else gathered_step,
        mesh=mesh,
        in_specs=placed,
        out_specs=(
            P("dp", "pipe", None),
            P("dp", "pipe", None),
            P("dp", "pipe", None),
            P(None, None, ("dp", "pipe"), None),
            P(None, ("dp", "pipe"), None),
            P(None, ("dp", "pipe"), None),
            P(("dp", "pipe"), None),
            P(None, ("dp", "pipe")),
        ),
        check_vma=False,
    )
```

```python
import functools
from types import SimpleNamespace

import jax
import jax.numpy as jnp
from jax import lax
from jax.experimental import pallas as pl
from jax.experimental.pallas import tpu as pltpu
from jax.sharding import PartitionSpec as P

HEADS = 16
HEAD_DIM = 64
EPSILON = 1e-06
NEGATIVE = -1e30
SCALE = HEAD_DIM ** (-0.5)
BF = jnp.bfloat16
F32 = jnp.float32
MESH = pl.DeviceIdType.MESH


def dot(left, right, contract):
    return lax.dot_general(left, right, (contract, ((), ())), preferred_element_type=F32)


def product(left, right):
    return dot(left, right, ((1,), (0,)))


def product_left(left, right):
    return dot(left, right, ((0,), (0,)))


def product_right(left, right):
    return dot(left, right, ((1,), (1,)))


def norm_rows(values, gain):
    factor = lax.rsqrt(jnp.mean(values * values, axis=-1, keepdims=True) + EPSILON)
    return (values * factor * gain).astype(BF), factor


def norm_back(values, factor, gain, gradient):
    weighted = gradient * gain
    grad_gain = jnp.sum(gradient * values * factor, axis=0)
    grad_values = factor * weighted - values * factor**3 * jnp.mean(weighted * values, axis=-1, keepdims=True)
    return grad_values, grad_gain


def heads_of(values):
    return values.reshape(values.shape[0], HEADS, HEAD_DIM).transpose(1, 0, 2)


def rows_of(values):
    return values.transpose(1, 0, 2).reshape(values.shape[1], -1).astype(BF)


def batched(left, right, left_dim, right_dim):
    return lax.dot_general(left, right, (((left_dim,), (right_dim,)), ((0,), (0,))), preferred_element_type=F32)


def attend(queries, keys, values, allowed):
    scores = batched(queries, keys, 2, 2) * SCALE
    weights = jax.nn.softmax(jnp.where(allowed[None], scores, NEGATIVE), axis=-1)
    low = weights.astype(BF)
    return weights, low, rows_of(batched(low, values, 2, 1))


def attend_back(queries, keys, values, weights, low, grad_mixed):
    grad_weights = batched(grad_mixed, values, 2, 2)
    grad_scores = weights * (grad_weights - jnp.sum(weights * grad_weights, axis=-1, keepdims=True))
    grad_scores = grad_scores.astype(BF)
    return (
        rows_of(batched(grad_scores, keys, 2, 1) * SCALE),
        rows_of(batched(grad_scores, queries, 1, 1) * SCALE),
        rows_of(batched(low, grad_mixed, 1, 1)),
    )


def gathered_step(patch_states, byte_states, cotangent, patch_lengths, row_lengths, attn_weights, out_weights, gate_up, down_weight, gains):
    everyone = ("dp", "pipe")
    micro = patch_states.shape[0]
    stages = lax.axis_size("pipe")
    share = stages // micro
    place = lax.axis_index("pipe")
    row, part = place // share, place % share
    attn = lax.all_gather(attn_weights, everyone, axis=2, tiled=True)
    outw = lax.all_gather(out_weights, everyone, axis=1, tiled=True)
    gate_stack = lax.all_gather(gate_up, everyone, axis=1, tiled=True)
    down = lax.all_gather(down_weight, everyone, axis=0, tiled=True)

    def mine(source):
        return lax.dynamic_index_in_dim(source, row, 0, keepdims=False)

    def half(values):
        count = values.shape[0] // share
        return lax.dynamic_slice_in_dim(values, part * count, count, 0)

    def weight_grad(left, right):
        return product_left(half(left), half(right)).astype(BF)

    patch = mine(patch_states).astype(F32)
    byte = mine(byte_states).astype(F32)
    cot = mine(cotangent)
    sizes = mine(patch_lengths)
    length = mine(row_lengths)
    patches, bytes_ = patch.shape[0], byte.shape[0]

    nq, fq = norm_rows(patch, gains[0])
    nb, fb = norm_rows(byte, gains[1])
    qc = heads_of(product(nq, attn[0, 0]).astype(BF))
    kc = heads_of(product(nb, attn[0, 1]).astype(BF))
    vc = heads_of(product(nb, attn[0, 2]).astype(BF))
    ends = jnp.cumsum(sizes)[:, None]
    position = jnp.arange(bytes_, dtype=jnp.int32)[None, :]
    window = (position >= ends - sizes[:, None]) & (position < ends)
    pc32, pc, oc = attend(qc, kc, vc, window)
    x1 = (patch + product(oc, outw[0])).astype(BF)
    x1f = x1.astype(F32)
    n1, f1 = norm_rows(x1f, gains[2])
    q = heads_of(product(n1, attn[1, 0]).astype(BF))
    k = heads_of(product(n1, attn[1, 1]).astype(BF))
    v = heads_of(product(n1, attn[1, 2]).astype(BF))
    slot = jnp.arange(patches, dtype=jnp.int32)
    allowed = (slot[None, :] <= slot[:, None]) & (slot[None, :] < length)
    a32, a, o = attend(q, k, v, allowed)
    x2 = (x1f + product(o, outw[1])).astype(BF)
    x2f = x2.astype(F32)
    n2, f2 = norm_rows(x2f, gains[3])
    gate = product(n2, gate_stack[0])
    up = product(n2, gate_stack[1])
    sig = jax.nn.sigmoid(gate)
    hidden = (gate * sig * up).astype(BF)
    result = (x2f + product(hidden, down)).astype(BF)

    grad_down = weight_grad(hidden, cot)
    dh = product_right(cot, down).astype(BF).astype(F32)
    dgate = (dh * up * sig * (1.0 + gate * (1.0 - sig))).astype(BF)
    dup = (dh * gate * sig).astype(BF)
    grad_gate_up = jnp.stack([weight_grad(n2, dgate), weight_grad(n2, dup)])
    dn2 = product_right(dgate, gate_stack[0]) + product_right(dup, gate_stack[1])
    back, gain3 = norm_back(x2f, f2, gains[3], dn2)
    dx2 = (cot.astype(F32) + back).astype(BF)
    do = heads_of(product_right(dx2, outw[1]).astype(BF))
    dq, dk, dv = attend_back(q, k, v, a32, a, do)
    dn1 = product_right(dq, attn[1, 0]) + product_right(dk, attn[1, 1]) + product_right(dv, attn[1, 2])
    back, gain2 = norm_back(x1f, f1, gains[2], dn1)
    dx1 = (dx2.astype(F32) + back).astype(BF)
    doc = heads_of(product_right(dx1, outw[0]).astype(BF))
    dqc, dkc, dvc = attend_back(qc, kc, vc, pc32, pc, doc)
    back, gain0 = norm_back(patch, fq, gains[0], product_right(dqc, attn[0, 0]))
    grad_patch = (dx1.astype(F32) + back).astype(BF)
    back, gain1 = norm_back(byte, fb, gains[1], product_right(dkc, attn[0, 1]) + product_right(dvc, attn[0, 2]))
    grad_byte = back.astype(BF)
    grad_attn = jnp.stack(
        [
            jnp.stack([weight_grad(nq, dqc), weight_grad(nb, dkc), weight_grad(nb, dvc)]),
            jnp.stack([weight_grad(n1, dq), weight_grad(n1, dk), weight_grad(n1, dv)]),
        ]
    )
    grad_out = jnp.stack([weight_grad(oc, dx1), weight_grad(o, dx2)])
    grad_gains = jnp.where(part == 0, jnp.stack([gain0, gain1, gain2, gain3]), 0.0)

    def to_owner(values):
        whole = lax.all_gather(half(values), "pipe", axis=0, tiled=True)
        whole = whole.reshape(micro, -1, values.shape[1])
        count = whole.shape[1] // stages
        return lax.dynamic_slice_in_dim(whole, place * count, count, 1)

    def summed(values, axis):
        return lax.psum_scatter(values, everyone, scatter_dimension=axis, tiled=True).astype(F32)

    return (
        to_owner(result),
        to_owner(grad_patch),
        to_owner(grad_byte),
        summed(grad_attn, 2),
        summed(grad_out, 1),
        summed(grad_gate_up, 1),
        summed(grad_down, 0),
        summed(grad_gains, 1),
    )


LINE = 4
SIDE = 2
RANKS = 4
GROUPS = LINE * SIDE
ROWS_HERE = 2
PATCHES = 256
BYTES = 640
WIDTH = 1024
MINE = WIDTH // RANKS
HEADS_MINE = MINE // HEAD_DIM
TOKENS = PATCHES // RANKS
TOKENS_B = BYTES // RANKS
SHARD = WIDTH // (GROUPS * RANKS)
SEG = SHARD * RANKS
UNITS = 88
PADDED = 96
HIDDEN = GROUPS * PADDED
NSEM = 400
BIG = (("attn0", 0), ("attn1", 1))


def scratch_plan():
    b = lambda *shape: pltpu.VMEM(shape, BF)
    plan = dict(
        sem=pltpu.SemaphoreType.DMA((NSEM,)),
        patch=b(ROWS_HERE, PATCHES, WIDTH),
        cot=b(ROWS_HERE, PATCHES, WIDTH),
        attn=b(6, SHARD, WIDTH),
        gate_up=b(2, SHARD, GROUPS * RANKS * UNITS),
        wa=b(6, WIDTH, MINE),
        won=b(2, LINE, SIDE, SHARD, WIDTH),
        woh=b(2, 2, 2, HEAD_DIM, WIDTH),
        wg=b(WIDTH, 2 * HIDDEN),
        wd=b(HIDDEN, WIDTH),
        da=b(6, WIDTH, MINE),
        don=b(2, GROUPS, SHARD, WIDTH),
        dg=b(WIDTH, 2 * HIDDEN),
        dd=b(HIDDEN, WIDTH),
        xa=b(6, LINE, SEG, MINE),
        xo=b(2, LINE, SHARD, WIDTH),
        xg=b(LINE, SEG, 2 * HIDDEN),
        xd=b(PADDED, WIDTH),
        za=b(6, LINE + 1, SEG, MINE),
        zo=b(2, LINE + 1, SHARD, WIDTH),
        zg=b(LINE + 1, SEG, 2 * HIDDEN),
        zd=b(LINE + 1, SIDE * PADDED, WIDTH),
        nq=b(ROWS_HERE, PATCHES, WIDTH),
        nb=b(ROWS_HERE, BYTES, WIDTH),
        qc=b(ROWS_HERE, PATCHES, MINE),
        kc=b(ROWS_HERE, BYTES, MINE),
        vc=b(ROWS_HERE, BYTES, MINE),
        oc=b(ROWS_HERE, PATCHES, MINE),
        x1=b(8, TOKENS, WIDTH),
        n1=b(ROWS_HERE, PATCHES, WIDTH),
        qkv=b(3, ROWS_HERE, PATCHES, MINE),
        o=b(ROWS_HERE, PATCHES, MINE),
        x2=b(8, TOKENS, WIDTH),
        n2=b(ROWS_HERE, PATCHES, WIDTH),
        fac=b(ROWS_HERE, PATCHES, 2 * HIDDEN),
        hid=b(ROWS_HERE, PATCHES, HIDDEN),
        dx2=b(8, TOKENS, WIDTH),
        dx1=b(8, TOKENS, WIDTH),
        dmix=b(ROWS_HERE, PATCHES, MINE),
        dqkv=b(ROWS_HERE, PATCHES, 3 * MINE),
        dqc=b(ROWS_HERE, PATCHES, MINE),
        dkvc=b(ROWS_HERE, BYTES, 2 * MINE),
        p=b(8, TOKENS, WIDTH),
        r1=b(ROWS_HERE, 2, TOKENS, WIDTH),
        q2=b(ROWS_HERE, TOKENS, WIDTH),
        r2=b(ROWS_HERE, TOKENS, WIDTH),
        bp=b(8, TOKENS_B, WIDTH),
        br1=b(ROWS_HERE, 2, TOKENS_B, WIDTH),
        br2=b(ROWS_HERE, TOKENS_B, WIDTH),
    )
    return plan


INS = ("patch_in", "byte", "cot_in", "sizes", "lengths", "attn_in", "wo_in", "gate_up_in", "down", "gains")
OUTS = ("out", "gpatch", "gbyte", "g_attn", "g_out", "g_gate", "g_down")


def step_kernel(names, *refs):
    m = SimpleNamespace(**dict(zip(INS + OUTS + tuple(names), refs)))
    dp, pipe = lax.axis_index("dp"), lax.axis_index("pipe")
    z, x, y, c = dp // SIDE, dp % SIDE, pipe // 2, pipe % 2
    at = lambda z, x, y, c: (z * SIDE + x, y * 2 + c)
    sibling, across, aside = at(z, x, y, 1 - c), at(z, x, 1 - y, c), at(z, 1 - x, y, c)
    right, left = at((z + 1) % LINE, x, y, c), at((z + LINE - 1) % LINE, x, y, c)
    corner = at(z, x, 1 - y, 1 - c)
    counter = [0]

    def take(count=1):
        first = counter[0]
        counter[0] += count
        assert counter[0] <= NSEM
        return first

    unfinished = []

    def remote(src, dst, device, send=None, recv=None):
        send = take() if send is None else send
        recv = take() if recv is None else recv
        return pltpu.make_async_remote_copy(
            src_ref=src, dst_ref=dst, send_sem=m.sem.at[send], recv_sem=m.sem.at[recv], device_id=device, device_id_type=MESH
        )

    def begin(copy):
        copy.start()
        unfinished.append(copy.wait_send)
        return copy

    def near(src, dst):
        copy = pltpu.make_async_copy(src, dst, m.sem.at[take()])
        copy.start()
        return copy

    local_out = near(m.wo_in, m.won.at[:, z, x])
    attn_here, gate_here, patch_here = near(m.attn_in, m.attn), near(m.gate_up_in, m.gate_up), near(m.patch_in, m.patch)
    bytes_in, cot_here = near(m.byte, m.bp), near(m.cot_in, m.cot)

    barrier = pltpu.get_barrier_semaphore()
    for device in (sibling, across, corner, aside):
        pl.semaphore_signal(barrier, inc=1, device_id=device, device_id_type=MESH)

    @pl.when(z < LINE - 1)
    def _():
        pl.semaphore_signal(barrier, inc=1, device_id=right, device_id_type=MESH)

    @pl.when(z > 0)
    def _():
        pl.semaphore_signal(barrier, inc=1, device_id=left, device_id_type=MESH)

    pl.semaphore_wait(barrier, 4 + (z < LINE - 1).astype(jnp.int32) + (z > 0).astype(jnp.int32))

    class Gather:
        def __init__(self, view):
            self.view = view
            self.sx, self.rx = take(LINE), take(LINE)
            self.sz, self.rz = take(LINE + 1), take(LINE)

        def copy(self, block, device, send, recv):
            there = self.view(block * SIDE + x)
            return remote(there, there, device, send, recv + block)

        def aside(self, block):
            return self.copy(block, aside, self.sx + block, self.rx)

        def right(self, block):
            return self.copy(block, right, self.sz + block, self.rz)

        def left(self, block):
            return self.copy(block, left, self.sz + jnp.where(block == z, LINE, block), self.rz)

        def start(self):
            self.aside(z).start()

            @pl.when(z < LINE - 1)
            def _():
                self.right(z).start()

            @pl.when(z > 0)
            def _():
                self.left(z).start()

        def hop(self, k):
            @pl.when(z - k >= 0)
            def _():
                self.right(z - k).wait_recv()
                self.aside(z - k).start()

                @pl.when(z < LINE - 1)
                def _():
                    self.right(z - k).start()

            @pl.when(z + k < LINE)
            def _():
                self.left(z + k).wait_recv()
                self.aside(z + k).start()

                @pl.when(z > 0)
                def _():
                    self.left(z + k).start()

        def ready(self):
            for block in range(LINE):
                self.aside(block).wait_recv()

        def finish(self):
            for block in range(LINE):
                self.aside(block).wait_send()

                @pl.when((z < LINE - 1) & (z >= block))
                def _():
                    self.right(block).wait_send()

                @pl.when((z > 0) & (z <= block))
                def _():
                    self.left(block).wait_send()

    class GatherPairs(Gather):
        def copy(self, block, device, send, recv):
            there = self.view(block * SIDE, SIDE)
            return remote(there, there, device, send, recv + block)

        def start(self):
            there = self.view(z * SIDE + x, 1)
            self.side = begin(remote(there, there, aside, self.sx, self.rx))

        def line(self):
            self.side.wait_recv()

            @pl.when(z < LINE - 1)
            def _():
                self.right(z).start()

            @pl.when(z > 0)
            def _():
                self.left(z).start()

        def hop(self, k):
            @pl.when(z - k >= 0)
            def _():
                self.right(z - k).wait_recv()

                @pl.when(z < LINE - 1)
                def _():
                    self.right(z - k).start()

            @pl.when(z + k < LINE)
            def _():
                self.left(z + k).wait_recv()

                @pl.when(z > 0)
                def _():
                    self.left(z + k).start()

        def ready(self):
            pass

        def finish(self):
            for block in range(LINE):

                @pl.when((z < LINE - 1) & (z >= block))
                def _():
                    self.right(block).wait_send()

                @pl.when((z > 0) & (z <= block))
                def _():
                    self.left(block).wait_send()

    g_out0 = Gather(lambda d: m.won.at[0, d // SIDE, d % SIDE])
    g_out1 = Gather(lambda d: m.won.at[1, d // SIDE, d % SIDE])
    g_attn0 = Gather(lambda d: m.wa.at[pl.ds(0, 3), pl.ds(d * SEG, SEG)])
    g_attn1 = Gather(lambda d: m.wa.at[pl.ds(3, 3), pl.ds(d * SEG, SEG)])
    g_gate = Gather(lambda d: m.wg.at[pl.ds(d * SEG, SEG)])
    g_down = GatherPairs(lambda d, count: m.wd.at[pl.ds(d * PADDED, count * PADDED)])

    def pieces(values, starts, width):
        return jnp.concatenate([values[:, first : first + width] for first in starts], axis=1)

    def spread(src, dst):
        copies = [near(src(pipe), dst)]
        for device in (across, corner, sibling):
            copies.append(begin_early(remote(src(device[1]), dst, device)))
        return copies

    early_sends = []

    def begin_early(copy):
        copy.start()
        early_sends.append(copy.wait_send)
        return copy

    def arrived(copies):
        copies[0].wait()
        for copy in copies[1:]:
            copy.wait_recv()

    def spread_attn(layer):
        for part in range(3 * layer, 3 * layer + 3):
            values = m.attn[part].astype(F32)
            for rank in range(RANKS):
                heads = [8 * (rank % 2) + 2 * j + rank // 2 for j in range(HEADS_MINE)]
                m.xa[part, rank, 0:SHARD, :] = pieces(values, [h * HEAD_DIM for h in heads], HEAD_DIM).astype(BF)
        three = pl.ds(3 * layer, 3)
        return spread(lambda q: m.xa.at[three, q, pl.ds(0, SHARD)], m.wa.at[three, pl.ds(dp * SEG + pipe * SHARD, SHARD)])

    def spread_gate():
        for which in range(2):
            values = m.gate_up[which].astype(F32)
            values = jnp.concatenate([values, jnp.zeros((SHARD, 128), F32)], axis=1)
            keep = (lax.broadcasted_iota(jnp.int32, (SHARD, HIDDEN), 1) % PADDED) < UNITS
            for rank in range(RANKS):
                starts = [UNITS * (RANKS * d + rank) for d in range(GROUPS)]
                runs = jnp.where(keep, pieces(values, starts, PADDED), 0.0)
                m.xg[rank, 0:SHARD, which * HIDDEN : (which + 1) * HIDDEN] = runs.astype(BF)
        return spread(lambda q: m.xg.at[q, pl.ds(0, SHARD)], m.wg.at[pl.ds(dp * SEG + pipe * SHARD, SHARD)])

    def begin_after(copies, gather):
        arrived(copies)
        gather.start()

    queue = []

    def pump(count):
        for _ in range(min(count, len(queue))):
            queue.pop(0)()

    def swap_out(layer):
        mine, there = m.won.at[layer, pl.ds(2 * c, 2)], m.woh.at[layer, :, :, pl.ds(c * SHARD, SHARD)]
        keep = near(mine, there)
        give = remote(m.won.at[layer, pl.ds(2 * (1 - c), 2)], there, sibling)
        give.start()
        return keep, give

    def swapped(swap):
        swap[0].wait()
        swap[1].wait_recv()

    lane = lax.broadcasted_iota(jnp.int32, (1, MINE), 1) // HEAD_DIM
    head_mask = [(lane == j).astype(F32).astype(BF) for j in range(HEADS_MINE)]
    scaled_mask = [((lane == j).astype(F32) * SCALE).astype(BF) for j in range(HEADS_MINE)]

    def gain(index):
        return m.gains[index : index + 1, :]

    def factor_of(values):
        return lax.rsqrt(jnp.mean(values * values, axis=-1, keepdims=True) + EPSILON)

    def normed(values, index):
        values = values.astype(F32)
        return (values * factor_of(values) * gain(index)).astype(BF)

    def norm_back(values, gradient, index):
        values = values.astype(F32)
        factor = factor_of(values)
        weighted = gradient * gain(index)
        return factor * weighted - values * (factor * factor * factor) * jnp.mean(weighted * values, axis=-1, keepdims=True)

    def normed_rows(src, dst, index, r):
        for part in range(RANKS):
            for half in range(2):
                rows = pl.ds(half * (TOKENS // 2), TOKENS // 2)
                dst[r, pl.ds(part * TOKENS + half * (TOKENS // 2), TOKENS // 2)] = normed(src[4 * r + part, rows], index)

    class Reduce:
        def __init__(self, p, r1, q2, r2, tokens, sems):
            self.p, self.r1, self.q2, self.r2, self.tokens, self.sems = p, r1, q2, r2, tokens, sems
            self.first, self.second = {}, {}

        def give(self, r):
            self.first[r] = [
                remote(self.p.at[4 * r + 2 * side + 1 - c], self.r1.at[r, side], sibling, *pair_at(self.sems, 2 * r + side))
                for side in range(2)
            ]
            for copy in self.first[r]:
                copy.start()

        def cross(self, r):
            for copy in self.first[r]:
                copy.wait_recv()
            other = 4 * r + 2 * (1 - y) + c
            self.q2[r] = (self.p[other].astype(F32) + self.r1[r, 1 - y].astype(F32)).astype(BF)
            self.second[r] = remote(self.q2.at[r], self.r2.at[r], across, *pair_at(self.sems, 4 + r))
            self.second[r].start()

        def arrive(self, r):
            self.second[r].wait_recv()

        def free(self):
            for r in range(ROWS_HERE):
                for copy in self.first[r]:
                    copy.wait_send()
                self.second[r].wait_send()

        def total(self, r, rows):
            own = 4 * r + pipe
            return (
                self.p[own, rows].astype(F32) + self.r1[r, y, rows].astype(F32) + self.r2[r, rows].astype(F32)
            )

    class Share:
        def __init__(self, values, sems):
            self.values, self.sems, self.copies, self.last = values, sems, {}, {}

        def give(self, r):
            there = self.values.at[4 * r + pipe]
            self.copies[r] = [
                remote(there, there, device, *pair_at(self.sems, 3 * r + k)) for k, device in enumerate((across, sibling))
            ]
            for copy in self.copies[r]:
                copy.start()

        def relay(self, r):
            self.copies[r][0].wait_recv()
            there = self.values.at[4 * r + 2 * (1 - y) + c]
            self.last[r] = remote(there, there, sibling, *pair_at(self.sems, 3 * r + 2))
            self.last[r].start()

        def ready(self, r):
            self.copies[r][1].wait_recv()
            self.last[r].wait_recv()

        def free(self):
            for r in range(ROWS_HERE):
                for copy in self.copies[r] + [self.last[r]]:
                    copy.wait_send()

    def pair_at(first, index):
        return first + 2 * index, first + 2 * index + 1

    sums_a, sums_b, shares = take(12), take(12), take(12)

    halves = [pl.ds(h * (TOKENS // 2), TOKENS // 2) for h in range(2)]

    def to_owner(reduce, left_of, r):
        for n in range(4):
            cols = pl.ds(n * 256, 256)
            reduce.p[4 * r : 4 * r + 4, :, cols] = left_of(r, n).astype(BF).reshape(4, reduce.tokens, 256)
        reduce.give(r)

    local_out.wait()
    g_out0.start()
    g_out1.start()
    m.wd[pl.ds(pl.multiple_of(dp * PADDED, 32), PADDED), :] = jnp.concatenate(
        [m.down[...], jnp.zeros((PADDED - UNITS, WIDTH), BF)], axis=0
    )
    g_down.start()
    attn_here.wait()
    exchange0 = spread_attn(0)
    exchange1 = spread_attn(1)
    gate_here.wait()
    exchange2 = spread_gate()
    begin_after(exchange0, g_attn0)
    patch_here.wait()

    @pl.loop(0, ROWS_HERE * PATCHES // 32)
    def _(i):
        rows = pl.ds((i % 8) * 32, 32)
        m.nq[i // 8, rows] = normed(m.patch[i // 8, rows], 0)

    bytes_in.wait()
    cot_here.wait()

    @pl.loop(0, 8)
    def _(i):
        for part in range(5):
            rows = pl.ds(part * 32, 32)
            m.nb[i // 4, pl.ds((i % 4) * TOKENS_B + part * 32, 32)] = normed(m.bp[i, rows], 1)

    def hops(gather):
        return [functools.partial(gather.hop, k) for k in (1, 2, 3)]

    h_out0, h_attn0, h_out1, h_attn1, h_gate, h_down = map(hops, (g_out0, g_attn0, g_out1, g_attn1, g_gate, g_down))
    queue += [h_out0[0], h_out1[0], h_attn0[0], h_out0[1], h_out1[1], h_attn0[1], h_out0[2], h_out1[2]]
    queue += [lambda: begin_after(exchange1, g_attn1), h_attn0[2]]
    queue += [h_attn1[0], lambda: begin_after(exchange2, g_gate), h_attn1[1], h_attn1[2]]
    pump(len(queue))
    queue += [lambda: [wait() for wait in early_sends]] + h_gate[:2] + [g_down.line, h_gate[2]] + h_down
    g_out0.ready()
    swap0 = swap_out(0)
    g_attn0.ready()

    for r in range(ROWS_HERE):
        m.qc[r] = product(m.nq[r], m.wa[0]).astype(BF)

    @pl.loop(0, 4)
    def _(i):
        rows = pl.ds((i % 2) * (BYTES // 2), BYTES // 2)
        block = m.nb[i // 2, rows]
        m.kc[i // 2, rows] = product(block, m.wa[1]).astype(BF)
        m.vc[i // 2, rows] = product(block, m.wa[2]).astype(BF)

    def window(r):
        sizes = m.sizes[pl.ds(r, 1), :].astype(F32)
        i = lax.broadcasted_iota(jnp.int32, (PATCHES, PATCHES), 0)
        j = lax.broadcasted_iota(jnp.int32, (PATCHES, PATCHES), 1)
        first = jnp.sum(jnp.where(j < i, sizes, 0.0), axis=1, keepdims=True)
        last = jnp.sum(jnp.where(j <= i, sizes, 0.0), axis=1, keepdims=True)
        position = lax.broadcasted_iota(jnp.int32, (PATCHES, BYTES), 1).astype(F32)
        return (position >= first) & (position < last)

    def causal(r):
        length = m.lengths[r]
        i = lax.broadcasted_iota(jnp.int32, (PATCHES, PATCHES), 0)
        j = lax.broadcasted_iota(jnp.int32, (PATCHES, PATCHES), 1)
        return (j <= i) & (j < length)

    def weights_of(query, keys, allowed):
        scores = jnp.where(allowed, product_right(query, keys), NEGATIVE)
        raised = jnp.exp(scores - jnp.max(scores, axis=-1, keepdims=True))
        return raised * (1.0 / jnp.sum(raised, axis=-1, keepdims=True))

    def attend(r, allowed, queries, keys, values, mixed):
        total = None
        for j in range(HEADS_MINE):
            low = weights_of(queries[r] * scaled_mask[j], keys[r], allowed).astype(BF)
            term = product(low, values[r] * head_mask[j])
            total = term if total is None else total + term
        mixed[r] = total.astype(BF)

    def attend_back(r, allowed, queries, keys, values, grad):
        sums = [None, None, None]
        for j in range(HEADS_MINE):
            query, mixed = queries[r] * scaled_mask[j], grad[r] * head_mask[j]
            weights = weights_of(query, keys[r], allowed)
            grad_weights = product_right(mixed, values[r])
            grad_scores = weights * (grad_weights - jnp.sum(weights * grad_weights, axis=-1, keepdims=True))
            grad_scores = grad_scores.astype(BF)
            terms = (
                product(grad_scores, keys[r] * head_mask[j]),
                product_left(grad_scores, query),
                product_left(weights.astype(BF), mixed),
            )
            sums = [t if s is None else s + t for s, t in zip(sums, terms)]
        return (sums[0] * SCALE).astype(BF), sums[1].astype(BF), sums[2].astype(BF)

    def out_rows(layer):
        return lambda n: m.woh[layer, :, :, :, pl.ds(n * 256, 256)].reshape(MINE, 256)

    def residual(reduce, share, base, result, r):
        reduce.arrive(r)
        for rows in halves:
            result[4 * r + pipe, rows] = (base(r, rows) + reduce.total(r, rows)).astype(BF)
        share.give(r)

    first_sum, first_share = Reduce(m.p, m.r1, m.q2, m.r2, TOKENS, sums_a), Share(m.x1, shares)
    attend(0, window(0), m.qc, m.kc, m.vc, m.oc)
    swapped(swap0)
    to_owner(first_sum, lambda r, n: product(m.oc[r], out_rows(0)(n)), 0)
    attend(1, window(1), m.qc, m.kc, m.vc, m.oc)
    first_sum.cross(0)
    to_owner(first_sum, lambda r, n: product(m.oc[r], out_rows(0)(n)), 1)
    pump(2)
    first_sum.cross(1)
    pump(2)
    own_patch = lambda r, rows: m.patch[r, pl.ds(pipe * TOKENS + rows.start, TOKENS // 2)].astype(F32)
    for r in range(ROWS_HERE):
        residual(first_sum, first_share, own_patch, m.x1, r)
    first_share.relay(0)
    g_out1.ready()
    swap1 = swap_out(1)
    g_attn1.ready()
    queries, keys, values = m.qkv.at[0], m.qkv.at[1], m.qkv.at[2]

    def project(r):
        first_share.ready(r)
        normed_rows(m.x1, m.n1, 2, r)
        for part in range(3):
            m.qkv[part, r] = product(m.n1[r], m.wa[3 + part]).astype(BF)

    project(0)
    attend(0, causal(0), queries, keys, values, m.o)
    first_sum.free()
    second_sum, second_share = Reduce(m.p, m.r1, m.q2, m.r2, TOKENS, sums_a), Share(m.x2, shares)
    swapped(swap1)
    to_owner(second_sum, lambda r, n: product(m.o[r], out_rows(1)(n)), 0)
    first_share.relay(1)
    project(1)
    first_share.free()
    attend(1, causal(1), queries, keys, values, m.o)
    second_sum.cross(0)
    to_owner(second_sum, lambda r, n: product(m.o[r], out_rows(1)(n)), 1)
    pump(1)
    second_sum.cross(1)
    pump(1)
    own_of = lambda values: lambda r, rows: values[4 * r + pipe, rows].astype(F32)
    for r in range(ROWS_HERE):
        residual(second_sum, second_share, own_of(m.x1), m.x2, r)
    for r in range(ROWS_HERE):
        second_share.relay(r)
    for r in range(ROWS_HERE):
        second_share.ready(r)
        normed_rows(m.x2, m.n2, 3, r)

    pump(len(queue) - 1)
    g_gate.ready()
    tiles = HIDDEN // 256
    for r in range(ROWS_HERE):
        for n in range(tiles):
            first, later = pl.ds(n * 256, 256), pl.ds(HIDDEN + n * 256, 256)
            gate = product(m.n2[r], m.wg[:, first])
            up = product(m.n2[r], m.wg[:, later])
            sig = jax.nn.sigmoid(gate)
            silu = gate * sig
            m.hid[r, :, first] = (silu * up).astype(BF)
            m.fac[r, :, first] = (up * sig * (1.0 + gate * (1.0 - sig))).astype(BF)
            m.fac[r, :, later] = silu.astype(BF)

    class Scatter:
        def __init__(self, mine, xbuf, zbuf):
            self.mine, self.xbuf, self.zbuf = mine, xbuf, zbuf
            self.sx, self.rx = take(LINE), take(LINE)
            self.sz, self.rz = take(LINE), take(LINE + 1)

        def aside(self, block):
            return remote(self.mine(block * SIDE + 1 - x), self.xbuf(block), aside, self.sx + block, self.rx + block)

        def start(self):
            for block in (3, 0, 2, 1):
                self.aside(block).start()

        def add(self, into, values):
            into[...] = (into[...].astype(F32) + values[...].astype(F32)).astype(BF)

        def line(self, block):
            return self.mine(block * SIDE + x)

        def right(self, block):
            return remote(self.line(block), self.zbuf(block), right, self.sz + block, self.rz + block)

        def left(self, block, slot):
            return remote(self.line(block), self.zbuf(slot), left, self.sz + block, self.rz + slot)

        def send_left(self, block):
            self.left(block, jnp.where(z - 1 == block, LINE, block)).start()

        def emit(self, rightward, leftward):
            @pl.when(z == 0)
            def _():
                for block in rightward:
                    self.right(block).start()

            @pl.when(z == LINE - 1)
            def _():
                for block in leftward:
                    self.send_left(block)

        def take(self, block):
            self.aside(block).wait_recv()
            self.add(self.line(block), self.xbuf(block))
            self.emit(*{3: ((3,), ()), 0: ((), (0,)), 2: ((2,), ()), 1: ((1,), (1, 2))}[block])

        def tick(self, t):
            @pl.when((z >= 1) & (z <= t))
            def _():
                block = LINE - 1 - t + z
                self.right(block).wait_recv()
                self.add(self.line(block), self.zbuf(block))

                @pl.when(z < block)
                def _():
                    self.right(block).start()

            @pl.when((z < LINE - 1) & (z >= LINE - 1 - t))
            def _():
                block = t - (LINE - 1) + z
                slot = jnp.where(z == block, LINE, block)
                self.left(block, slot).wait_recv()
                self.add(self.line(block), self.zbuf(slot))

                @pl.when(z > block)
                def _():
                    self.send_left(block)

        def finish(self):
            for block in range(LINE):
                self.aside(block).wait_send()
            self.finish_line()

        def finish_line(self):
            for block in range(LINE):

                @pl.when(z < block)
                def _():
                    self.right(block).wait_send()

                @pl.when(z > block)
                def _():
                    self.left(block, 0).wait_send()

    class ScatterPairs(Scatter):
        def line(self, block):
            return self.mine(block * SIDE, SIDE)

        def start(self):
            self.emit((3, 2, 1), (0, 1, 2))

        def cross(self):
            self.side = begin(remote(self.mine(z * SIDE + 1 - x, 1), self.xbuf, aside, self.sx, self.rx))

        def last(self):
            self.side.wait_recv()
            self.add(self.mine(z * SIDE + x, 1), self.xbuf)

    pump(1)

    s_down = ScatterPairs(lambda d, count: m.dd.at[pl.ds(d * PADDED, count * PADDED)], m.xd, lambda b: m.zd.at[b])
    s_gate = Scatter(lambda d: m.dg.at[pl.ds(d * SEG, SEG)], lambda b: m.xg.at[b], lambda b: m.zg.at[b])

    def hidden_back(r):
        for n in range(tiles):
            first, later = pl.ds(n * 256, 256), pl.ds(HIDDEN + n * 256, 256)
            grad = product_right(m.cot[r], m.wd[first, :]).astype(BF).astype(F32)
            m.fac[r, :, first] = (grad * m.fac[r, :, first].astype(F32)).astype(BF)
            m.fac[r, :, later] = (grad * m.fac[r, :, later].astype(F32)).astype(BF)

    def gate_grad(block):
        rows = pl.ds(block * 256, 256)
        total = product_left(m.n2[0, :, rows], m.fac[0]) + product_left(m.n2[1, :, rows], m.fac[1])
        m.dg[rows, :] = total.astype(BF)
        s_gate.aside(block).start()

    second_sum.free()
    second_share.free()
    third_sum, third_share = Reduce(m.p, m.r1, m.q2, m.r2, TOKENS, sums_a), Share(m.dx2, shares)
    for r in range(ROWS_HERE):
        hidden_back(r)
        to_owner(third_sum, lambda r, n: product_right(m.fac[r], m.wg[n * 256 : n * 256 + 256, :]), r)
    third_sum.cross(0)
    gate_grad(3)
    third_sum.cross(1)
    gate_grad(0)

    @pl.loop(0, tiles)
    def _(n):
        cols = pl.ds(pl.multiple_of(n * 256, 256), 256)
        for half in range(2):
            wide = pl.ds(half * 512, 512)
            total = product_left(m.hid[0, :, cols], m.cot[0, :, wide]) + product_left(m.hid[1, :, cols], m.cot[1, :, wide])
            m.dd[cols, wide] = total.astype(BF)

    s_down.start()
    gate_grad(2)
    gate_grad(1)

    def gradient_in(reduce, share, base, values, index, result, r):
        reduce.arrive(r)
        for rows in halves:
            back = norm_back(values(r, rows), reduce.total(r, rows), index)
            result(r, rows, (base(r, rows) + back).astype(BF))
        if share is not None:
            share.give(r)

    def into(ref):
        def store(r, rows, value):
            ref[4 * r + pipe, rows] = value

        return store

    own_cot = lambda r, rows: m.cot[r, pl.ds(pipe * TOKENS + rows.start, TOKENS // 2)].astype(F32)
    for r in range(ROWS_HERE):
        gradient_in(third_sum, third_share, own_cot, own_of(m.x2), 3, into(m.dx2), r)

    early = pl.ds(0, TOKENS)
    out_sum = Reduce(m.bp.at[:, early], m.br1.at[:, :, early], m.n2.at[:, early], m.br2.at[:, early], TOKENS, sums_b)
    for r in range(ROWS_HERE):
        to_owner(out_sum, lambda r, n: product(m.hid[r], m.wd[:, n * 256 : n * 256 + 256]), r)
    third_share.relay(0)
    for r in range(ROWS_HERE):
        out_sum.cross(r)
    third_share.relay(1)

    def rows_of(ref, r):
        return ref[4 * r : 4 * r + 4].reshape(PATCHES, WIDTH)

    def mixed_back(share, grads, layer, r):
        share.ready(r)
        m.dmix[r] = product_right(rows_of(grads, r), m.woh[layer].reshape(MINE, WIDTH)).astype(BF)

    def attn_back(left, n, first, count):
        total = None
        for part in range(count):
            term = product_right(left[:, part * MINE : part * MINE + MINE], m.wa[first + part, pl.ds(n * 256, 256), :])
            total = term if total is None else total + term
        return total

    def global_back(r):
        mixed_back(third_share, m.dx2, 1, r)
        dq, dk, dv = attend_back(r, causal(r), queries, keys, values, m.dmix)
        m.dqkv[r, :, 0:MINE] = dq
        m.dqkv[r, :, MINE : 2 * MINE] = dk
        m.dqkv[r, :, 2 * MINE : 3 * MINE] = dv

    s_down.tick(1)
    global_back(0)
    third_sum.free()
    fourth_sum, fourth_share = Reduce(m.p, m.r1, m.q2, m.r2, TOKENS, sums_a), Share(m.dx1, shares)
    to_owner(fourth_sum, lambda r, n: attn_back(m.dqkv.at[r], n, 3, 3), 0)
    global_back(1)
    third_share.free()
    fourth_sum.cross(0)
    to_owner(fourth_sum, lambda r, n: attn_back(m.dqkv.at[r], n, 3, 3), 1)

    def own_half(layer, which):
        return m.won.at[layer, :, which]

    def out_grad(layer, mixed, grads):
        (g_out0, g_out1)[layer].finish()
        (swap0, swap1)[layer][1].wait_send()
        total = None
        for r in range(ROWS_HERE):
            term = product_left(mixed[r], rows_of(grads, r))
            total = term if total is None else total + term
        m.won[layer] = total.astype(BF).reshape(LINE, SIDE, SHARD, WIDTH)
        there = m.don.at[layer, pl.ds(HEADS_MINE * c, HEADS_MINE)]
        keep = near(own_half(layer, c), there)
        give = remote(own_half(layer, 1 - c), there, sibling)
        begin(give)
        return keep, give

    def attn_grad(first, count, left, right):
        @pl.loop(0, 4)
        def _(n):
            cols = pl.ds(pl.multiple_of(n * 256, 256), 256)
            total = product_left(left[0, :, cols], right[0]) + product_left(left[1, :, cols], right[1])
            for part in range(count):
                m.da[first + part, cols, :] = total[:, part * MINE : part * MINE + MINE].astype(BF)

    def scatter_out(layer):
        return Scatter(lambda d: m.don.at[layer, d], lambda b: m.xo.at[layer, b], lambda b: m.zo.at[layer, b])

    def scatter_attn(first, count):
        part = pl.ds(first, count)
        return Scatter(lambda d: m.da.at[part, pl.ds(d * SEG, SEG)], lambda b: m.xa.at[part, b], lambda b: m.za.at[part, b])

    swap2 = out_grad(1, m.o, m.dx2)
    fourth_sum.cross(1)
    attn_grad(3, 3, m.n1, m.dqkv)
    s_out1, s_attn1 = scatter_out(1), scatter_attn(3, 3)
    swapped(swap2)
    s_out1.start()
    s_attn1.start()
    s_gate.take(3)
    s_gate.take(0)
    s_down.tick(2)
    for r in range(ROWS_HERE):
        out_sum.arrive(r)
        for rows in halves:
            m.out[r, rows] = (own_of(m.x2)(r, rows) + out_sum.total(r, rows)).astype(BF)
    for r in range(ROWS_HERE):
        gradient_in(fourth_sum, fourth_share, own_of(m.dx2), own_of(m.x1), 2, into(m.dx1), r)
    s_gate.take(2)
    fourth_share.relay(0)

    def cross_back(r):
        mixed_back(fourth_share, m.dx1, 0, r)
        dq, dk, dv = attend_back(r, window(r), m.qc, m.kc, m.vc, m.dmix)
        m.dqc[r] = dq
        m.dkvc[r, :, 0:MINE] = dk
        m.dkvc[r, :, MINE : 2 * MINE] = dv

    cross_back(0)
    fourth_share.relay(1)
    s_down.tick(3)
    s_down.cross()
    s_gate.take(1)
    cross_back(1)
    s_gate.tick(1)
    attn_grad(1, 2, m.nb, m.dkvc)
    s_attn0b = scatter_attn(1, 2)
    s_attn0b.start()
    attn_grad(0, 1, m.nq, m.dqc)
    s_attn0a = scatter_attn(0, 1)
    s_attn0a.start()
    swap3 = out_grad(0, m.oc, m.dx1)

    out_sum.free()
    fourth_sum.free()
    byte_sum = Reduce(m.bp, m.br1, m.n2.at[:, pl.ds(0, TOKENS_B)], m.br2, TOKENS_B, sums_b)
    fifth_sum = Reduce(m.p, m.r1, m.q2, m.r2, TOKENS, sums_a)
    for r in range(ROWS_HERE):
        to_owner(byte_sum, lambda r, n: attn_back(m.dkvc.at[r], n, 1, 2), r)
    for r in range(ROWS_HERE):
        to_owner(fifth_sum, lambda r, n: attn_back(m.dqc.at[r], n, 0, 1), r)
    own_bytes = [near(m.byte.at[4 * r + pipe], m.gbyte.at[r]) for r in range(ROWS_HERE)]
    s_out0 = scatter_out(0)
    swapped(swap3)
    s_out0.start()
    for r in range(ROWS_HERE):
        byte_sum.cross(r)
    for r in range(ROWS_HERE):
        fifth_sum.cross(r)
    def back_to_pipe(rows_ref, dst):
        copies = [near(rows_ref(pipe), dst)]
        for device in (across, corner, sibling):
            copies.append(begin(remote(rows_ref(device[1]), dst, device)))
        return copies

    def attn_home(first, count):
        src = lambda q: m.da.at[pl.ds(first, count), pl.ds(dp * SEG + q * SHARD, SHARD)]
        return back_to_pipe(src, m.g_attn.at[pipe, pl.ds(first, count)])

    def gate_home():
        src = lambda q: m.dg.at[pl.ds(dp * SEG + q * SHARD, SHARD)]
        return back_to_pipe(src, m.g_gate.at[pipe])

    for block in (3, 0, 2, 1):
        s_out1.take(block)
    s_gate.tick(2)
    s_attn1.take(3)
    s_out1.tick(1)
    s_attn1.take(0)
    s_out1.tick(2)
    s_gate.tick(3)
    home = [gate_home()]
    s_attn1.take(2)
    s_attn1.tick(1)
    s_out1.tick(3)
    for r in range(ROWS_HERE):
        gradient_in(
            fifth_sum,
            None,
            own_of(m.dx1),
            own_patch,
            0,
            lambda r, rows, value: m.gpatch.__setitem__((r, rows), value),
            r,
        )
    s_attn1.take(1)
    s_attn1.tick(2)
    s_attn0b.take(3)
    s_attn0b.take(0)
    s_attn1.tick(3)
    home.append(attn_home(3, 3))
    s_attn0b.take(2)
    s_attn0b.tick(1)
    s_attn0b.take(1)
    for copy in own_bytes:
        copy.wait()
    for r in range(ROWS_HERE):
        byte_sum.arrive(r)
        for part in range(5):
            rows = pl.ds(part * 32, 32)
            back = norm_back(m.gbyte[r, rows], byte_sum.total(r, rows), 1)
            m.gbyte[r, rows] = back.astype(BF)
    s_attn0b.tick(2)
    for block in (3, 0, 2, 1):
        s_attn0a.take(block)
    s_attn0b.tick(3)
    home.append(attn_home(1, 2))
    s_attn0a.tick(1)
    for block in (3, 0):
        s_out0.take(block)
    s_attn0a.tick(2)
    for block in (2, 1):
        s_out0.take(block)
    s_attn0a.tick(3)
    home.append(attn_home(0, 1))
    s_down.last()
    s_out0.tick(1)
    s_out0.tick(2)
    s_out0.tick(3)
    m.g_down[...] = m.dd[pl.ds(pl.multiple_of(dp * PADDED, 32), PADDED), :]
    for layer in range(2):
        m.g_out[layer] = m.don[layer, dp]
    for copies in home:
        arrived(copies)
    for gather in (g_attn0, g_attn1, g_gate, g_down):
        gather.finish()
    s_down.finish_line()
    for scatter in (s_gate, s_attn1, s_out1, s_attn0a, s_attn0b, s_out0):
        scatter.finish()
    byte_sum.free()
    fifth_sum.free()
    fourth_share.free()
    for wait in unfinished:
        wait()


def finish_kernel(out, gpatch, gbyte, attn, gate_up, gains, da, do, dg, dd, out_, gpatch_, gbyte_, g_attn, g_out, g_gate, g_down, g_gain):
    for src, dst in ((out, out_), (gpatch, gpatch_), (gbyte, gbyte_)):
        dst[...] = src[...]
    place = lax.axis_index("dp") * RANKS + lax.axis_index("pipe")
    for part in range(6):
        got = [da[rank, part].astype(F32) for rank in range(RANKS)]
        heads = []
        for head in range(HEADS):
            rank, j = 2 * (head % 2) + head // 8, (head % 8) // 2
            heads.append(got[rank][:, j * HEAD_DIM : (j + 1) * HEAD_DIM])
        g_attn[part] = jnp.concatenate(heads, axis=1)
    for which in range(2):
        got = [dg[rank, :, which * HIDDEN : (which + 1) * HIDDEN].astype(F32) for rank in range(RANKS)]
        runs = [got[rank][:, PADDED * d : PADDED * d + UNITS] for d in range(GROUPS) for rank in range(RANKS)]
        g_gate[which] = jnp.concatenate(runs, axis=1)
    g_out[...] = do[...].astype(F32)
    g_down[...] = dd[0:UNITS].astype(F32)

    column = lax.broadcasted_iota(jnp.int32, (SHARD, WIDTH), 1)
    own = column == lax.broadcasted_iota(jnp.int32, (SHARD, WIDTH), 0) + place * SHARD

    def gain_gradient(row, parts):
        total = None
        for weight, grad in parts:
            term = jnp.sum(weight.astype(F32) * grad, axis=1, keepdims=True)
            total = term if total is None else total + term
        total = total / jnp.sum(jnp.where(own, gains[row : row + 1, :], 0.0), axis=1, keepdims=True)
        g_gain[row : row + 1, :] = jnp.transpose(jnp.broadcast_to(total, (SHARD, 128)))[0:1, :]

    gain_gradient(0, [(attn[0], g_attn[0])])
    gain_gradient(1, [(attn[i], g_attn[i]) for i in (1, 2)])
    gain_gradient(2, [(attn[i], g_attn[i]) for i in (3, 4, 5)])
    gain_gradient(3, [(gate_up[i], g_gate[i]) for i in range(2)])

def fused_step(patch_states, byte_states, cotangent, patch_lengths, row_lengths, attn_weights, out_weights, gate_up, down_weight, gains):
    plan = scratch_plan()
    vmem, anywhere = pl.BlockSpec(memory_space=pltpu.VMEM), pl.BlockSpec(memory_space=pl.ANY)
    shape = jax.ShapeDtypeStruct
    results = pl.pallas_call(
        functools.partial(step_kernel, tuple(plan)),
        out_shape=(
            shape((ROWS_HERE, TOKENS, WIDTH), BF),
            shape((ROWS_HERE, TOKENS, WIDTH), BF),
            shape((ROWS_HERE, TOKENS_B, WIDTH), BF),
            shape((RANKS, 6, SHARD, MINE), BF),
            shape((2, SHARD, WIDTH), BF),
            shape((RANKS, SHARD, 2 * HIDDEN), BF),
            shape((PADDED, WIDTH), BF),
        ),
        in_specs=[anywhere] * 3 + [vmem, pl.BlockSpec(memory_space=pltpu.SMEM)] + [anywhere] * 3 + [vmem] * 2,
        out_specs=[vmem] * 7,
        scratch_shapes=list(plan.values()),
        compiler_params=pltpu.CompilerParams(collective_id=0, has_side_effects=True, vmem_limit_bytes=63 * 2**20),
    )(
        patch_states,
        byte_states.reshape(8, TOKENS_B, WIDTH),
        cotangent,
        patch_lengths,
        row_lengths,
        attn_weights.reshape(6, SHARD, WIDTH),
        out_weights,
        gate_up,
        down_weight,
        gains,
    )
    finished = pl.pallas_call(
        finish_kernel,
        out_shape=(
            *(shape(array.shape, array.dtype) for array in results[:3]),
            shape((6, SHARD, WIDTH), F32),
            shape(out_weights.shape, F32),
            shape(gate_up.shape, F32),
            shape(down_weight.shape, F32),
            shape((4, SHARD), F32),
        ),
        in_specs=[vmem] * 10,
        out_specs=[vmem] * 8,
        compiler_params=pltpu.CompilerParams(vmem_limit_bytes=63 * 2**20),
    )(*results[:3], attn_weights.reshape(6, SHARD, WIDTH), gate_up, gains, *results[3:])
    return (*finished[:3], finished[3].reshape(attn_weights.shape), *finished[4:])


def solution(mesh):
    placed = (
        P("dp", None, None),
        P("dp", None, None),
        P("dp", None, None),
        P("dp", None),
        P("dp"),
        P(None, None, ("dp", "pipe"), None),
        P(None, ("dp", "pipe"), None),
        P(None, ("dp", "pipe"), None),
        P(("dp", "pipe"), None),
        P(),
    )
    return jax.shard_map(
        fused_step if mesh.shape["dp"] == GROUPS else gathered_step,
        mesh=mesh,
        in_specs=placed,
        out_specs=(
            P("dp", "pipe", None),
            P("dp", "pipe", None),
            P("dp", "pipe", None),
            P(None, None, ("dp", "pipe"), None),
            P(None, ("dp", "pipe"), None),
            P(None, ("dp", "pipe"), None),
            P(("dp", "pipe"), None),
            P(None, ("dp", "pipe")),
        ),
        check_vma=False,
    )
```

```python
import functools
from types import SimpleNamespace

import jax
import jax.numpy as jnp
from jax import lax
from jax.experimental import pallas as pl
from jax.experimental.pallas import tpu as pltpu
from jax.sharding import PartitionSpec as P

HEADS = 16
HEAD_DIM = 64
EPSILON = 1e-06
NEGATIVE = -1e30
SCALE = HEAD_DIM ** (-0.5)
BF = jnp.bfloat16
F32 = jnp.float32
MESH = pl.DeviceIdType.MESH


def dot(left, right, contract):
    return lax.dot_general(left, right, (contract, ((), ())), preferred_element_type=F32)


def product(left, right):
    return dot(left, right, ((1,), (0,)))


def product_left(left, right):
    return dot(left, right, ((0,), (0,)))


def product_right(left, right):
    return dot(left, right, ((1,), (1,)))


def norm_rows(values, gain):
    factor = lax.rsqrt(jnp.mean(values * values, axis=-1, keepdims=True) + EPSILON)
    return (values * factor * gain).astype(BF), factor


def norm_back(values, factor, gain, gradient):
    weighted = gradient * gain
    grad_gain = jnp.sum(gradient * values * factor, axis=0)
    grad_values = factor * weighted - values * factor**3 * jnp.mean(weighted * values, axis=-1, keepdims=True)
    return grad_values, grad_gain


def heads_of(values):
    return values.reshape(values.shape[0], HEADS, HEAD_DIM).transpose(1, 0, 2)


def rows_of(values):
    return values.transpose(1, 0, 2).reshape(values.shape[1], -1).astype(BF)


def batched(left, right, left_dim, right_dim):
    return lax.dot_general(left, right, (((left_dim,), (right_dim,)), ((0,), (0,))), preferred_element_type=F32)


def attend(queries, keys, values, allowed):
    scores = batched(queries, keys, 2, 2) * SCALE
    weights = jax.nn.softmax(jnp.where(allowed[None], scores, NEGATIVE), axis=-1)
    low = weights.astype(BF)
    return weights, low, rows_of(batched(low, values, 2, 1))


def attend_back(queries, keys, values, weights, low, grad_mixed):
    grad_weights = batched(grad_mixed, values, 2, 2)
    grad_scores = weights * (grad_weights - jnp.sum(weights * grad_weights, axis=-1, keepdims=True))
    grad_scores = grad_scores.astype(BF)
    return (
        rows_of(batched(grad_scores, keys, 2, 1) * SCALE),
        rows_of(batched(grad_scores, queries, 1, 1) * SCALE),
        rows_of(batched(low, grad_mixed, 1, 1)),
    )


def gathered_step(patch_states, byte_states, cotangent, patch_lengths, row_lengths, attn_weights, out_weights, gate_up, down_weight, gains):
    everyone = ("dp", "pipe")
    micro = patch_states.shape[0]
    stages = lax.axis_size("pipe")
    share = stages // micro
    place = lax.axis_index("pipe")
    row, part = place // share, place % share
    attn = lax.all_gather(attn_weights, everyone, axis=2, tiled=True)
    outw = lax.all_gather(out_weights, everyone, axis=1, tiled=True)
    gate_stack = lax.all_gather(gate_up, everyone, axis=1, tiled=True)
    down = lax.all_gather(down_weight, everyone, axis=0, tiled=True)

    def mine(source):
        return lax.dynamic_index_in_dim(source, row, 0, keepdims=False)

    def half(values):
        count = values.shape[0] // share
        return lax.dynamic_slice_in_dim(values, part * count, count, 0)

    def weight_grad(left, right):
        return product_left(half(left), half(right)).astype(BF)

    patch = mine(patch_states).astype(F32)
    byte = mine(byte_states).astype(F32)
    cot = mine(cotangent)
    sizes = mine(patch_lengths)
    length = mine(row_lengths)
    patches, bytes_ = patch.shape[0], byte.shape[0]

    nq, fq = norm_rows(patch, gains[0])
    nb, fb = norm_rows(byte, gains[1])
    qc = heads_of(product(nq, attn[0, 0]).astype(BF))
    kc = heads_of(product(nb, attn[0, 1]).astype(BF))
    vc = heads_of(product(nb, attn[0, 2]).astype(BF))
    ends = jnp.cumsum(sizes)[:, None]
    position = jnp.arange(bytes_, dtype=jnp.int32)[None, :]
    window = (position >= ends - sizes[:, None]) & (position < ends)
    pc32, pc, oc = attend(qc, kc, vc, window)
    x1 = (patch + product(oc, outw[0])).astype(BF)
    x1f = x1.astype(F32)
    n1, f1 = norm_rows(x1f, gains[2])
    q = heads_of(product(n1, attn[1, 0]).astype(BF))
    k = heads_of(product(n1, attn[1, 1]).astype(BF))
    v = heads_of(product(n1, attn[1, 2]).astype(BF))
    slot = jnp.arange(patches, dtype=jnp.int32)
    allowed = (slot[None, :] <= slot[:, None]) & (slot[None, :] < length)
    a32, a, o = attend(q, k, v, allowed)
    x2 = (x1f + product(o, outw[1])).astype(BF)
    x2f = x2.astype(F32)
    n2, f2 = norm_rows(x2f, gains[3])
    gate = product(n2, gate_stack[0])
    up = product(n2, gate_stack[1])
    sig = jax.nn.sigmoid(gate)
    hidden = (gate * sig * up).astype(BF)
    result = (x2f + product(hidden, down)).astype(BF)

    grad_down = weight_grad(hidden, cot)
    dh = product_right(cot, down).astype(BF).astype(F32)
    dgate = (dh * up * sig * (1.0 + gate * (1.0 - sig))).astype(BF)
    dup = (dh * gate * sig).astype(BF)
    grad_gate_up = jnp.stack([weight_grad(n2, dgate), weight_grad(n2, dup)])
    dn2 = product_right(dgate, gate_stack[0]) + product_right(dup, gate_stack[1])
    back, gain3 = norm_back(x2f, f2, gains[3], dn2)
    dx2 = (cot.astype(F32) + back).astype(BF)
    do = heads_of(product_right(dx2, outw[1]).astype(BF))
    dq, dk, dv = attend_back(q, k, v, a32, a, do)
    dn1 = product_right(dq, attn[1, 0]) + product_right(dk, attn[1, 1]) + product_right(dv, attn[1, 2])
    back, gain2 = norm_back(x1f, f1, gains[2], dn1)
    dx1 = (dx2.astype(F32) + back).astype(BF)
    doc = heads_of(product_right(dx1, outw[0]).astype(BF))
    dqc, dkc, dvc = attend_back(qc, kc, vc, pc32, pc, doc)
    back, gain0 = norm_back(patch, fq, gains[0], product_right(dqc, attn[0, 0]))
    grad_patch = (dx1.astype(F32) + back).astype(BF)
    back, gain1 = norm_back(byte, fb, gains[1], product_right(dkc, attn[0, 1]) + product_right(dvc, attn[0, 2]))
    grad_byte = back.astype(BF)
    grad_attn = jnp.stack(
        [
            jnp.stack([weight_grad(nq, dqc), weight_grad(nb, dkc), weight_grad(nb, dvc)]),
            jnp.stack([weight_grad(n1, dq), weight_grad(n1, dk), weight_grad(n1, dv)]),
        ]
    )
    grad_out = jnp.stack([weight_grad(oc, dx1), weight_grad(o, dx2)])
    grad_gains = jnp.where(part == 0, jnp.stack([gain0, gain1, gain2, gain3]), 0.0)

    def to_owner(values):
        whole = lax.all_gather(half(values), "pipe", axis=0, tiled=True)
        whole = whole.reshape(micro, -1, values.shape[1])
        count = whole.shape[1] // stages
        return lax.dynamic_slice_in_dim(whole, place * count, count, 1)

    def summed(values, axis):
        return lax.psum_scatter(values, everyone, scatter_dimension=axis, tiled=True).astype(F32)

    return (
        to_owner(result),
        to_owner(grad_patch),
        to_owner(grad_byte),
        summed(grad_attn, 2),
        summed(grad_out, 1),
        summed(grad_gate_up, 1),
        summed(grad_down, 0),
        summed(grad_gains, 1),
    )


LINE = 4
SIDE = 2
RANKS = 4
GROUPS = LINE * SIDE
ROWS_HERE = 2
PATCHES = 256
BYTES = 640
WIDTH = 1024
MINE = WIDTH // RANKS
HEADS_MINE = MINE // HEAD_DIM
TOKENS = PATCHES // RANKS
TOKENS_B = BYTES // RANKS
SHARD = WIDTH // (GROUPS * RANKS)
SEG = SHARD * RANKS
UNITS = 88
PADDED = 96
HIDDEN = GROUPS * PADDED
NSEM = 328
BIG = (("attn0", 0), ("attn1", 1))


def scratch_plan():
    b = lambda *shape: pltpu.VMEM(shape, BF)
    plan = dict(
        sem=pltpu.SemaphoreType.DMA((NSEM,)),
        patch=b(ROWS_HERE, PATCHES, WIDTH),
        cot=b(ROWS_HERE, PATCHES, WIDTH),
        attn=b(6, SHARD, WIDTH),
        gate_up=b(2, SHARD, GROUPS * RANKS * UNITS),
        wa=b(6, WIDTH, MINE),
        won=b(2, LINE, SIDE, SHARD, WIDTH),
        woh=b(2, 2, 2, HEAD_DIM, WIDTH),
        wg=b(WIDTH, 2 * HIDDEN),
        wd=b(HIDDEN, WIDTH),
        da=b(6, WIDTH, MINE),
        don=b(2, GROUPS, SHARD, WIDTH),
        dg=b(WIDTH, 2 * HIDDEN),
        dd=b(HIDDEN, WIDTH),
        xa=b(6, LINE, SEG, MINE),
        xo=b(2, LINE, SHARD, WIDTH),
        xg=b(LINE, SEG, 2 * HIDDEN),
        xd=b(PADDED, WIDTH),
        za=b(6, LINE + 1, SEG, MINE),
        zo=b(2, LINE + 1, SHARD, WIDTH),
        zg=b(LINE + 1, SEG, 2 * HIDDEN),
        zd=b(LINE + 1, SIDE * PADDED, WIDTH),
        nq=b(ROWS_HERE, PATCHES, WIDTH),
        nb=b(ROWS_HERE, BYTES, WIDTH),
        qc=b(ROWS_HERE, PATCHES, MINE),
        kc=b(ROWS_HERE, BYTES, MINE),
        vc=b(ROWS_HERE, BYTES, MINE),
        oc=b(ROWS_HERE, PATCHES, MINE),
        x1=b(8, TOKENS, WIDTH),
        n1=b(ROWS_HERE, PATCHES, WIDTH),
        qkv=b(3, ROWS_HERE, PATCHES, MINE),
        o=b(ROWS_HERE, PATCHES, MINE),
        x2=b(8, TOKENS, WIDTH),
        n2=b(ROWS_HERE, PATCHES, WIDTH),
        fac=b(ROWS_HERE, PATCHES, 2 * HIDDEN),
        hid=b(ROWS_HERE, PATCHES, HIDDEN),
        dx2=b(8, TOKENS, WIDTH),
        dx1=b(8, TOKENS, WIDTH),
        dmix=b(ROWS_HERE, PATCHES, MINE),
        dqkv=b(ROWS_HERE, PATCHES, 3 * MINE),
        dqc=b(ROWS_HERE, PATCHES, MINE),
        dkvc=b(ROWS_HERE, BYTES, 2 * MINE),
        p=b(8, TOKENS, WIDTH),
        r1=b(ROWS_HERE, 2, TOKENS, WIDTH),
        q2=b(ROWS_HERE, TOKENS, WIDTH),
        r2=b(ROWS_HERE, TOKENS, WIDTH),
        bp=b(8, TOKENS_B, WIDTH),
        br1=b(ROWS_HERE, 2, TOKENS_B, WIDTH),
        br2=b(ROWS_HERE, TOKENS_B, WIDTH),
    )
    return plan


INS = ("patch_in", "byte", "cot_in", "sizes", "lengths", "attn_in", "wo_in", "gate_up_in", "down", "gains")
OUTS = ("out", "gpatch", "gbyte", "g_attn", "g_out", "g_gate", "g_down")


def step_kernel(names, *refs):
    m = SimpleNamespace(**dict(zip(INS + OUTS + tuple(names), refs)))
    dp, pipe = lax.axis_index("dp"), lax.axis_index("pipe")
    z, x, y, c = dp // SIDE, dp % SIDE, pipe // 2, pipe % 2
    at = lambda z, x, y, c: (z * SIDE + x, y * 2 + c)
    sibling, across, aside = at(z, x, y, 1 - c), at(z, x, 1 - y, c), at(z, 1 - x, y, c)
    right, left = at((z + 1) % LINE, x, y, c), at((z + LINE - 1) % LINE, x, y, c)
    corner = at(z, x, 1 - y, 1 - c)
    counter = [0]

    def take(count=1):
        first = counter[0]
        counter[0] += count
        assert counter[0] <= NSEM
        return first

    unfinished = []

    def remote(src, dst, device, send=None, recv=None):
        send = take() if send is None else send
        recv = take() if recv is None else recv
        return pltpu.make_async_remote_copy(
            src_ref=src, dst_ref=dst, send_sem=m.sem.at[send], recv_sem=m.sem.at[recv], device_id=device, device_id_type=MESH
        )

    def begin(copy):
        copy.start()
        unfinished.append(copy.wait_send)
        return copy

    def near(src, dst):
        copy = pltpu.make_async_copy(src, dst, m.sem.at[take()])
        copy.start()
        return copy

    local_out = near(m.wo_in, m.won.at[:, z, x])
    attn_here, gate_here, patch_here = near(m.attn_in, m.attn), near(m.gate_up_in, m.gate_up), near(m.patch_in, m.patch)
    bytes_in, cot_here = near(m.byte, m.bp), near(m.cot_in, m.cot)

    barrier = pltpu.get_barrier_semaphore()
    for device in (sibling, across, corner, aside):
        pl.semaphore_signal(barrier, inc=1, device_id=device, device_id_type=MESH)

    @pl.when(z < LINE - 1)
    def _():
        pl.semaphore_signal(barrier, inc=1, device_id=right, device_id_type=MESH)

    @pl.when(z > 0)
    def _():
        pl.semaphore_signal(barrier, inc=1, device_id=left, device_id_type=MESH)

    pl.semaphore_wait(barrier, 4 + (z < LINE - 1).astype(jnp.int32) + (z > 0).astype(jnp.int32))

    class Gather:
        def __init__(self, view):
            self.view = view
            self.sx, self.rx = take(LINE), take(LINE)
            self.sz, self.rz = take(LINE + 1), take(LINE)

        def copy(self, block, device, send, recv):
            there = self.view(block * SIDE + x)
            return remote(there, there, device, send, recv + block)

        def aside(self, block):
            return self.copy(block, aside, self.sx + block, self.rx)

        def right(self, block):
            return self.copy(block, right, self.sz + block, self.rz)

        def left(self, block):
            return self.copy(block, left, self.sz + jnp.where(block == z, LINE, block), self.rz)

        def start(self):
            self.aside(z).start()

            @pl.when(z < LINE - 1)
            def _():
                self.right(z).start()

            @pl.when(z > 0)
            def _():
                self.left(z).start()

        def hop(self, k):
            @pl.when(z - k >= 0)
            def _():
                self.right(z - k).wait_recv()
                self.aside(z - k).start()

                @pl.when(z < LINE - 1)
                def _():
                    self.right(z - k).start()

            @pl.when(z + k < LINE)
            def _():
                self.left(z + k).wait_recv()
                self.aside(z + k).start()

                @pl.when(z > 0)
                def _():
                    self.left(z + k).start()

        def ready(self):
            for block in range(LINE):
                self.aside(block).wait_recv()

        def finish(self):
            for block in range(LINE):
                self.aside(block).wait_send()

                @pl.when((z < LINE - 1) & (z >= block))
                def _():
                    self.right(block).wait_send()

                @pl.when((z > 0) & (z <= block))
                def _():
                    self.left(block).wait_send()

    class GatherPairs(Gather):
        def copy(self, block, device, send, recv):
            there = self.view(block * SIDE, SIDE)
            return remote(there, there, device, send, recv + block)

        def start(self):
            there = self.view(z * SIDE + x, 1)
            self.side = begin(remote(there, there, aside, self.sx, self.rx))

        def line(self):
            self.side.wait_recv()

            @pl.when(z < LINE - 1)
            def _():
                self.right(z).start()

            @pl.when(z > 0)
            def _():
                self.left(z).start()

        def hop(self, k):
            @pl.when(z - k >= 0)
            def _():
                self.right(z - k).wait_recv()

                @pl.when(z < LINE - 1)
                def _():
                    self.right(z - k).start()

            @pl.when(z + k < LINE)
            def _():
                self.left(z + k).wait_recv()

                @pl.when(z > 0)
                def _():
                    self.left(z + k).start()

        def ready(self):
            pass

        def finish(self):
            for block in range(LINE):

                @pl.when((z < LINE - 1) & (z >= block))
                def _():
                    self.right(block).wait_send()

                @pl.when((z > 0) & (z <= block))
                def _():
                    self.left(block).wait_send()

    g_out0 = Gather(lambda d: m.won.at[0, d // SIDE, d % SIDE])
    g_out1 = Gather(lambda d: m.won.at[1, d // SIDE, d % SIDE])
    g_attn0 = Gather(lambda d: m.wa.at[pl.ds(0, 3), pl.ds(d * SEG, SEG)])
    g_attn1 = Gather(lambda d: m.wa.at[pl.ds(3, 3), pl.ds(d * SEG, SEG)])
    g_gate = Gather(lambda d: m.wg.at[pl.ds(d * SEG, SEG)])
    g_down = GatherPairs(lambda d, count: m.wd.at[pl.ds(d * PADDED, count * PADDED)])

    def pieces(values, starts, width):
        return jnp.concatenate([values[:, first : first + width] for first in starts], axis=1)

    def spread(src, dst):
        copies = [near(src(pipe), dst)]
        for device in (across, corner, sibling):
            copies.append(begin_early(remote(src(device[1]), dst, device)))
        return copies

    early_sends = []

    def begin_early(copy):
        copy.start()
        early_sends.append(copy.wait_send)
        return copy

    def arrived(copies):
        copies[0].wait()
        for copy in copies[1:]:
            copy.wait_recv()

    def spread_attn(layer):
        for part in range(3 * layer, 3 * layer + 3):
            values = m.attn[part].astype(F32)
            for rank in range(RANKS):
                heads = [8 * (rank % 2) + 2 * j + rank // 2 for j in range(HEADS_MINE)]
                m.xa[part, rank, 0:SHARD, :] = pieces(values, [h * HEAD_DIM for h in heads], HEAD_DIM).astype(BF)
        three = pl.ds(3 * layer, 3)
        return spread(lambda q: m.xa.at[three, q, pl.ds(0, SHARD)], m.wa.at[three, pl.ds(dp * SEG + pipe * SHARD, SHARD)])

    def spread_gate():
        for which in range(2):
            values = m.gate_up[which].astype(F32)
            values = jnp.concatenate([values, jnp.zeros((SHARD, 128), F32)], axis=1)
            keep = (lax.broadcasted_iota(jnp.int32, (SHARD, HIDDEN), 1) % PADDED) < UNITS
            for rank in range(RANKS):
                starts = [UNITS * (RANKS * d + rank) for d in range(GROUPS)]
                runs = jnp.where(keep, pieces(values, starts, PADDED), 0.0)
                m.xg[rank, 0:SHARD, which * HIDDEN : (which + 1) * HIDDEN] = runs.astype(BF)
        return spread(lambda q: m.xg.at[q, pl.ds(0, SHARD)], m.wg.at[pl.ds(dp * SEG + pipe * SHARD, SHARD)])

    def begin_after(copies, gather):
        arrived(copies)
        gather.start()

    queue = []

    def pump(count):
        for _ in range(min(count, len(queue))):
            queue.pop(0)()

    def swap_out(layer):
        mine, there = m.won.at[layer, pl.ds(2 * c, 2)], m.woh.at[layer, :, :, pl.ds(c * SHARD, SHARD)]
        keep = near(mine, there)
        give = remote(m.won.at[layer, pl.ds(2 * (1 - c), 2)], there, sibling)
        give.start()
        return keep, give

    def swapped(swap):
        swap[0].wait()
        swap[1].wait_recv()

    lane = lax.broadcasted_iota(jnp.int32, (1, MINE), 1) // HEAD_DIM
    head_mask = [(lane == j).astype(F32).astype(BF) for j in range(HEADS_MINE)]
    scaled_mask = [((lane == j).astype(F32) * SCALE).astype(BF) for j in range(HEADS_MINE)]

    def gain(index):
        return m.gains[index : index + 1, :]

    def factor_of(values):
        return lax.rsqrt(jnp.mean(values * values, axis=-1, keepdims=True) + EPSILON)

    def normed(values, index):
        values = values.astype(F32)
        return (values * factor_of(values) * gain(index)).astype(BF)

    def norm_back(values, gradient, index):
        values = values.astype(F32)
        factor = factor_of(values)
        weighted = gradient * gain(index)
        return factor * weighted - values * (factor * factor * factor) * jnp.mean(weighted * values, axis=-1, keepdims=True)

    def normed_rows(src, dst, index, r):
        for part in range(RANKS):
            for half in range(2):
                rows = pl.ds(half * (TOKENS // 2), TOKENS // 2)
                dst[r, pl.ds(part * TOKENS + half * (TOKENS // 2), TOKENS // 2)] = normed(src[4 * r + part, rows], index)

    class Reduce:
        def __init__(self, p, r1, q2, r2, tokens, sems):
            self.p, self.r1, self.q2, self.r2, self.tokens, self.sems = p, r1, q2, r2, tokens, sems
            self.first, self.second = {}, {}

        def give(self, r):
            self.first[r] = [
                remote(self.p.at[4 * r + 2 * side + 1 - c], self.r1.at[r, side], sibling, *pair_at(self.sems, 2 * r + side))
                for side in range(2)
            ]
            for copy in self.first[r]:
                copy.start()

        def cross(self, r):
            for copy in self.first[r]:
                copy.wait_recv()
            other = 4 * r + 2 * (1 - y) + c
            self.q2[r] = (self.p[other].astype(F32) + self.r1[r, 1 - y].astype(F32)).astype(BF)
            self.second[r] = remote(self.q2.at[r], self.r2.at[r], across, *pair_at(self.sems, 4 + r))
            self.second[r].start()

        def arrive(self, r):
            self.second[r].wait_recv()

        def free(self):
            for r in range(ROWS_HERE):
                for copy in self.first[r]:
                    copy.wait_send()
                self.second[r].wait_send()

        def total(self, r, rows):
            own = 4 * r + pipe
            return (
                self.p[own, rows].astype(F32) + self.r1[r, y, rows].astype(F32) + self.r2[r, rows].astype(F32)
            )

    class Share:
        def __init__(self, values, sems):
            self.values, self.sems, self.copies, self.last = values, sems, {}, {}

        def give(self, r):
            there = self.values.at[4 * r + pipe]
            self.copies[r] = [
                remote(there, there, device, *pair_at(self.sems, 3 * r + k)) for k, device in enumerate((across, sibling))
            ]
            for copy in self.copies[r]:
                copy.start()

        def relay(self, r):
            self.copies[r][0].wait_recv()
            there = self.values.at[4 * r + 2 * (1 - y) + c]
            self.last[r] = remote(there, there, sibling, *pair_at(self.sems, 3 * r + 2))
            self.last[r].start()

        def ready(self, r):
            self.copies[r][1].wait_recv()
            self.last[r].wait_recv()

        def free(self):
            for r in range(ROWS_HERE):
                for copy in self.copies[r] + [self.last[r]]:
                    copy.wait_send()

    def pair_at(first, index):
        return first + 2 * index, first + 2 * index + 1

    sums_a, sums_b, shares = take(12), take(12), take(12)

    halves = [pl.ds(h * (TOKENS // 2), TOKENS // 2) for h in range(2)]

    def to_owner(reduce, left_of, r):
        for n in range(4):
            cols = pl.ds(n * 256, 256)
            reduce.p[4 * r : 4 * r + 4, :, cols] = left_of(r, n).astype(BF).reshape(4, reduce.tokens, 256)
        reduce.give(r)

    local_out.wait()
    g_out0.start()
    g_out1.start()
    m.wd[pl.ds(pl.multiple_of(dp * PADDED, 32), PADDED), :] = jnp.concatenate(
        [m.down[...], jnp.zeros((PADDED - UNITS, WIDTH), BF)], axis=0
    )
    g_down.start()
    attn_here.wait()
    exchange0 = spread_attn(0)
    exchange1 = spread_attn(1)
    gate_here.wait()
    exchange2 = spread_gate()
    begin_after(exchange0, g_attn0)
    patch_here.wait()

    @pl.loop(0, ROWS_HERE * PATCHES // 32)
    def _(i):
        rows = pl.ds((i % 8) * 32, 32)
        m.nq[i // 8, rows] = normed(m.patch[i // 8, rows], 0)

    bytes_in.wait()
    cot_here.wait()

    @pl.loop(0, 8)
    def _(i):
        for part in range(5):
            rows = pl.ds(part * 32, 32)
            m.nb[i // 4, pl.ds((i % 4) * TOKENS_B + part * 32, 32)] = normed(m.bp[i, rows], 1)

    def hops(gather):
        return [functools.partial(gather.hop, k) for k in (1, 2, 3)]

    h_out0, h_attn0, h_out1, h_attn1, h_gate, h_down = map(hops, (g_out0, g_attn0, g_out1, g_attn1, g_gate, g_down))
    queue += [h_out0[0], h_out1[0], h_attn0[0], h_out0[1], h_out1[1], h_attn0[1], h_out0[2], h_out1[2]]
    queue += [lambda: begin_after(exchange1, g_attn1), h_attn0[2]]
    queue += [h_attn1[0], lambda: begin_after(exchange2, g_gate), h_attn1[1], h_attn1[2]]
    pump(len(queue))
    queue += [lambda: [wait() for wait in early_sends]] + h_gate[:2] + [g_down.line, h_gate[2]] + h_down
    g_out0.ready()
    swap0 = swap_out(0)
    g_attn0.ready()

    for r in range(ROWS_HERE):
        m.qc[r] = product(m.nq[r], m.wa[0]).astype(BF)

    @pl.loop(0, 4)
    def _(i):
        rows = pl.ds((i % 2) * (BYTES // 2), BYTES // 2)
        block = m.nb[i // 2, rows]
        m.kc[i // 2, rows] = product(block, m.wa[1]).astype(BF)
        m.vc[i // 2, rows] = product(block, m.wa[2]).astype(BF)

    def window(r):
        sizes = m.sizes[pl.ds(r, 1), :].astype(F32)
        i = lax.broadcasted_iota(jnp.int32, (PATCHES, PATCHES), 0)
        j = lax.broadcasted_iota(jnp.int32, (PATCHES, PATCHES), 1)
        first = jnp.sum(jnp.where(j < i, sizes, 0.0), axis=1, keepdims=True)
        last = jnp.sum(jnp.where(j <= i, sizes, 0.0), axis=1, keepdims=True)
        position = lax.broadcasted_iota(jnp.int32, (PATCHES, BYTES), 1).astype(F32)
        return (position >= first) & (position < last)

    def causal(r):
        length = m.lengths[r]
        i = lax.broadcasted_iota(jnp.int32, (PATCHES, PATCHES), 0)
        j = lax.broadcasted_iota(jnp.int32, (PATCHES, PATCHES), 1)
        return (j <= i) & (j < length)

    def weights_of(query, keys, allowed):
        scores = jnp.where(allowed, product_right(query, keys), NEGATIVE)
        raised = jnp.exp(scores - jnp.max(scores, axis=-1, keepdims=True))
        return raised * (1.0 / jnp.sum(raised, axis=-1, keepdims=True))

    def attend(r, allowed, queries, keys, values, mixed):
        total = None
        for j in range(HEADS_MINE):
            low = weights_of(queries[r] * scaled_mask[j], keys[r], allowed).astype(BF)
            term = product(low, values[r] * head_mask[j])
            total = term if total is None else total + term
        mixed[r] = total.astype(BF)

    def attend_back(r, allowed, queries, keys, values, grad):
        sums = [None, None, None]
        for j in range(HEADS_MINE):
            query, mixed = queries[r] * scaled_mask[j], grad[r] * head_mask[j]
            weights = weights_of(query, keys[r], allowed)
            grad_weights = product_right(mixed, values[r])
            grad_scores = weights * (grad_weights - jnp.sum(weights * grad_weights, axis=-1, keepdims=True))
            grad_scores = grad_scores.astype(BF)
            terms = (
                product(grad_scores, keys[r] * head_mask[j]),
                product_left(grad_scores, query),
                product_left(weights.astype(BF), mixed),
            )
            sums = [t if s is None else s + t for s, t in zip(sums, terms)]
        return (sums[0] * SCALE).astype(BF), sums[1].astype(BF), sums[2].astype(BF)

    def out_rows(layer):
        return lambda n: m.woh[layer, :, :, :, pl.ds(n * 256, 256)].reshape(MINE, 256)

    def residual(reduce, share, base, result, r):
        reduce.arrive(r)
        for rows in halves:
            result[4 * r + pipe, rows] = (base(r, rows) + reduce.total(r, rows)).astype(BF)
        share.give(r)

    first_sum, first_share = Reduce(m.p, m.r1, m.q2, m.r2, TOKENS, sums_a), Share(m.x1, shares)
    attend(0, window(0), m.qc, m.kc, m.vc, m.oc)
    swapped(swap0)
    to_owner(first_sum, lambda r, n: product(m.oc[r], out_rows(0)(n)), 0)
    attend(1, window(1), m.qc, m.kc, m.vc, m.oc)
    first_sum.cross(0)
    to_owner(first_sum, lambda r, n: product(m.oc[r], out_rows(0)(n)), 1)
    pump(2)
    first_sum.cross(1)
    pump(2)
    own_patch = lambda r, rows: m.patch[r, pl.ds(pipe * TOKENS + rows.start, TOKENS // 2)].astype(F32)
    for r in range(ROWS_HERE):
        residual(first_sum, first_share, own_patch, m.x1, r)
    first_share.relay(0)
    g_out1.ready()
    swap1 = swap_out(1)
    g_attn1.ready()
    queries, keys, values = m.qkv.at[0], m.qkv.at[1], m.qkv.at[2]

    def project(r):
        first_share.ready(r)
        normed_rows(m.x1, m.n1, 2, r)
        for part in range(3):
            m.qkv[part, r] = product(m.n1[r], m.wa[3 + part]).astype(BF)

    project(0)
    attend(0, causal(0), queries, keys, values, m.o)
    first_sum.free()
    second_sum, second_share = Reduce(m.p, m.r1, m.q2, m.r2, TOKENS, sums_a), Share(m.x2, shares)
    swapped(swap1)
    to_owner(second_sum, lambda r, n: product(m.o[r], out_rows(1)(n)), 0)
    first_share.relay(1)
    project(1)
    first_share.free()
    attend(1, causal(1), queries, keys, values, m.o)
    second_sum.cross(0)
    to_owner(second_sum, lambda r, n: product(m.o[r], out_rows(1)(n)), 1)
    pump(1)
    second_sum.cross(1)
    pump(1)
    own_of = lambda values: lambda r, rows: values[4 * r + pipe, rows].astype(F32)
    for r in range(ROWS_HERE):
        residual(second_sum, second_share, own_of(m.x1), m.x2, r)
    for r in range(ROWS_HERE):
        second_share.relay(r)
    for r in range(ROWS_HERE):
        second_share.ready(r)
        normed_rows(m.x2, m.n2, 3, r)

    pump(len(queue) - 1)
    g_gate.ready()
    tiles = HIDDEN // 256
    for r in range(ROWS_HERE):
        for n in range(tiles):
            first, later = pl.ds(n * 256, 256), pl.ds(HIDDEN + n * 256, 256)
            gate = product(m.n2[r], m.wg[:, first])
            up = product(m.n2[r], m.wg[:, later])
            sig = jax.nn.sigmoid(gate)
            silu = gate * sig
            m.hid[r, :, first] = (silu * up).astype(BF)
            m.fac[r, :, first] = (up * sig * (1.0 + gate * (1.0 - sig))).astype(BF)
            m.fac[r, :, later] = silu.astype(BF)

    class Scatter:
        def __init__(self, mine, xbuf, zbuf):
            self.mine, self.xbuf, self.zbuf = mine, xbuf, zbuf
            self.sx, self.rx = take(LINE), take(LINE)
            self.sz, self.rz = take(LINE), take(LINE + 1)

        def aside(self, block):
            return remote(self.mine(block * SIDE + 1 - x), self.xbuf(block), aside, self.sx + block, self.rx + block)

        def start(self):
            for block in (3, 0, 2, 1):
                self.aside(block).start()

        def add(self, into, values):
            into[...] = (into[...].astype(F32) + values[...].astype(F32)).astype(BF)

        def line(self, block):
            return self.mine(block * SIDE + x)

        def right(self, block):
            return remote(self.line(block), self.zbuf(block), right, self.sz + block, self.rz + block)

        def left(self, block, slot):
            return remote(self.line(block), self.zbuf(slot), left, self.sz + block, self.rz + slot)

        def send_left(self, block):
            self.left(block, jnp.where(z - 1 == block, LINE, block)).start()

        def emit(self, rightward, leftward):
            @pl.when(z == 0)
            def _():
                for block in rightward:
                    self.right(block).start()

            @pl.when(z == LINE - 1)
            def _():
                for block in leftward:
                    self.send_left(block)

        def take(self, block):
            self.aside(block).wait_recv()
            self.add(self.line(block), self.xbuf(block))
            self.emit(*{3: ((3,), ()), 0: ((), (0,)), 2: ((2,), ()), 1: ((1,), (1, 2))}[block])

        def tick(self, t):
            @pl.when((z >= 1) & (z <= t))
            def _():
                block = LINE - 1 - t + z
                self.right(block).wait_recv()
                self.add(self.line(block), self.zbuf(block))

                @pl.when(z < block)
                def _():
                    self.right(block).start()

            @pl.when((z < LINE - 1) & (z >= LINE - 1 - t))
            def _():
                block = t - (LINE - 1) + z
                slot = jnp.where(z == block, LINE, block)
                self.left(block, slot).wait_recv()
                self.add(self.line(block), self.zbuf(slot))

                @pl.when(z > block)
                def _():
                    self.send_left(block)

        def finish(self):
            for block in range(LINE):
                self.aside(block).wait_send()
            self.finish_line()

        def finish_line(self):
            for block in range(LINE):

                @pl.when(z < block)
                def _():
                    self.right(block).wait_send()

                @pl.when(z > block)
                def _():
                    self.left(block, 0).wait_send()

    class ScatterPairs(Scatter):
        def line(self, block):
            return self.mine(block * SIDE, SIDE)

        def start(self):
            self.emit((3, 2, 1), (0, 1, 2))

        def cross(self):
            self.side = begin(remote(self.mine(z * SIDE + 1 - x, 1), self.xbuf, aside, self.sx, self.rx))

        def last(self):
            self.side.wait_recv()
            self.add(self.mine(z * SIDE + x, 1), self.xbuf)

    pump(1)

    s_down = ScatterPairs(lambda d, count: m.dd.at[pl.ds(d * PADDED, count * PADDED)], m.xd, lambda b: m.zd.at[b])
    s_gate = Scatter(lambda d: m.dg.at[pl.ds(d * SEG, SEG)], lambda b: m.xg.at[b], lambda b: m.zg.at[b])

    def hidden_back(r):
        for n in range(tiles):
            first, later = pl.ds(n * 256, 256), pl.ds(HIDDEN + n * 256, 256)
            grad = product_right(m.cot[r], m.wd[first, :]).astype(BF).astype(F32)
            m.fac[r, :, first] = (grad * m.fac[r, :, first].astype(F32)).astype(BF)
            m.fac[r, :, later] = (grad * m.fac[r, :, later].astype(F32)).astype(BF)

    def gate_grad(block):
        rows = pl.ds(block * 256, 256)
        total = product_left(m.n2[0, :, rows], m.fac[0]) + product_left(m.n2[1, :, rows], m.fac[1])
        m.dg[rows, :] = total.astype(BF)
        s_gate.aside(block).start()

    second_sum.free()
    second_share.free()
    third_sum, third_share = Reduce(m.p, m.r1, m.q2, m.r2, TOKENS, sums_a), Share(m.dx2, shares)
    for r in range(ROWS_HERE):
        hidden_back(r)
        to_owner(third_sum, lambda r, n: product_right(m.fac[r], m.wg[n * 256 : n * 256 + 256, :]), r)
    third_sum.cross(0)
    gate_grad(3)
    third_sum.cross(1)
    gate_grad(0)

    @pl.loop(0, tiles)
    def _(n):
        cols = pl.ds(pl.multiple_of(n * 256, 256), 256)
        for half in range(2):
            wide = pl.ds(half * 512, 512)
            total = product_left(m.hid[0, :, cols], m.cot[0, :, wide]) + product_left(m.hid[1, :, cols], m.cot[1, :, wide])
            m.dd[cols, wide] = total.astype(BF)

    s_down.start()
    gate_grad(2)
    gate_grad(1)

    def gradient_in(reduce, share, base, values, index, result, r):
        reduce.arrive(r)
        for rows in halves:
            back = norm_back(values(r, rows), reduce.total(r, rows), index)
            result(r, rows, (base(r, rows) + back).astype(BF))
        if share is not None:
            share.give(r)

    def into(ref):
        def store(r, rows, value):
            ref[4 * r + pipe, rows] = value

        return store

    own_cot = lambda r, rows: m.cot[r, pl.ds(pipe * TOKENS + rows.start, TOKENS // 2)].astype(F32)
    for r in range(ROWS_HERE):
        gradient_in(third_sum, third_share, own_cot, own_of(m.x2), 3, into(m.dx2), r)

    early = pl.ds(0, TOKENS)
    out_sum = Reduce(m.bp.at[:, early], m.br1.at[:, :, early], m.n2.at[:, early], m.br2.at[:, early], TOKENS, sums_b)
    for r in range(ROWS_HERE):
        to_owner(out_sum, lambda r, n: product(m.hid[r], m.wd[:, n * 256 : n * 256 + 256]), r)
    third_share.relay(0)
    for r in range(ROWS_HERE):
        out_sum.cross(r)
    third_share.relay(1)

    def rows_of(ref, r):
        return ref[4 * r : 4 * r + 4].reshape(PATCHES, WIDTH)

    def mixed_back(share, grads, layer, r):
        share.ready(r)
        m.dmix[r] = product_right(rows_of(grads, r), m.woh[layer].reshape(MINE, WIDTH)).astype(BF)

    def attn_back(left, n, first, count):
        total = None
        for part in range(count):
            term = product_right(left[:, part * MINE : part * MINE + MINE], m.wa[first + part, pl.ds(n * 256, 256), :])
            total = term if total is None else total + term
        return total

    def global_back(r):
        mixed_back(third_share, m.dx2, 1, r)
        dq, dk, dv = attend_back(r, causal(r), queries, keys, values, m.dmix)
        m.dqkv[r, :, 0:MINE] = dq
        m.dqkv[r, :, MINE : 2 * MINE] = dk
        m.dqkv[r, :, 2 * MINE : 3 * MINE] = dv

    s_down.tick(1)
    global_back(0)
    third_sum.free()
    fourth_sum, fourth_share = Reduce(m.p, m.r1, m.q2, m.r2, TOKENS, sums_a), Share(m.dx1, shares)
    to_owner(fourth_sum, lambda r, n: attn_back(m.dqkv.at[r], n, 3, 3), 0)
    global_back(1)
    third_share.free()
    fourth_sum.cross(0)
    to_owner(fourth_sum, lambda r, n: attn_back(m.dqkv.at[r], n, 3, 3), 1)

    def own_half(layer, which):
        return m.won.at[layer, :, which]

    def out_grad(layer, mixed, grads):
        (g_out0, g_out1)[layer].finish()
        (swap0, swap1)[layer][1].wait_send()
        total = None
        for r in range(ROWS_HERE):
            term = product_left(mixed[r], rows_of(grads, r))
            total = term if total is None else total + term
        m.won[layer] = total.astype(BF).reshape(LINE, SIDE, SHARD, WIDTH)
        there = m.don.at[layer, pl.ds(HEADS_MINE * c, HEADS_MINE)]
        keep = near(own_half(layer, c), there)
        give = remote(own_half(layer, 1 - c), there, sibling)
        begin(give)
        return keep, give

    def attn_grad(first, count, left, right):
        @pl.loop(0, 4)
        def _(n):
            cols = pl.ds(pl.multiple_of(n * 256, 256), 256)
            total = product_left(left[0, :, cols], right[0]) + product_left(left[1, :, cols], right[1])
            for part in range(count):
                m.da[first + part, cols, :] = total[:, part * MINE : part * MINE + MINE].astype(BF)

    def scatter_out(layer):
        return Scatter(lambda d: m.don.at[layer, d], lambda b: m.xo.at[layer, b], lambda b: m.zo.at[layer, b])

    def scatter_attn(first, count):
        part = pl.ds(first, count)
        return Scatter(lambda d: m.da.at[part, pl.ds(d * SEG, SEG)], lambda b: m.xa.at[part, b], lambda b: m.za.at[part, b])

    swap2 = out_grad(1, m.o, m.dx2)
    fourth_sum.cross(1)
    attn_grad(3, 3, m.n1, m.dqkv)
    s_out1, s_attn1 = scatter_out(1), scatter_attn(3, 3)
    swapped(swap2)
    s_out1.start()
    s_attn1.start()
    s_gate.take(3)
    s_gate.take(0)
    s_down.tick(2)
    for r in range(ROWS_HERE):
        out_sum.arrive(r)
        for rows in halves:
            m.out[r, rows] = (own_of(m.x2)(r, rows) + out_sum.total(r, rows)).astype(BF)
    for r in range(ROWS_HERE):
        gradient_in(fourth_sum, fourth_share, own_of(m.dx2), own_of(m.x1), 2, into(m.dx1), r)
    s_gate.take(2)
    fourth_share.relay(0)

    out_sum.free()
    fourth_sum.free()
    byte_sum = Reduce(m.bp, m.br1, m.n2.at[:, pl.ds(0, TOKENS_B)], m.br2, TOKENS_B, sums_b)
    fifth_sum = Reduce(m.p, m.r1, m.q2, m.r2, TOKENS, sums_a)

    def cross_back(r):
        mixed_back(fourth_share, m.dx1, 0, r)
        dq, dk, dv = attend_back(r, window(r), m.qc, m.kc, m.vc, m.dmix)
        m.dqc[r] = dq
        m.dkvc[r, :, 0:MINE] = dk
        m.dkvc[r, :, MINE : 2 * MINE] = dv
        to_owner(byte_sum, lambda r, n: attn_back(m.dkvc.at[r], n, 1, 2), r)
        to_owner(fifth_sum, lambda r, n: attn_back(m.dqc.at[r], n, 0, 1), r)

    cross_back(0)
    fourth_share.relay(1)
    s_down.tick(3)
    s_down.cross()
    s_gate.take(1)
    byte_sum.cross(0)
    fifth_sum.cross(0)
    cross_back(1)
    s_gate.tick(1)
    attn_grad(1, 2, m.nb, m.dkvc)
    s_attn0b = scatter_attn(1, 2)
    s_attn0b.start()
    byte_sum.cross(1)
    fifth_sum.cross(1)
    attn_grad(0, 1, m.nq, m.dqc)
    s_attn0a = scatter_attn(0, 1)
    s_attn0a.start()
    swap3 = out_grad(0, m.oc, m.dx1)

    own_bytes = [near(m.byte.at[4 * r + pipe], m.gbyte.at[r]) for r in range(ROWS_HERE)]
    s_out0 = scatter_out(0)
    swapped(swap3)
    s_out0.start()
    def back_to_pipe(rows_ref, dst):
        copies = [near(rows_ref(pipe), dst)]
        for device in (across, corner, sibling):
            copies.append(begin(remote(rows_ref(device[1]), dst, device)))
        return copies

    def attn_home(first, count):
        src = lambda q: m.da.at[pl.ds(first, count), pl.ds(dp * SEG + q * SHARD, SHARD)]
        return back_to_pipe(src, m.g_attn.at[pipe, pl.ds(first, count)])

    def gate_home():
        src = lambda q: m.dg.at[pl.ds(dp * SEG + q * SHARD, SHARD)]
        return back_to_pipe(src, m.g_gate.at[pipe])

    for block in (3, 0, 2, 1):
        s_out1.take(block)
    s_gate.tick(2)
    s_attn1.take(3)
    s_out1.tick(1)
    s_attn1.take(0)
    s_out1.tick(2)
    s_gate.tick(3)
    home = [gate_home()]
    s_attn1.take(2)
    s_attn1.tick(1)
    s_out1.tick(3)
    for r in range(ROWS_HERE):
        gradient_in(
            fifth_sum,
            None,
            own_of(m.dx1),
            own_patch,
            0,
            lambda r, rows, value: m.gpatch.__setitem__((r, rows), value),
            r,
        )
    s_attn1.take(1)
    s_attn1.tick(2)
    s_attn0b.take(3)
    s_attn0b.take(0)
    s_attn1.tick(3)
    home.append(attn_home(3, 3))
    s_attn0b.take(2)
    s_attn0b.tick(1)
    s_attn0b.take(1)
    s_attn0b.tick(2)
    for block in (3, 0, 2, 1):
        s_attn0a.take(block)
    s_attn0b.tick(3)
    home.append(attn_home(1, 2))
    s_attn0a.tick(1)
    for block in (3, 0, 2, 1):
        s_out0.take(block)
    s_attn0a.tick(2)
    s_out0.tick(1)
    s_attn0a.tick(3)
    home.append(attn_home(0, 1))
    s_down.last()
    s_out0.tick(2)
    for copy in own_bytes:
        copy.wait()
    for r in range(ROWS_HERE):
        byte_sum.arrive(r)
        for part in range(5):
            rows = pl.ds(part * 32, 32)
            back = norm_back(m.gbyte[r, rows], byte_sum.total(r, rows), 1)
            m.gbyte[r, rows] = back.astype(BF)
    s_out0.tick(3)
    m.g_down[...] = m.dd[pl.ds(pl.multiple_of(dp * PADDED, 32), PADDED), :]
    for layer in range(2):
        m.g_out[layer] = m.don[layer, dp]
    for copies in home:
        arrived(copies)
    for gather in (g_attn0, g_attn1, g_gate, g_down):
        gather.finish()
    s_down.finish_line()
    for scatter in (s_gate, s_attn1, s_out1, s_attn0a, s_attn0b, s_out0):
        scatter.finish()
    byte_sum.free()
    fifth_sum.free()
    fourth_share.free()
    for wait in unfinished:
        wait()


def finish_kernel(out, gpatch, gbyte, attn, gate_up, gains, da, do, dg, dd, out_, gpatch_, gbyte_, g_attn, g_out, g_gate, g_down, g_gain):
    for src, dst in ((out, out_), (gpatch, gpatch_), (gbyte, gbyte_)):
        dst[...] = src[...]
    place = lax.axis_index("dp") * RANKS + lax.axis_index("pipe")
    for part in range(6):
        got = [da[rank, part].astype(F32) for rank in range(RANKS)]
        heads = []
        for head in range(HEADS):
            rank, j = 2 * (head % 2) + head // 8, (head % 8) // 2
            heads.append(got[rank][:, j * HEAD_DIM : (j + 1) * HEAD_DIM])
        g_attn[part] = jnp.concatenate(heads, axis=1)
    for which in range(2):
        got = [dg[rank, :, which * HIDDEN : (which + 1) * HIDDEN].astype(F32) for rank in range(RANKS)]
        runs = [got[rank][:, PADDED * d : PADDED * d + UNITS] for d in range(GROUPS) for rank in range(RANKS)]
        g_gate[which] = jnp.concatenate(runs, axis=1)
    g_out[...] = do[...].astype(F32)
    g_down[...] = dd[0:UNITS].astype(F32)

    column = lax.broadcasted_iota(jnp.int32, (SHARD, WIDTH), 1)
    own = column == lax.broadcasted_iota(jnp.int32, (SHARD, WIDTH), 0) + place * SHARD

    def gain_gradient(row, parts):
        total = None
        for weight, grad in parts:
            term = jnp.sum(weight.astype(F32) * grad, axis=1, keepdims=True)
            total = term if total is None else total + term
        total = total / jnp.sum(jnp.where(own, gains[row : row + 1, :], 0.0), axis=1, keepdims=True)
        g_gain[row : row + 1, :] = jnp.transpose(jnp.broadcast_to(total, (SHARD, 128)))[0:1, :]

    gain_gradient(0, [(attn[0], g_attn[0])])
    gain_gradient(1, [(attn[i], g_attn[i]) for i in (1, 2)])
    gain_gradient(2, [(attn[i], g_attn[i]) for i in (3, 4, 5)])
    gain_gradient(3, [(gate_up[i], g_gate[i]) for i in range(2)])

def fused_step(patch_states, byte_states, cotangent, patch_lengths, row_lengths, attn_weights, out_weights, gate_up, down_weight, gains):
    plan = scratch_plan()
    vmem, anywhere = pl.BlockSpec(memory_space=pltpu.VMEM), pl.BlockSpec(memory_space=pl.ANY)
    shape = jax.ShapeDtypeStruct
    results = pl.pallas_call(
        functools.partial(step_kernel, tuple(plan)),
        out_shape=(
            shape((ROWS_HERE, TOKENS, WIDTH), BF),
            shape((ROWS_HERE, TOKENS, WIDTH), BF),
            shape((ROWS_HERE, TOKENS_B, WIDTH), BF),
            shape((RANKS, 6, SHARD, MINE), BF),
            shape((2, SHARD, WIDTH), BF),
            shape((RANKS, SHARD, 2 * HIDDEN), BF),
            shape((PADDED, WIDTH), BF),
        ),
        in_specs=[anywhere] * 3 + [vmem, pl.BlockSpec(memory_space=pltpu.SMEM)] + [anywhere] * 3 + [vmem] * 2,
        out_specs=[vmem] * 7,
        scratch_shapes=list(plan.values()),
        compiler_params=pltpu.CompilerParams(collective_id=0, has_side_effects=True, vmem_limit_bytes=63 * 2**20),
    )(
        patch_states,
        byte_states.reshape(8, TOKENS_B, WIDTH),
        cotangent,
        patch_lengths,
        row_lengths,
        attn_weights.reshape(6, SHARD, WIDTH),
        out_weights,
        gate_up,
        down_weight,
        gains,
    )
    finished = pl.pallas_call(
        finish_kernel,
        out_shape=(
            *(shape(array.shape, array.dtype) for array in results[:3]),
            shape((6, SHARD, WIDTH), F32),
            shape(out_weights.shape, F32),
            shape(gate_up.shape, F32),
            shape(down_weight.shape, F32),
            shape((4, SHARD), F32),
        ),
        in_specs=[vmem] * 10,
        out_specs=[vmem] * 8,
        compiler_params=pltpu.CompilerParams(vmem_limit_bytes=63 * 2**20),
    )(*results[:3], attn_weights.reshape(6, SHARD, WIDTH), gate_up, gains, *results[3:])
    return (*finished[:3], finished[3].reshape(attn_weights.shape), *finished[4:])


def solution(mesh):
    placed = (
        P("dp", None, None),
        P("dp", None, None),
        P("dp", None, None),
        P("dp", None),
        P("dp"),
        P(None, None, ("dp", "pipe"), None),
        P(None, ("dp", "pipe"), None),
        P(None, ("dp", "pipe"), None),
        P(("dp", "pipe"), None),
        P(),
    )
    return jax.shard_map(
        fused_step if mesh.shape["dp"] == GROUPS else gathered_step,
        mesh=mesh,
        in_specs=placed,
        out_specs=(
            P("dp", "pipe", None),
            P("dp", "pipe", None),
            P("dp", "pipe", None),
            P(None, None, ("dp", "pipe"), None),
            P(None, ("dp", "pipe"), None),
            P(None, ("dp", "pipe"), None),
            P(("dp", "pipe"), None),
            P(None, ("dp", "pipe")),
        ),
        check_vma=False,
    )
```

```python
import functools
from types import SimpleNamespace

import jax
import jax.numpy as jnp
from jax import lax
from jax.experimental import pallas as pl
from jax.experimental.pallas import tpu as pltpu
from jax.sharding import PartitionSpec as P

HEADS = 16
HEAD_DIM = 64
EPSILON = 1e-06
NEGATIVE = -1e30
SCALE = HEAD_DIM ** (-0.5)
BF = jnp.bfloat16
F32 = jnp.float32
MESH = pl.DeviceIdType.MESH


def dot(left, right, contract):
    return lax.dot_general(left, right, (contract, ((), ())), preferred_element_type=F32)


def product(left, right):
    return dot(left, right, ((1,), (0,)))


def product_left(left, right):
    return dot(left, right, ((0,), (0,)))


def product_right(left, right):
    return dot(left, right, ((1,), (1,)))


def norm_rows(values, gain):
    factor = lax.rsqrt(jnp.mean(values * values, axis=-1, keepdims=True) + EPSILON)
    return (values * factor * gain).astype(BF), factor


def norm_back(values, factor, gain, gradient):
    weighted = gradient * gain
    grad_gain = jnp.sum(gradient * values * factor, axis=0)
    grad_values = factor * weighted - values * factor**3 * jnp.mean(weighted * values, axis=-1, keepdims=True)
    return grad_values, grad_gain


def heads_of(values):
    return values.reshape(values.shape[0], HEADS, HEAD_DIM).transpose(1, 0, 2)


def rows_of(values):
    return values.transpose(1, 0, 2).reshape(values.shape[1], -1).astype(BF)


def batched(left, right, left_dim, right_dim):
    return lax.dot_general(left, right, (((left_dim,), (right_dim,)), ((0,), (0,))), preferred_element_type=F32)


def attend(queries, keys, values, allowed):
    scores = batched(queries, keys, 2, 2) * SCALE
    weights = jax.nn.softmax(jnp.where(allowed[None], scores, NEGATIVE), axis=-1)
    low = weights.astype(BF)
    return weights, low, rows_of(batched(low, values, 2, 1))


def attend_back(queries, keys, values, weights, low, grad_mixed):
    grad_weights = batched(grad_mixed, values, 2, 2)
    grad_scores = weights * (grad_weights - jnp.sum(weights * grad_weights, axis=-1, keepdims=True))
    grad_scores = grad_scores.astype(BF)
    return (
        rows_of(batched(grad_scores, keys, 2, 1) * SCALE),
        rows_of(batched(grad_scores, queries, 1, 1) * SCALE),
        rows_of(batched(low, grad_mixed, 1, 1)),
    )


def gathered_step(patch_states, byte_states, cotangent, patch_lengths, row_lengths, attn_weights, out_weights, gate_up, down_weight, gains):
    everyone = ("dp", "pipe")
    micro = patch_states.shape[0]
    stages = lax.axis_size("pipe")
    share = stages // micro
    place = lax.axis_index("pipe")
    row, part = place // share, place % share
    attn = lax.all_gather(attn_weights, everyone, axis=2, tiled=True)
    outw = lax.all_gather(out_weights, everyone, axis=1, tiled=True)
    gate_stack = lax.all_gather(gate_up, everyone, axis=1, tiled=True)
    down = lax.all_gather(down_weight, everyone, axis=0, tiled=True)

    def mine(source):
        return lax.dynamic_index_in_dim(source, row, 0, keepdims=False)

    def half(values):
        count = values.shape[0] // share
        return lax.dynamic_slice_in_dim(values, part * count, count, 0)

    def weight_grad(left, right):
        return product_left(half(left), half(right)).astype(BF)

    patch = mine(patch_states).astype(F32)
    byte = mine(byte_states).astype(F32)
    cot = mine(cotangent)
    sizes = mine(patch_lengths)
    length = mine(row_lengths)
    patches, bytes_ = patch.shape[0], byte.shape[0]

    nq, fq = norm_rows(patch, gains[0])
    nb, fb = norm_rows(byte, gains[1])
    qc = heads_of(product(nq, attn[0, 0]).astype(BF))
    kc = heads_of(product(nb, attn[0, 1]).astype(BF))
    vc = heads_of(product(nb, attn[0, 2]).astype(BF))
    ends = jnp.cumsum(sizes)[:, None]
    position = jnp.arange(bytes_, dtype=jnp.int32)[None, :]
    window = (position >= ends - sizes[:, None]) & (position < ends)
    pc32, pc, oc = attend(qc, kc, vc, window)
    x1 = (patch + product(oc, outw[0])).astype(BF)
    x1f = x1.astype(F32)
    n1, f1 = norm_rows(x1f, gains[2])
    q = heads_of(product(n1, attn[1, 0]).astype(BF))
    k = heads_of(product(n1, attn[1, 1]).astype(BF))
    v = heads_of(product(n1, attn[1, 2]).astype(BF))
    slot = jnp.arange(patches, dtype=jnp.int32)
    allowed = (slot[None, :] <= slot[:, None]) & (slot[None, :] < length)
    a32, a, o = attend(q, k, v, allowed)
    x2 = (x1f + product(o, outw[1])).astype(BF)
    x2f = x2.astype(F32)
    n2, f2 = norm_rows(x2f, gains[3])
    gate = product(n2, gate_stack[0])
    up = product(n2, gate_stack[1])
    sig = jax.nn.sigmoid(gate)
    hidden = (gate * sig * up).astype(BF)
    result = (x2f + product(hidden, down)).astype(BF)

    grad_down = weight_grad(hidden, cot)
    dh = product_right(cot, down).astype(BF).astype(F32)
    dgate = (dh * up * sig * (1.0 + gate * (1.0 - sig))).astype(BF)
    dup = (dh * gate * sig).astype(BF)
    grad_gate_up = jnp.stack([weight_grad(n2, dgate), weight_grad(n2, dup)])
    dn2 = product_right(dgate, gate_stack[0]) + product_right(dup, gate_stack[1])
    back, gain3 = norm_back(x2f, f2, gains[3], dn2)
    dx2 = (cot.astype(F32) + back).astype(BF)
    do = heads_of(product_right(dx2, outw[1]).astype(BF))
    dq, dk, dv = attend_back(q, k, v, a32, a, do)
    dn1 = product_right(dq, attn[1, 0]) + product_right(dk, attn[1, 1]) + product_right(dv, attn[1, 2])
    back, gain2 = norm_back(x1f, f1, gains[2], dn1)
    dx1 = (dx2.astype(F32) + back).astype(BF)
    doc = heads_of(product_right(dx1, outw[0]).astype(BF))
    dqc, dkc, dvc = attend_back(qc, kc, vc, pc32, pc, doc)
    back, gain0 = norm_back(patch, fq, gains[0], product_right(dqc, attn[0, 0]))
    grad_patch = (dx1.astype(F32) + back).astype(BF)
    back, gain1 = norm_back(byte, fb, gains[1], product_right(dkc, attn[0, 1]) + product_right(dvc, attn[0, 2]))
    grad_byte = back.astype(BF)
    grad_attn = jnp.stack(
        [
            jnp.stack([weight_grad(nq, dqc), weight_grad(nb, dkc), weight_grad(nb, dvc)]),
            jnp.stack([weight_grad(n1, dq), weight_grad(n1, dk), weight_grad(n1, dv)]),
        ]
    )
    grad_out = jnp.stack([weight_grad(oc, dx1), weight_grad(o, dx2)])
    grad_gains = jnp.where(part == 0, jnp.stack([gain0, gain1, gain2, gain3]), 0.0)

    def to_owner(values):
        whole = lax.all_gather(half(values), "pipe", axis=0, tiled=True)
        whole = whole.reshape(micro, -1, values.shape[1])
        count = whole.shape[1] // stages
        return lax.dynamic_slice_in_dim(whole, place * count, count, 1)

    def summed(values, axis):
        return lax.psum_scatter(values, everyone, scatter_dimension=axis, tiled=True).astype(F32)

    return (
        to_owner(result),
        to_owner(grad_patch),
        to_owner(grad_byte),
        summed(grad_attn, 2),
        summed(grad_out, 1),
        summed(grad_gate_up, 1),
        summed(grad_down, 0),
        summed(grad_gains, 1),
    )


LINE = 4
SIDE = 2
RANKS = 4
GROUPS = LINE * SIDE
ROWS_HERE = 2
PATCHES = 256
BYTES = 640
WIDTH = 1024
MINE = WIDTH // RANKS
HEADS_MINE = MINE // HEAD_DIM
TOKENS = PATCHES // RANKS
TOKENS_B = BYTES // RANKS
SHARD = WIDTH // (GROUPS * RANKS)
SEG = SHARD * RANKS
UNITS = 88
PADDED = 96
HIDDEN = GROUPS * PADDED
NSEM = 328
BIG = (("attn0", 0), ("attn1", 1))


def scratch_plan():
    b = lambda *shape: pltpu.VMEM(shape, BF)
    plan = dict(
        sem=pltpu.SemaphoreType.DMA((NSEM,)),
        patch=b(ROWS_HERE, PATCHES, WIDTH),
        cot=b(ROWS_HERE, PATCHES, WIDTH),
        attn=b(6, SHARD, WIDTH),
        gate_up=b(2, SHARD, GROUPS * RANKS * UNITS),
        wa=b(6, WIDTH, MINE),
        won=b(2, LINE, SIDE, SHARD, WIDTH),
        woh=b(2, 2, 2, HEAD_DIM, WIDTH),
        wg=b(WIDTH, 2 * HIDDEN),
        wd=b(HIDDEN, WIDTH),
        da=b(6, WIDTH, MINE),
        don=b(2, GROUPS, SHARD, WIDTH),
        dg=b(WIDTH, 2 * HIDDEN),
        dd=b(HIDDEN, WIDTH),
        xa=b(6, LINE, SEG, MINE),
        xo=b(2, LINE, SHARD, WIDTH),
        xg=b(LINE, SEG, 2 * HIDDEN),
        xd=b(PADDED, WIDTH),
        za=b(6, LINE + 1, SEG, MINE),
        zo=b(2, LINE + 1, SHARD, WIDTH),
        zg=b(LINE + 1, SEG, 2 * HIDDEN),
        zd=b(LINE + 1, SIDE * PADDED, WIDTH),
        nq=b(ROWS_HERE, PATCHES, WIDTH),
        nb=b(ROWS_HERE, BYTES, WIDTH),
        qc=b(ROWS_HERE, PATCHES, MINE),
        kc=b(ROWS_HERE, BYTES, MINE),
        vc=b(ROWS_HERE, BYTES, MINE),
        oc=b(ROWS_HERE, PATCHES, MINE),
        x1=b(8, TOKENS, WIDTH),
        n1=b(ROWS_HERE, PATCHES, WIDTH),
        qkv=b(3, ROWS_HERE, PATCHES, MINE),
        o=b(ROWS_HERE, PATCHES, MINE),
        x2=b(8, TOKENS, WIDTH),
        n2=b(ROWS_HERE, PATCHES, WIDTH),
        fac=b(ROWS_HERE, PATCHES, 2 * HIDDEN),
        hid=b(ROWS_HERE, PATCHES, HIDDEN),
        dx2=b(8, TOKENS, WIDTH),
        dx1=b(8, TOKENS, WIDTH),
        dmix=b(ROWS_HERE, PATCHES, MINE),
        dqkv=b(ROWS_HERE, PATCHES, 3 * MINE),
        dqc=b(ROWS_HERE, PATCHES, MINE),
        dkvc=b(ROWS_HERE, BYTES, 2 * MINE),
        p=b(8, TOKENS, WIDTH),
        r1=b(ROWS_HERE, 2, TOKENS, WIDTH),
        q2=b(ROWS_HERE, TOKENS, WIDTH),
        r2=b(ROWS_HERE, TOKENS, WIDTH),
        bp=b(8, TOKENS_B, WIDTH),
        br1=b(ROWS_HERE, 2, TOKENS_B, WIDTH),
        br2=b(ROWS_HERE, TOKENS_B, WIDTH),
    )
    return plan


INS = ("patch_in", "byte", "cot_in", "sizes", "lengths", "attn_in", "wo_in", "gate_up_in", "down", "gains")
OUTS = ("out", "gpatch", "gbyte", "g_attn", "g_out", "g_gate", "g_down")


def step_kernel(names, *refs):
    m = SimpleNamespace(**dict(zip(INS + OUTS + tuple(names), refs)))
    dp, pipe = lax.axis_index("dp"), lax.axis_index("pipe")
    z, x, y, c = dp // SIDE, dp % SIDE, pipe // 2, pipe % 2
    at = lambda z, x, y, c: (z * SIDE + x, y * 2 + c)
    sibling, across, aside = at(z, x, y, 1 - c), at(z, x, 1 - y, c), at(z, 1 - x, y, c)
    right, left = at((z + 1) % LINE, x, y, c), at((z + LINE - 1) % LINE, x, y, c)
    corner = at(z, x, 1 - y, 1 - c)
    counter = [0]

    def take(count=1):
        first = counter[0]
        counter[0] += count
        assert counter[0] <= NSEM
        return first

    unfinished = []

    def remote(src, dst, device, send=None, recv=None):
        send = take() if send is None else send
        recv = take() if recv is None else recv
        return pltpu.make_async_remote_copy(
            src_ref=src, dst_ref=dst, send_sem=m.sem.at[send], recv_sem=m.sem.at[recv], device_id=device, device_id_type=MESH
        )

    def begin(copy):
        copy.start()
        unfinished.append(copy.wait_send)
        return copy

    def near(src, dst):
        copy = pltpu.make_async_copy(src, dst, m.sem.at[take()])
        copy.start()
        return copy

    local_out = near(m.wo_in, m.won.at[:, z, x])
    attn_here, gate_here, patch_here = near(m.attn_in, m.attn), near(m.gate_up_in, m.gate_up), near(m.patch_in, m.patch)
    bytes_in, cot_here = near(m.byte, m.bp), near(m.cot_in, m.cot)

    barrier = pltpu.get_barrier_semaphore()
    for device in (sibling, across, corner, aside):
        pl.semaphore_signal(barrier, inc=1, device_id=device, device_id_type=MESH)

    @pl.when(z < LINE - 1)
    def _():
        pl.semaphore_signal(barrier, inc=1, device_id=right, device_id_type=MESH)

    @pl.when(z > 0)
    def _():
        pl.semaphore_signal(barrier, inc=1, device_id=left, device_id_type=MESH)

    pl.semaphore_wait(barrier, 4 + (z < LINE - 1).astype(jnp.int32) + (z > 0).astype(jnp.int32))

    class Gather:
        def __init__(self, view):
            self.view = view
            self.sx, self.rx = take(LINE), take(LINE)
            self.sz, self.rz = take(LINE + 1), take(LINE)

        def copy(self, block, device, send, recv):
            there = self.view(block * SIDE + x)
            return remote(there, there, device, send, recv + block)

        def aside(self, block):
            return self.copy(block, aside, self.sx + block, self.rx)

        def right(self, block):
            return self.copy(block, right, self.sz + block, self.rz)

        def left(self, block):
            return self.copy(block, left, self.sz + jnp.where(block == z, LINE, block), self.rz)

        def start(self):
            self.aside(z).start()

            @pl.when(z < LINE - 1)
            def _():
                self.right(z).start()

            @pl.when(z > 0)
            def _():
                self.left(z).start()

        def hop(self, k):
            @pl.when(z - k >= 0)
            def _():
                self.right(z - k).wait_recv()
                self.aside(z - k).start()

                @pl.when(z < LINE - 1)
                def _():
                    self.right(z - k).start()

            @pl.when(z + k < LINE)
            def _():
                self.left(z + k).wait_recv()
                self.aside(z + k).start()

                @pl.when(z > 0)
                def _():
                    self.left(z + k).start()

        def ready(self):
            for block in range(LINE):
                self.aside(block).wait_recv()

        def finish(self):
            for block in range(LINE):
                self.aside(block).wait_send()

                @pl.when((z < LINE - 1) & (z >= block))
                def _():
                    self.right(block).wait_send()

                @pl.when((z > 0) & (z <= block))
                def _():
                    self.left(block).wait_send()

    class GatherPairs(Gather):
        def copy(self, block, device, send, recv):
            there = self.view(block * SIDE, SIDE)
            return remote(there, there, device, send, recv + block)

        def start(self):
            there = self.view(z * SIDE + x, 1)
            self.side = begin(remote(there, there, aside, self.sx, self.rx))

        def line(self):
            self.side.wait_recv()

            @pl.when(z < LINE - 1)
            def _():
                self.right(z).start()

            @pl.when(z > 0)
            def _():
                self.left(z).start()

        def hop(self, k):
            @pl.when(z - k >= 0)
            def _():
                self.right(z - k).wait_recv()

                @pl.when(z < LINE - 1)
                def _():
                    self.right(z - k).start()

            @pl.when(z + k < LINE)
            def _():
                self.left(z + k).wait_recv()

                @pl.when(z > 0)
                def _():
                    self.left(z + k).start()

        def ready(self):
            pass

        def finish(self):
            for block in range(LINE):

                @pl.when((z < LINE - 1) & (z >= block))
                def _():
                    self.right(block).wait_send()

                @pl.when((z > 0) & (z <= block))
                def _():
                    self.left(block).wait_send()

    g_out0 = Gather(lambda d: m.won.at[0, d // SIDE, d % SIDE])
    g_out1 = Gather(lambda d: m.won.at[1, d // SIDE, d % SIDE])
    g_attn0 = Gather(lambda d: m.wa.at[pl.ds(0, 3), pl.ds(d * SEG, SEG)])
    g_attn1 = Gather(lambda d: m.wa.at[pl.ds(3, 3), pl.ds(d * SEG, SEG)])
    g_gate = Gather(lambda d: m.wg.at[pl.ds(d * SEG, SEG)])
    g_down = GatherPairs(lambda d, count: m.wd.at[pl.ds(d * PADDED, count * PADDED)])

    def pieces(values, starts, width):
        return jnp.concatenate([values[:, first : first + width] for first in starts], axis=1)

    def spread(src, dst):
        copies = [near(src(pipe), dst)]
        for device in (across, corner, sibling):
            copies.append(begin_early(remote(src(device[1]), dst, device)))
        return copies

    early_sends = []

    def begin_early(copy):
        copy.start()
        early_sends.append(copy.wait_send)
        return copy

    def arrived(copies):
        copies[0].wait()
        for copy in copies[1:]:
            copy.wait_recv()

    def spread_attn(layer):
        for part in range(3 * layer, 3 * layer + 3):
            values = m.attn[part].astype(F32)
            for rank in range(RANKS):
                heads = [8 * (rank % 2) + 2 * j + rank // 2 for j in range(HEADS_MINE)]
                m.xa[part, rank, 0:SHARD, :] = pieces(values, [h * HEAD_DIM for h in heads], HEAD_DIM).astype(BF)
        three = pl.ds(3 * layer, 3)
        return spread(lambda q: m.xa.at[three, q, pl.ds(0, SHARD)], m.wa.at[three, pl.ds(dp * SEG + pipe * SHARD, SHARD)])

    def spread_gate():
        for which in range(2):
            values = m.gate_up[which].astype(F32)
            values = jnp.concatenate([values, jnp.zeros((SHARD, 128), F32)], axis=1)
            keep = (lax.broadcasted_iota(jnp.int32, (SHARD, HIDDEN), 1) % PADDED) < UNITS
            for rank in range(RANKS):
                starts = [UNITS * (RANKS * d + rank) for d in range(GROUPS)]
                runs = jnp.where(keep, pieces(values, starts, PADDED), 0.0)
                m.xg[rank, 0:SHARD, which * HIDDEN : (which + 1) * HIDDEN] = runs.astype(BF)
        return spread(lambda q: m.xg.at[q, pl.ds(0, SHARD)], m.wg.at[pl.ds(dp * SEG + pipe * SHARD, SHARD)])

    def begin_after(copies, gather):
        arrived(copies)
        gather.start()

    queue = []

    def pump(count):
        for _ in range(min(count, len(queue))):
            queue.pop(0)()

    def swap_out(layer):
        mine, there = m.won.at[layer, pl.ds(2 * c, 2)], m.woh.at[layer, :, :, pl.ds(c * SHARD, SHARD)]
        keep = near(mine, there)
        give = remote(m.won.at[layer, pl.ds(2 * (1 - c), 2)], there, sibling)
        give.start()
        return keep, give

    def swapped(swap):
        swap[0].wait()
        swap[1].wait_recv()

    lane = lax.broadcasted_iota(jnp.int32, (1, MINE), 1) // HEAD_DIM
    head_mask = [(lane == j).astype(F32).astype(BF) for j in range(HEADS_MINE)]
    scaled_mask = [((lane == j).astype(F32) * SCALE).astype(BF) for j in range(HEADS_MINE)]

    def gain(index):
        return m.gains[index : index + 1, :]

    def factor_of(values):
        return lax.rsqrt(jnp.mean(values * values, axis=-1, keepdims=True) + EPSILON)

    def normed(values, index):
        values = values.astype(F32)
        return (values * factor_of(values) * gain(index)).astype(BF)

    def norm_back(values, gradient, index):
        values = values.astype(F32)
        factor = factor_of(values)
        weighted = gradient * gain(index)
        return factor * weighted - values * (factor * factor * factor) * jnp.mean(weighted * values, axis=-1, keepdims=True)

    def normed_rows(src, dst, index, r):
        for part in range(RANKS):
            for half in range(2):
                rows = pl.ds(half * (TOKENS // 2), TOKENS // 2)
                dst[r, pl.ds(part * TOKENS + half * (TOKENS // 2), TOKENS // 2)] = normed(src[4 * r + part, rows], index)

    class Reduce:
        def __init__(self, p, r1, q2, r2, tokens, sems):
            self.p, self.r1, self.q2, self.r2, self.tokens, self.sems = p, r1, q2, r2, tokens, sems
            self.first, self.second = {}, {}

        def give(self, r):
            self.first[r] = [
                remote(self.p.at[4 * r + 2 * side + 1 - c], self.r1.at[r, side], sibling, *pair_at(self.sems, 2 * r + side))
                for side in range(2)
            ]
            for copy in self.first[r]:
                copy.start()

        def cross(self, r):
            for copy in self.first[r]:
                copy.wait_recv()
            other = 4 * r + 2 * (1 - y) + c
            self.q2[r] = (self.p[other].astype(F32) + self.r1[r, 1 - y].astype(F32)).astype(BF)
            self.second[r] = remote(self.q2.at[r], self.r2.at[r], across, *pair_at(self.sems, 4 + r))
            self.second[r].start()

        def arrive(self, r):
            self.second[r].wait_recv()

        def free(self):
            for r in range(ROWS_HERE):
                for copy in self.first[r]:
                    copy.wait_send()
                self.second[r].wait_send()

        def total(self, r, rows):
            own = 4 * r + pipe
            return (
                self.p[own, rows].astype(F32) + self.r1[r, y, rows].astype(F32) + self.r2[r, rows].astype(F32)
            )

    class Share:
        def __init__(self, values, sems):
            self.values, self.sems, self.copies, self.last = values, sems, {}, {}

        def give(self, r):
            there = self.values.at[4 * r + pipe]
            self.copies[r] = [
                remote(there, there, device, *pair_at(self.sems, 3 * r + k)) for k, device in enumerate((across, sibling))
            ]
            for copy in self.copies[r]:
                copy.start()

        def relay(self, r):
            self.copies[r][0].wait_recv()
            there = self.values.at[4 * r + 2 * (1 - y) + c]
            self.last[r] = remote(there, there, sibling, *pair_at(self.sems, 3 * r + 2))
            self.last[r].start()

        def ready(self, r):
            self.copies[r][1].wait_recv()
            self.last[r].wait_recv()

        def free(self):
            for r in range(ROWS_HERE):
                for copy in self.copies[r] + [self.last[r]]:
                    copy.wait_send()

    def pair_at(first, index):
        return first + 2 * index, first + 2 * index + 1

    sums_a, sums_b, shares = take(12), take(12), take(12)

    halves = [pl.ds(h * (TOKENS // 2), TOKENS // 2) for h in range(2)]

    def to_owner(reduce, left_of, r):
        for n in range(4):
            cols = pl.ds(n * 256, 256)
            reduce.p[4 * r : 4 * r + 4, :, cols] = left_of(r, n).astype(BF).reshape(4, reduce.tokens, 256)
        reduce.give(r)

    local_out.wait()
    g_out0.start()
    g_out1.start()
    m.wd[pl.ds(pl.multiple_of(dp * PADDED, 32), PADDED), :] = jnp.concatenate(
        [m.down[...], jnp.zeros((PADDED - UNITS, WIDTH), BF)], axis=0
    )
    g_down.start()
    attn_here.wait()
    exchange0 = spread_attn(0)
    exchange1 = spread_attn(1)
    gate_here.wait()
    exchange2 = spread_gate()
    begin_after(exchange0, g_attn0)
    patch_here.wait()

    @pl.loop(0, ROWS_HERE * PATCHES // 32)
    def _(i):
        rows = pl.ds((i % 8) * 32, 32)
        m.nq[i // 8, rows] = normed(m.patch[i // 8, rows], 0)

    bytes_in.wait()
    cot_here.wait()

    @pl.loop(0, 8)
    def _(i):
        for part in range(5):
            rows = pl.ds(part * 32, 32)
            m.nb[i // 4, pl.ds((i % 4) * TOKENS_B + part * 32, 32)] = normed(m.bp[i, rows], 1)

    def hops(gather):
        return [functools.partial(gather.hop, k) for k in (1, 2, 3)]

    h_out0, h_attn0, h_out1, h_attn1, h_gate, h_down = map(hops, (g_out0, g_attn0, g_out1, g_attn1, g_gate, g_down))
    queue += [h_out0[0], h_out1[0], h_attn0[0], h_out0[1], h_out1[1], h_attn0[1], h_out0[2], h_out1[2]]
    queue += [lambda: begin_after(exchange1, g_attn1), h_attn0[2]]
    queue += [h_attn1[0], lambda: begin_after(exchange2, g_gate), h_attn1[1], h_attn1[2]]
    pump(len(queue))
    queue += [lambda: [wait() for wait in early_sends]] + h_gate[:2] + [g_down.line, h_gate[2]] + h_down
    g_out0.ready()
    swap0 = swap_out(0)
    g_attn0.ready()

    for r in range(ROWS_HERE):
        m.qc[r] = product(m.nq[r], m.wa[0]).astype(BF)

    @pl.loop(0, 4)
    def _(i):
        rows = pl.ds((i % 2) * (BYTES // 2), BYTES // 2)
        block = m.nb[i // 2, rows]
        m.kc[i // 2, rows] = product(block, m.wa[1]).astype(BF)
        m.vc[i // 2, rows] = product(block, m.wa[2]).astype(BF)

    def window(r):
        sizes = m.sizes[pl.ds(r, 1), :].astype(F32)
        i = lax.broadcasted_iota(jnp.int32, (PATCHES, PATCHES), 0)
        j = lax.broadcasted_iota(jnp.int32, (PATCHES, PATCHES), 1)
        first = jnp.sum(jnp.where(j < i, sizes, 0.0), axis=1, keepdims=True)
        last = jnp.sum(jnp.where(j <= i, sizes, 0.0), axis=1, keepdims=True)
        position = lax.broadcasted_iota(jnp.int32, (PATCHES, BYTES), 1).astype(F32)
        return (position >= first) & (position < last)

    def causal(r):
        length = m.lengths[r]
        i = lax.broadcasted_iota(jnp.int32, (PATCHES, PATCHES), 0)
        j = lax.broadcasted_iota(jnp.int32, (PATCHES, PATCHES), 1)
        return (j <= i) & (j < length)

    def weights_of(query, keys, allowed):
        scores = jnp.where(allowed, product_right(query, keys), NEGATIVE)
        raised = jnp.exp(scores - jnp.max(scores, axis=-1, keepdims=True))
        return raised * (1.0 / jnp.sum(raised, axis=-1, keepdims=True))

    def attend(r, allowed, queries, keys, values, mixed):
        total = None
        for j in range(HEADS_MINE):
            low = weights_of(queries[r] * scaled_mask[j], keys[r], allowed).astype(BF)
            term = product(low, values[r] * head_mask[j])
            total = term if total is None else total + term
        mixed[r] = total.astype(BF)

    def attend_back(r, allowed, queries, keys, values, grad):
        sums = [None, None, None]
        for j in range(HEADS_MINE):
            query, mixed = queries[r] * scaled_mask[j], grad[r] * head_mask[j]
            weights = weights_of(query, keys[r], allowed)
            grad_weights = product_right(mixed, values[r])
            grad_scores = weights * (grad_weights - jnp.sum(weights * grad_weights, axis=-1, keepdims=True))
            grad_scores = grad_scores.astype(BF)
            terms = (
                product(grad_scores, keys[r] * head_mask[j]),
                product_left(grad_scores, query),
                product_left(weights.astype(BF), mixed),
            )
            sums = [t if s is None else s + t for s, t in zip(sums, terms)]
        return (sums[0] * SCALE).astype(BF), sums[1].astype(BF), sums[2].astype(BF)

    def out_rows(layer):
        return lambda n: m.woh[layer, :, :, :, pl.ds(n * 256, 256)].reshape(MINE, 256)

    def residual(reduce, share, base, result, r):
        reduce.arrive(r)
        for rows in halves:
            result[4 * r + pipe, rows] = (base(r, rows) + reduce.total(r, rows)).astype(BF)
        share.give(r)

    first_sum, first_share = Reduce(m.p, m.r1, m.q2, m.r2, TOKENS, sums_a), Share(m.x1, shares)
    attend(0, window(0), m.qc, m.kc, m.vc, m.oc)
    swapped(swap0)
    to_owner(first_sum, lambda r, n: product(m.oc[r], out_rows(0)(n)), 0)
    attend(1, window(1), m.qc, m.kc, m.vc, m.oc)
    first_sum.cross(0)
    to_owner(first_sum, lambda r, n: product(m.oc[r], out_rows(0)(n)), 1)
    pump(2)
    first_sum.cross(1)
    pump(2)
    own_patch = lambda r, rows: m.patch[r, pl.ds(pipe * TOKENS + rows.start, TOKENS // 2)].astype(F32)
    for r in range(ROWS_HERE):
        residual(first_sum, first_share, own_patch, m.x1, r)
    first_share.relay(0)
    g_out1.ready()
    swap1 = swap_out(1)
    g_attn1.ready()
    queries, keys, values = m.qkv.at[0], m.qkv.at[1], m.qkv.at[2]

    def project(r):
        first_share.ready(r)
        normed_rows(m.x1, m.n1, 2, r)
        for part in range(3):
            m.qkv[part, r] = product(m.n1[r], m.wa[3 + part]).astype(BF)

    project(0)
    attend(0, causal(0), queries, keys, values, m.o)
    first_sum.free()
    second_sum, second_share = Reduce(m.p, m.r1, m.q2, m.r2, TOKENS, sums_a), Share(m.x2, shares)
    swapped(swap1)
    to_owner(second_sum, lambda r, n: product(m.o[r], out_rows(1)(n)), 0)
    first_share.relay(1)
    project(1)
    first_share.free()
    attend(1, causal(1), queries, keys, values, m.o)
    second_sum.cross(0)
    to_owner(second_sum, lambda r, n: product(m.o[r], out_rows(1)(n)), 1)
    pump(1)
    second_sum.cross(1)
    pump(1)
    own_of = lambda values: lambda r, rows: values[4 * r + pipe, rows].astype(F32)
    for r in range(ROWS_HERE):
        residual(second_sum, second_share, own_of(m.x1), m.x2, r)
    for r in range(ROWS_HERE):
        second_share.relay(r)
    for r in range(ROWS_HERE):
        second_share.ready(r)
        normed_rows(m.x2, m.n2, 3, r)

    pump(len(queue) - 1)
    g_gate.ready()
    tiles = HIDDEN // 256
    for r in range(ROWS_HERE):
        for n in range(tiles):
            first, later = pl.ds(n * 256, 256), pl.ds(HIDDEN + n * 256, 256)
            gate = product(m.n2[r], m.wg[:, first])
            up = product(m.n2[r], m.wg[:, later])
            sig = jax.nn.sigmoid(gate)
            silu = gate * sig
            m.hid[r, :, first] = (silu * up).astype(BF)
            m.fac[r, :, first] = (up * sig * (1.0 + gate * (1.0 - sig))).astype(BF)
            m.fac[r, :, later] = silu.astype(BF)

    class Scatter:
        def __init__(self, mine, xbuf, zbuf):
            self.mine, self.xbuf, self.zbuf = mine, xbuf, zbuf
            self.sx, self.rx = take(LINE), take(LINE)
            self.sz, self.rz = take(LINE), take(LINE + 1)

        def aside(self, block):
            return remote(self.mine(block * SIDE + 1 - x), self.xbuf(block), aside, self.sx + block, self.rx + block)

        def start(self):
            for block in (3, 0, 2, 1):
                self.aside(block).start()

        def add(self, into, values):
            into[...] = (into[...].astype(F32) + values[...].astype(F32)).astype(BF)

        def line(self, block):
            return self.mine(block * SIDE + x)

        def right(self, block):
            return remote(self.line(block), self.zbuf(block), right, self.sz + block, self.rz + block)

        def left(self, block, slot):
            return remote(self.line(block), self.zbuf(slot), left, self.sz + block, self.rz + slot)

        def send_left(self, block):
            self.left(block, jnp.where(z - 1 == block, LINE, block)).start()

        def emit(self, rightward, leftward):
            @pl.when(z == 0)
            def _():
                for block in rightward:
                    self.right(block).start()

            @pl.when(z == LINE - 1)
            def _():
                for block in leftward:
                    self.send_left(block)

        def take(self, block):
            self.aside(block).wait_recv()
            self.add(self.line(block), self.xbuf(block))
            self.emit(*{3: ((3,), ()), 0: ((), (0,)), 2: ((2,), ()), 1: ((1,), (1, 2))}[block])

        def tick(self, t):
            @pl.when((z >= 1) & (z <= t))
            def _():
                block = LINE - 1 - t + z
                self.right(block).wait_recv()
                self.add(self.line(block), self.zbuf(block))

                @pl.when(z < block)
                def _():
                    self.right(block).start()

            @pl.when((z < LINE - 1) & (z >= LINE - 1 - t))
            def _():
                block = t - (LINE - 1) + z
                slot = jnp.where(z == block, LINE, block)
                self.left(block, slot).wait_recv()
                self.add(self.line(block), self.zbuf(slot))

                @pl.when(z > block)
                def _():
                    self.send_left(block)

        def finish(self):
            for block in range(LINE):
                self.aside(block).wait_send()
            self.finish_line()

        def finish_line(self):
            for block in range(LINE):

                @pl.when(z < block)
                def _():
                    self.right(block).wait_send()

                @pl.when(z > block)
                def _():
                    self.left(block, 0).wait_send()

    class ScatterPairs(Scatter):
        def line(self, block):
            return self.mine(block * SIDE, SIDE)

        def start(self):
            self.emit((3, 2, 1), (0, 1, 2))

        def cross(self):
            self.side = begin(remote(self.mine(z * SIDE + 1 - x, 1), self.xbuf, aside, self.sx, self.rx))

        def last(self):
            self.side.wait_recv()
            self.add(self.mine(z * SIDE + x, 1), self.xbuf)

    pump(1)

    s_down = ScatterPairs(lambda d, count: m.dd.at[pl.ds(d * PADDED, count * PADDED)], m.xd, lambda b: m.zd.at[b])
    s_gate = Scatter(lambda d: m.dg.at[pl.ds(d * SEG, SEG)], lambda b: m.xg.at[b], lambda b: m.zg.at[b])

    def hidden_back(r):
        for n in range(tiles):
            first, later = pl.ds(n * 256, 256), pl.ds(HIDDEN + n * 256, 256)
            grad = product_right(m.cot[r], m.wd[first, :]).astype(BF).astype(F32)
            m.fac[r, :, first] = (grad * m.fac[r, :, first].astype(F32)).astype(BF)
            m.fac[r, :, later] = (grad * m.fac[r, :, later].astype(F32)).astype(BF)

    def gate_grad(block):
        rows = pl.ds(block * 256, 256)
        total = product_left(m.n2[0, :, rows], m.fac[0]) + product_left(m.n2[1, :, rows], m.fac[1])
        m.dg[rows, :] = total.astype(BF)
        s_gate.aside(block).start()

    second_sum.free()
    second_share.free()
    third_sum, third_share = Reduce(m.p, m.r1, m.q2, m.r2, TOKENS, sums_a), Share(m.dx2, shares)
    for r in range(ROWS_HERE):
        hidden_back(r)
        to_owner(third_sum, lambda r, n: product_right(m.fac[r], m.wg[n * 256 : n * 256 + 256, :]), r)
    gate_grad(3)
    third_sum.cross(0)
    third_sum.cross(1)
    gate_grad(0)

    @pl.loop(0, tiles)
    def _(n):
        cols = pl.ds(pl.multiple_of(n * 256, 256), 256)
        for half in range(2):
            wide = pl.ds(half * 512, 512)
            total = product_left(m.hid[0, :, cols], m.cot[0, :, wide]) + product_left(m.hid[1, :, cols], m.cot[1, :, wide])
            m.dd[cols, wide] = total.astype(BF)

    s_down.start()
    gate_grad(2)
    gate_grad(1)

    def gradient_in(reduce, share, base, values, index, result, r):
        reduce.arrive(r)
        for rows in halves:
            back = norm_back(values(r, rows), reduce.total(r, rows), index)
            result(r, rows, (base(r, rows) + back).astype(BF))
        if share is not None:
            share.give(r)

    def into(ref):
        def store(r, rows, value):
            ref[4 * r + pipe, rows] = value

        return store

    own_cot = lambda r, rows: m.cot[r, pl.ds(pipe * TOKENS + rows.start, TOKENS // 2)].astype(F32)
    for r in range(ROWS_HERE):
        gradient_in(third_sum, third_share, own_cot, own_of(m.x2), 3, into(m.dx2), r)

    early = pl.ds(0, TOKENS)
    out_sum = Reduce(m.bp.at[:, early], m.br1.at[:, :, early], m.n2.at[:, early], m.br2.at[:, early], TOKENS, sums_b)
    for r in range(ROWS_HERE):
        to_owner(out_sum, lambda r, n: product(m.hid[r], m.wd[:, n * 256 : n * 256 + 256]), r)
    third_share.relay(0)
    for r in range(ROWS_HERE):
        out_sum.cross(r)
    third_share.relay(1)

    def rows_of(ref, r):
        return ref[4 * r : 4 * r + 4].reshape(PATCHES, WIDTH)

    def mixed_back(share, grads, layer, r):
        share.ready(r)
        m.dmix[r] = product_right(rows_of(grads, r), m.woh[layer].reshape(MINE, WIDTH)).astype(BF)

    def attn_back(left, n, first, count):
        total = None
        for part in range(count):
            term = product_right(left[:, part * MINE : part * MINE + MINE], m.wa[first + part, pl.ds(n * 256, 256), :])
            total = term if total is None else total + term
        return total

    def global_back(r):
        mixed_back(third_share, m.dx2, 1, r)
        dq, dk, dv = attend_back(r, causal(r), queries, keys, values, m.dmix)
        m.dqkv[r, :, 0:MINE] = dq
        m.dqkv[r, :, MINE : 2 * MINE] = dk
        m.dqkv[r, :, 2 * MINE : 3 * MINE] = dv

    s_down.tick(1)
    global_back(0)
    third_sum.free()
    fourth_sum, fourth_share = Reduce(m.p, m.r1, m.q2, m.r2, TOKENS, sums_a), Share(m.dx1, shares)
    to_owner(fourth_sum, lambda r, n: attn_back(m.dqkv.at[r], n, 3, 3), 0)
    global_back(1)
    third_share.free()
    fourth_sum.cross(0)
    to_owner(fourth_sum, lambda r, n: attn_back(m.dqkv.at[r], n, 3, 3), 1)

    def own_half(layer, which):
        return m.won.at[layer, :, which]

    def out_grad(layer, mixed, grads):
        (g_out0, g_out1)[layer].finish()
        (swap0, swap1)[layer][1].wait_send()
        total = None
        for r in range(ROWS_HERE):
            term = product_left(mixed[r], rows_of(grads, r))
            total = term if total is None else total + term
        m.won[layer] = total.astype(BF).reshape(LINE, SIDE, SHARD, WIDTH)
        there = m.don.at[layer, pl.ds(HEADS_MINE * c, HEADS_MINE)]
        keep = near(own_half(layer, c), there)
        give = remote(own_half(layer, 1 - c), there, sibling)
        begin(give)
        return keep, give

    def attn_grad(first, count, left, right):
        @pl.loop(0, 4)
        def _(n):
            cols = pl.ds(pl.multiple_of(n * 256, 256), 256)
            total = product_left(left[0, :, cols], right[0]) + product_left(left[1, :, cols], right[1])
            for part in range(count):
                m.da[first + part, cols, :] = total[:, part * MINE : part * MINE + MINE].astype(BF)

    def scatter_out(layer):
        return Scatter(lambda d: m.don.at[layer, d], lambda b: m.xo.at[layer, b], lambda b: m.zo.at[layer, b])

    def scatter_attn(first, count):
        part = pl.ds(first, count)
        return Scatter(lambda d: m.da.at[part, pl.ds(d * SEG, SEG)], lambda b: m.xa.at[part, b], lambda b: m.za.at[part, b])

    swap2 = out_grad(1, m.o, m.dx2)
    fourth_sum.cross(1)
    attn_grad(3, 3, m.n1, m.dqkv)
    s_out1, s_attn1 = scatter_out(1), scatter_attn(3, 3)
    swapped(swap2)
    s_out1.start()
    s_attn1.start()
    s_gate.take(3)
    s_gate.take(0)
    s_down.tick(2)
    for r in range(ROWS_HERE):
        out_sum.arrive(r)
        for rows in halves:
            m.out[r, rows] = (own_of(m.x2)(r, rows) + out_sum.total(r, rows)).astype(BF)
    for r in range(ROWS_HERE):
        gradient_in(fourth_sum, fourth_share, own_of(m.dx2), own_of(m.x1), 2, into(m.dx1), r)
    s_gate.take(2)
    fourth_share.relay(0)

    out_sum.free()
    fourth_sum.free()
    byte_sum = Reduce(m.bp, m.br1, m.n2.at[:, pl.ds(0, TOKENS_B)], m.br2, TOKENS_B, sums_b)
    fifth_sum = Reduce(m.p, m.r1, m.q2, m.r2, TOKENS, sums_a)

    def cross_back(r):
        mixed_back(fourth_share, m.dx1, 0, r)
        dq, dk, dv = attend_back(r, window(r), m.qc, m.kc, m.vc, m.dmix)
        m.dqc[r] = dq
        m.dkvc[r, :, 0:MINE] = dk
        m.dkvc[r, :, MINE : 2 * MINE] = dv
        to_owner(byte_sum, lambda r, n: attn_back(m.dkvc.at[r], n, 1, 2), r)
        to_owner(fifth_sum, lambda r, n: attn_back(m.dqc.at[r], n, 0, 1), r)

    cross_back(0)
    fourth_share.relay(1)
    s_down.tick(3)
    s_down.cross()
    s_gate.take(1)
    byte_sum.cross(0)
    fifth_sum.cross(0)
    cross_back(1)
    s_gate.tick(1)
    attn_grad(1, 2, m.nb, m.dkvc)
    byte_sum.cross(1)
    fifth_sum.cross(1)
    attn_grad(0, 1, m.nq, m.dqc)
    s_attn0b = scatter_attn(0, 3)
    s_attn0b.start()
    swap3 = out_grad(0, m.oc, m.dx1)

    own_bytes = [near(m.byte.at[4 * r + pipe], m.gbyte.at[r]) for r in range(ROWS_HERE)]
    s_out0 = scatter_out(0)
    swapped(swap3)
    s_out0.start()
    def back_to_pipe(rows_ref, dst):
        copies = [near(rows_ref(pipe), dst)]
        for device in (across, corner, sibling):
            copies.append(begin(remote(rows_ref(device[1]), dst, device)))
        return copies

    def attn_home(first, count):
        src = lambda q: m.da.at[pl.ds(first, count), pl.ds(dp * SEG + q * SHARD, SHARD)]
        return back_to_pipe(src, m.g_attn.at[pipe, pl.ds(first, count)])

    def gate_home():
        src = lambda q: m.dg.at[pl.ds(dp * SEG + q * SHARD, SHARD)]
        return back_to_pipe(src, m.g_gate.at[pipe])

    for block in (3, 0, 2, 1):
        s_out1.take(block)
    s_gate.tick(2)
    s_attn1.take(3)
    s_out1.tick(1)
    s_attn1.take(0)
    s_out1.tick(2)
    s_gate.tick(3)
    home = [gate_home()]
    s_attn1.take(2)
    s_attn1.tick(1)
    s_out1.tick(3)
    for r in range(ROWS_HERE):
        gradient_in(
            fifth_sum,
            None,
            own_of(m.dx1),
            own_patch,
            0,
            lambda r, rows, value: m.gpatch.__setitem__((r, rows), value),
            r,
        )
    s_attn1.take(1)
    s_attn1.tick(2)
    s_attn0b.take(3)
    s_attn0b.take(0)
    s_attn1.tick(3)
    home.append(attn_home(3, 3))
    s_attn0b.take(2)
    s_attn0b.tick(1)
    s_attn0b.take(1)
    s_attn0b.tick(2)
    s_attn0b.tick(3)
    home.append(attn_home(0, 3))
    for block in (3, 0, 2, 1):
        s_out0.take(block)
    s_out0.tick(1)
    s_down.last()
    s_out0.tick(2)
    for copy in own_bytes:
        copy.wait()
    for r in range(ROWS_HERE):
        byte_sum.arrive(r)
        for part in range(5):
            rows = pl.ds(part * 32, 32)
            back = norm_back(m.gbyte[r, rows], byte_sum.total(r, rows), 1)
            m.gbyte[r, rows] = back.astype(BF)
    s_out0.tick(3)
    m.g_down[...] = m.dd[pl.ds(pl.multiple_of(dp * PADDED, 32), PADDED), :]
    for layer in range(2):
        m.g_out[layer] = m.don[layer, dp]
    for copies in home:
        arrived(copies)
    for gather in (g_attn0, g_attn1, g_gate, g_down):
        gather.finish()
    s_down.finish_line()
    for scatter in (s_gate, s_attn1, s_out1, s_attn0b, s_out0):
        scatter.finish()
    byte_sum.free()
    fifth_sum.free()
    fourth_share.free()
    for wait in unfinished:
        wait()


def finish_kernel(out, gpatch, gbyte, attn, gate_up, gains, da, do, dg, dd, out_, gpatch_, gbyte_, g_attn, g_out, g_gate, g_down, g_gain):
    for src, dst in ((out, out_), (gpatch, gpatch_), (gbyte, gbyte_)):
        dst[...] = src[...]
    place = lax.axis_index("dp") * RANKS + lax.axis_index("pipe")
    for part in range(6):
        got = [da[rank, part].astype(F32) for rank in range(RANKS)]
        heads = []
        for head in range(HEADS):
            rank, j = 2 * (head % 2) + head // 8, (head % 8) // 2
            heads.append(got[rank][:, j * HEAD_DIM : (j + 1) * HEAD_DIM])
        g_attn[part] = jnp.concatenate(heads, axis=1)
    for which in range(2):
        got = [dg[rank, :, which * HIDDEN : (which + 1) * HIDDEN].astype(F32) for rank in range(RANKS)]
        runs = [got[rank][:, PADDED * d : PADDED * d + UNITS] for d in range(GROUPS) for rank in range(RANKS)]
        g_gate[which] = jnp.concatenate(runs, axis=1)
    g_out[...] = do[...].astype(F32)
    g_down[...] = dd[0:UNITS].astype(F32)

    column = lax.broadcasted_iota(jnp.int32, (SHARD, WIDTH), 1)
    own = column == lax.broadcasted_iota(jnp.int32, (SHARD, WIDTH), 0) + place * SHARD

    def gain_gradient(row, parts):
        total = None
        for weight, grad in parts:
            term = jnp.sum(weight.astype(F32) * grad, axis=1, keepdims=True)
            total = term if total is None else total + term
        total = total / jnp.sum(jnp.where(own, gains[row : row + 1, :], 0.0), axis=1, keepdims=True)
        g_gain[row : row + 1, :] = jnp.transpose(jnp.broadcast_to(total, (SHARD, 128)))[0:1, :]

    gain_gradient(0, [(attn[0], g_attn[0])])
    gain_gradient(1, [(attn[i], g_attn[i]) for i in (1, 2)])
    gain_gradient(2, [(attn[i], g_attn[i]) for i in (3, 4, 5)])
    gain_gradient(3, [(gate_up[i], g_gate[i]) for i in range(2)])

def fused_step(patch_states, byte_states, cotangent, patch_lengths, row_lengths, attn_weights, out_weights, gate_up, down_weight, gains):
    plan = scratch_plan()
    vmem, anywhere = pl.BlockSpec(memory_space=pltpu.VMEM), pl.BlockSpec(memory_space=pl.ANY)
    shape = jax.ShapeDtypeStruct
    results = pl.pallas_call(
        functools.partial(step_kernel, tuple(plan)),
        out_shape=(
            shape((ROWS_HERE, TOKENS, WIDTH), BF),
            shape((ROWS_HERE, TOKENS, WIDTH), BF),
            shape((ROWS_HERE, TOKENS_B, WIDTH), BF),
            shape((RANKS, 6, SHARD, MINE), BF),
            shape((2, SHARD, WIDTH), BF),
            shape((RANKS, SHARD, 2 * HIDDEN), BF),
            shape((PADDED, WIDTH), BF),
        ),
        in_specs=[anywhere] * 3 + [vmem, pl.BlockSpec(memory_space=pltpu.SMEM)] + [anywhere] * 3 + [vmem] * 2,
        out_specs=[vmem] * 7,
        scratch_shapes=list(plan.values()),
        compiler_params=pltpu.CompilerParams(collective_id=0, has_side_effects=True, vmem_limit_bytes=63 * 2**20),
    )(
        patch_states,
        byte_states.reshape(8, TOKENS_B, WIDTH),
        cotangent,
        patch_lengths,
        row_lengths,
        attn_weights.reshape(6, SHARD, WIDTH),
        out_weights,
        gate_up,
        down_weight,
        gains,
    )
    finished = pl.pallas_call(
        finish_kernel,
        out_shape=(
            *(shape(array.shape, array.dtype) for array in results[:3]),
            shape((6, SHARD, WIDTH), F32),
            shape(out_weights.shape, F32),
            shape(gate_up.shape, F32),
            shape(down_weight.shape, F32),
            shape((4, SHARD), F32),
        ),
        in_specs=[vmem] * 10,
        out_specs=[vmem] * 8,
        compiler_params=pltpu.CompilerParams(vmem_limit_bytes=63 * 2**20),
    )(*results[:3], attn_weights.reshape(6, SHARD, WIDTH), gate_up, gains, *results[3:])
    return (*finished[:3], finished[3].reshape(attn_weights.shape), *finished[4:])


def solution(mesh):
    placed = (
        P("dp", None, None),
        P("dp", None, None),
        P("dp", None, None),
        P("dp", None),
        P("dp"),
        P(None, None, ("dp", "pipe"), None),
        P(None, ("dp", "pipe"), None),
        P(None, ("dp", "pipe"), None),
        P(("dp", "pipe"), None),
        P(),
    )
    return jax.shard_map(
        fused_step if mesh.shape["dp"] == GROUPS else gathered_step,
        mesh=mesh,
        in_specs=placed,
        out_specs=(
            P("dp", "pipe", None),
            P("dp", "pipe", None),
            P("dp", "pipe", None),
            P(None, None, ("dp", "pipe"), None),
            P(None, ("dp", "pipe"), None),
            P(None, ("dp", "pipe"), None),
            P(("dp", "pipe"), None),
            P(None, ("dp", "pipe")),
        ),
        check_vma=False,
    )
```
